32 devices in a mesh: section: 2 (over core), expert: 4 (over y, x), shard: 4 (over z).
Axes of the slice: x: 2, y: 2, z: 4, core: 2. Of those that a mesh axis runs over, the one named last changes fastest.
Arguments:
- feed: bfloat16 [2, 2, 1024, 768], P('section', None, ('expert', 'shard')), may hold values from -6 to 6
- segments: int32 [2, 16, 64], P(None, ('expert', 'shard')), may hold values from 0 to 3, never falling along the last dimension, each value on 1 to 32 neighbouring positions
- routes: int32 [2, 2, 16, 64], P('section', None, ('expert', 'shard')), may hold values from 0 to 3, as said below
- rel_bucket: int32 [127], replicated, may hold values from 0 to 31
- gain_attn: bfloat16 [2, 768], P('section', ('expert', 'shard')), may hold values from 0.099609375 to 1.8984375
- gain_ffn: bfloat16 [2, 768], P('section', ('expert', 'shard')), may hold values from 0.099609375 to 1.8984375
- w_query: bfloat16 [2, 768, 768], P('section', ('expert', 'shard')), may hold values from -0.21875 to 0.21875
- w_key: bfloat16 [2, 768, 768], P('section', ('expert', 'shard')), may hold values from -0.21875 to 0.21875
- w_value: bfloat16 [2, 768, 768], P('section', ('expert', 'shard')), may hold values from -0.21875 to 0.21875
- w_out_attn: bfloat16 [2, 768, 768], P('section', ('expert', 'shard')), may hold values from -0.875 to 0.875
- rel_table: bfloat16 [2, 384], P('section', ('expert', 'shard')), may hold values from -4 to 4
- router: bfloat16 [2, 768, 4], P('section', ('expert', 'shard')), may hold values from -0.15625 to 0.15625
- expert_in: bfloat16 [2, 4, 768, 3072], P('section', 'expert', None, 'shard'), may hold values from -0.21875 to 0.21875
- expert_out: bfloat16 [2, 4, 3072, 768], P('section', 'expert', 'shard'), may hold values from -0.4375 to 0.4375
Outputs:
- layer_out: bfloat16 [2, 2, 1024, 768], P('section', None, ('expert', 'shard'))
- layer_in_grad: bfloat16 [2, 2, 1024, 768], P('section', None, ('expert', 'shard'))
- grad_gain_attn: float32 [2, 768], P('section', ('expert', 'shard'))
- grad_gain_ffn: float32 [2, 768], P('section', ('expert', 'shard'))
- grad_w_query: float32 [2, 768, 768], P('section', ('expert', 'shard'))
- grad_w_key: float32 [2, 768, 768], P('section', ('expert', 'shard'))
- grad_w_value: float32 [2, 768, 768], P('section', ('expert', 'shard'))
- grad_w_out_attn: float32 [2, 768, 768], P('section', ('expert', 'shard'))
- grad_rel_table: float32 [2, 384], P('section', ('expert', 'shard'))
- grad_router: float32 [2, 768, 4], P('section', ('expert', 'shard'))
- grad_expert_in: float32 [2, 4, 768, 3072], P('section', 'expert', None, 'shard')
- grad_expert_out: float32 [2, 4, 3072, 768], P('section', 'expert', 'shard')
The draws below stay inside these ranges and needn't reach their ends.
Inputs may be any that keep to these rules, and one draw needn't show every extreme that they name: `routes`: in each micro-batch of each layer no expert is named by more than 32 tokens of one sequence, and one expert, drawn from the seed, is named by exactly 32 tokens of every sequence. `segments`: along each sequence the segment numbers never fall.
All inputs are finite; a program needn't handle non-finite values.
Results may differ from the reference program's by a relative error of at most 0.022.
Values may be sent and summed in bfloat16 or wider, within the bound.
No kernel may reach another device: no remote copies, remote signals or barrier semaphores. Data moves between devices by JAX's collectives and lax.ppermute only.
A program may use at most 128 MiB of HBM per device.

```python
import math
import jax
import jax.numpy as jnp
import numpy as np
from jax import lax

D = 768
HEADS = 12
HEAD_DIM = 64
FF = 3072
NB = 32
DOCS = 4
MB = 2
SEQ = 64
LAYERS = 2
EXPERTS = 4
SEQS = 16
TOKENS = 1024
CAP = 32


def route_block(block_key, hot_expert, step_sizes):
    noise_key, order_key = jax.random.split(block_key)
    total_slots = EXPERTS * CAP
    slot_index = jnp.arange(total_slots, dtype=jnp.int32)
    owner = slot_index // CAP
    depth = slot_index % CAP
    noise = jax.random.randint(noise_key, (total_slots,), 0, SEQ, dtype=jnp.int32)
    ranking = noise + depth * step_sizes[owner]
    ranking = jnp.where(owner == hot_expert, (2 * CAP + 1) * SEQ, ranking)
    ordering = jnp.argsort(ranking * total_slots + slot_index)
    picked = owner[ordering[:SEQ - CAP]]
    assigned = jnp.concatenate([jnp.full((CAP,), hot_expert, jnp.int32), picked.astype(jnp.int32)])
    shuffle = jax.random.permutation(order_key, SEQ)
    return jnp.zeros((SEQ,), jnp.int32).at[shuffle].set(assigned)


def draw_routes(key, part):
    key = jax.random.fold_in(key, 7)
    hot_key, step_key, block_key = jax.random.split(key, 3)
    blocks = LAYERS * MB * SEQS
    hot = jax.random.randint(hot_key, (LAYERS, MB, 1), 0, EXPERTS, dtype=jnp.int32)
    steps_drawn = jax.random.randint(step_key, (LAYERS, MB, 1, EXPERTS), 0, 2 * SEQ, dtype=jnp.int32)
    hot_rows = jnp.broadcast_to(hot, (LAYERS, MB, SEQS)).reshape(blocks)
    step_rows = jnp.broadcast_to(steps_drawn, (LAYERS, MB, SEQS, EXPERTS)).reshape(blocks, EXPERTS)
    block_keys = jax.random.split(block_key, blocks)
    drawn = jax.vmap(route_block)(block_keys, hot_rows, step_rows)
    return drawn.reshape(LAYERS, MB, SEQS, SEQ)


def plant(entries, own_key, low, high):
    spot = [jax.random.randint(jax.random.fold_in(own_key, axis), (), 0, length) for axis, length in enumerate(entries.shape)]
    widest = entries.shape.index(max(entries.shape))
    beside = spot[:widest] + [(spot[widest] + 1) % entries.shape[widest]] + spot[widest + 1:]
    return entries.at[tuple(spot)].set(low).at[tuple(beside)].set(high)


def level_of(own_key, shape, cuts, low, high):
    level, own = 1.0, jax.random.fold_in(own_key, 6)
    for axis_at, blocks in cuts:
        draws = jnp.exp(jax.random.uniform(jax.random.fold_in(own, axis_at), (blocks,), jnp.float32, low / len(cuts), high / len(cuts)))
        level = level * jnp.repeat(draws, shape[axis_at] // blocks).reshape([-1 if axis == axis_at else 1 for axis in range(len(shape))])
    return level


def length_profile(count, total, most, slope):
    loads = [(1 << 20) // math.isqrt(grade ** slope) + 1 for grade in range(2, count + 1)]
    rest, holding = total - most - (count - 1), [1] * (count - 1)
    while rest > 0:
        movable = [i for i in range(count - 1) if holding[i] < most]
        whole, budget = sum([loads[i] for i in movable]), rest
        for i in movable:
            extra = min(most - holding[i], max(1, budget * loads[i] // whole), rest)
            holding[i] = holding[i] + extra
            rest = rest - extra
    return np.array([most] + holding)


def ragged(stream_key, number_of, total, reach, skew):
    if number_of == 2:
        one = jax.random.randint(stream_key, (), max(1, total - reach), min(reach, total - 1) + 1)
        return jnp.stack([one, total - one])
    tallies = jnp.asarray(length_profile(number_of, total, reach, skew), jnp.int32)
    pairs = (number_of - 1) // 2
    donor, receiver = tallies[1:1 + 2 * pairs:2], tallies[2:2 + 2 * pairs:2]
    margin = jnp.minimum(donor - 1, reach - receiver)
    shifted = jax.random.randint(jax.random.fold_in(stream_key, 1), (pairs,), 0, 1 << 20) % (margin + 1)
    tallies = tallies.at[1:1 + 2 * pairs:2].set(donor - shifted).at[2:2 + 2 * pairs:2].set(receiver + shifted)
    return tallies[jax.random.permutation(jax.random.fold_in(stream_key, 2), number_of)]


def normal_values(rng, extent, width, limit, cuts=(), kind=jnp.bfloat16):
    array = width * jax.random.normal(rng, extent, jnp.float32)
    if cuts:
        array = array * level_of(rng, extent, cuts, -0.22, 0.18)
    return jnp.clip(array, -limit, limit).astype(kind)


def setup_inputs(seed: int = 0) -> dict:
    splits = jax.random.split(jax.random.key(seed), 15)
    return {
        "feed": normal_values(splits[0], (LAYERS, MB, TOKENS, D), 1.0, 6.0, ((0, 2), (2, 16))),
        "segments": jax.vmap(lambda own: jnp.searchsorted(jnp.cumsum(ragged(own, DOCS, SEQ, SEQ // 2, 1)), jnp.arange(SEQ), side="right"))(jax.random.split(splits[1], MB * SEQS)).reshape((MB, SEQS, SEQ)).astype(jnp.int32),
        "routes": draw_routes(jax.random.fold_in(splits[14], 71), 0),
        "rel_bucket": plant(jax.random.randint(splits[3], (2 * SEQ - 1,), 0, NB), jax.random.fold_in(splits[3], 1), 0, NB - 1).astype(jnp.int32),
        "gain_attn": jnp.clip(1.0 + 0.18 * jax.random.normal(splits[4], (LAYERS, D), jnp.float32), 0.099609375, 1.8984375).astype(jnp.bfloat16),
        "gain_ffn": jnp.clip(1.0 + 0.18 * jax.random.normal(splits[5], (LAYERS, D), jnp.float32), 0.099609375, 1.8984375).astype(jnp.bfloat16),
        "w_query": normal_values(splits[6], (LAYERS, D, D), D ** -0.5, 0.21875, ((0, 2), (1, 16))),
        "w_key": normal_values(splits[7], (LAYERS, D, D), D ** -0.5, 0.21875, ((0, 2), (1, 16))),
        "w_value": normal_values(splits[8], (LAYERS, D, D), D ** -0.5, 0.21875, ((0, 2), (1, 16))),
        "w_out_attn": normal_values(splits[9], (LAYERS, D, D), (D // 16) ** -0.5, 0.875, ((0, 2), (1, 16))),
        "rel_table": normal_values(splits[10], (LAYERS, NB * HEADS), 1.0, 4.0, ((0, 2), (1, 16))),
        "router": normal_values(splits[11], (LAYERS, D, EXPERTS), (2 * D) ** -0.5, 0.15625, ((0, 2), (1, 16))),
        "expert_in": normal_values(splits[12], (LAYERS, EXPERTS, D, FF), D ** -0.5, 0.21875, ((0, 2), (1, 4), (3, 4))),
        "expert_out": normal_values(splits[13], (LAYERS, EXPERTS, FF, D), (max(1, FF // (EXPERTS * EXPERTS))) ** -0.5, 0.4375, ((0, 2), (1, 4), (2, 4))),
    }


EPSILON = 1e-06
MASK_FILL = -1e+30
HIGHEST = lax.Precision.HIGHEST

@jax.custom_vjp
def low(v):
    return lax.optimization_barrier(v.astype(jnp.bfloat16)).astype(jnp.float32)

@jax.custom_vjp
def low_back(v):
    return v

def low_keep(v):
    return (low(v), None)

def low_pass(kept, grad):
    return (grad,)

def back_keep(v):
    return (v, None)

def back_low(kept, grad):
    return (low(grad),)
low.defvjp(low_keep, low_pass)
low_back.defvjp(back_keep, back_low)

def normalize(resid_in, gain_in):
    return resid_in * lax.rsqrt(lax.optimization_barrier(jnp.mean(resid_in * resid_in, axis=-1, keepdims=True)) + EPSILON) * gain_in

def relative_bias(rel_flat, rel_bucket):
    table_grid = rel_flat.reshape(NB, HEADS)
    bucket_hot = (rel_bucket[:, None] == jnp.arange(NB, dtype=jnp.int32)[None, :]).astype(jnp.float32)
    per_offset = jnp.dot(bucket_hot, table_grid, precision=HIGHEST)
    span_len = (rel_bucket.shape[0] + 1) // 2
    positions = jnp.arange(span_len, dtype=jnp.int32)
    offsets = positions[None, :] - positions[:, None] + (span_len - 1)
    return jnp.transpose(per_offset[offsets], (2, 0, 1))

def gate_of(logits, chosen):
    return lax.optimization_barrier(jnp.sum(jax.nn.softmax(logits, axis=-1) * chosen, axis=-1))

def layer_forward(resid_in, seg_ids, route_ids, rel_bucket, params):
    gain_one, gain_two, w_query, w_key, w_value, w_attn_out, rel_flat, w_router, w_in, w_out = params
    groups, seq_length, model_width = resid_in.shape
    normed_one = low(normalize(resid_in, gain_one))

    def project(matrix):
        made_here = jnp.einsum('nsd,de->nse', normed_one, matrix, precision=HIGHEST)
        return low(low_back(made_here)).reshape(groups, seq_length, HEADS, HEAD_DIM)
    queries = project(w_query)
    keys_all = project(w_key)
    values = project(w_value)
    rel_bias = relative_bias(rel_flat, rel_bucket)
    scores = jnp.einsum('nqhd,nkhd->nhqk', queries, keys_all, precision=HIGHEST) * (1.0 / math.sqrt(HEAD_DIM)) + rel_bias[None]
    same_doc = seg_ids[:, :, None] == seg_ids[:, None, :]
    scores = low_back(jnp.where(same_doc[:, None], scores, MASK_FILL))
    row_max = lax.optimization_barrier(jnp.max(scores, axis=-1, keepdims=True))
    exp_scores = jnp.exp(scores - row_max)
    attn_probs = exp_scores / lax.optimization_barrier(jnp.sum(exp_scores, axis=-1, keepdims=True))
    context = jnp.einsum('nhqk,nkhd->nqhd', low(attn_probs), values, precision=HIGHEST)
    context = low(low_back(context.reshape(groups, seq_length, model_width)))
    hidden = resid_in + low_back(jnp.einsum('nsc,cd->nsd', context, w_attn_out, precision=HIGHEST))
    normed_two = low(normalize(hidden, gain_two))
    logits = low_back(jnp.einsum('nsd,de->nse', normed_two, w_router, precision=HIGHEST))
    expert_ids = jnp.arange(EXPERTS, dtype=jnp.int32)
    one_hot = (route_ids[..., None] == expert_ids).astype(jnp.int32)
    gate_value = gate_of(logits, one_hot.astype(jnp.float32))
    slot_rank = lax.optimization_barrier(jnp.sum((jnp.cumsum(one_hot, axis=1, dtype=jnp.int32) - one_hot) * one_hot, axis=-1, dtype=jnp.int32))
    slot_ids = jnp.arange(EXPERTS * CAP, dtype=jnp.int32)
    dispatch = ((route_ids * CAP + slot_rank)[..., None] == slot_ids).astype(jnp.float32)
    buffers = jnp.einsum('nsc,nsd->cnd', dispatch, normed_two, precision=HIGHEST)
    buffers = low_back(buffers.reshape(EXPERTS, CAP * groups, model_width))

    def one_expert(pieces):
        matrix_in, matrix_out, expert_rows = pieces
        pre_act = low_back(jnp.dot(expert_rows, matrix_in, precision=HIGHEST))
        activated = low(jax.nn.gelu(pre_act))
        return low(jnp.dot(activated, matrix_out, precision=HIGHEST))
    expert_rows_out = lax.map(one_expert, (w_in, w_out, buffers))
    expert_tok = jnp.einsum('nsc,cnd->nsd', dispatch, expert_rows_out.reshape(EXPERTS * CAP, groups, model_width), precision=HIGHEST)
    expert_tok = low_back(expert_tok)
    return low(hidden + gate_value[..., None] * expert_tok)

def reference(feed, segments, routes, rel_bucket, gain_attn, gain_ffn, w_query, w_key, w_value, w_out_attn, rel_table, router, expert_in, expert_out):
    weights = (gain_attn, gain_ffn, w_query, w_key, w_value, w_out_attn, rel_table, router, expert_in, expert_out)
    groups = MB * SEQS
    seg_ids = segments.reshape(groups, SEQ)
    route_ids = routes.reshape(LAYERS, groups, SEQ)
    first_in = feed[0].astype(jnp.float32).reshape(groups, SEQ, D)
    cotangent = feed[1].astype(jnp.float32).reshape(groups, SEQ, D)
    params_zero = tuple((weight_array[0].astype(jnp.float32) for weight_array in weights))
    params_one = tuple((weight_array[1].astype(jnp.float32) for weight_array in weights))
    out_zero, back_zero = jax.vjp(lambda resid_in, params: layer_forward(resid_in, seg_ids, route_ids[0], rel_bucket, params), first_in, params_zero)
    out_one, back_one = jax.vjp(lambda resid_in, params: layer_forward(resid_in, seg_ids, route_ids[1], rel_bucket, params), out_zero, params_one)
    grad_mid, grads_one = back_one(cotangent)
    grad_mid = low(grad_mid)
    grad_first, grads_zero = back_zero(grad_mid)
    layer_out = jnp.stack([out_zero, out_one]).reshape(LAYERS, MB, TOKENS, D).astype(jnp.bfloat16)
    layer_in_grad = jnp.stack([grad_first, grad_mid]).reshape(LAYERS, MB, TOKENS, D).astype(jnp.bfloat16)
    stacked = [jnp.stack([first_grad, second_grad]) for first_grad, second_grad in zip(grads_zero, grads_one)]
    return (layer_out, layer_in_grad, stacked[0], stacked[1], stacked[2], stacked[3], stacked[4], stacked[5], stacked[6], stacked[7], stacked[8], stacked[9])
```

```python
import math

import jax
import jax.numpy as jnp
from jax import lax
from jax.sharding import PartitionSpec as P

HEADS = 12
HEAD_DIM = 64
NB = 32
EXT = 128
EPSILON = 1e-06
MASK_FILL = -1e30
BF = jnp.bfloat16
F32 = jnp.float32


def dot(a, b):
    return jnp.dot(a, b, preferred_element_type=F32)


def dot_t(a, b):
    return lax.dot_general(a, b, (((1,), (1,)), ((), ())), preferred_element_type=F32)


def t_dot(a, b):
    return lax.dot_general(a, b, (((0,), (0,)), ((), ())), preferred_element_type=F32)


def swap(value):
    return lax.ppermute(value, "section", [(0, 1), (1, 0)])


def direct(axis):
    count = lax.axis_size(axis)
    return count <= 4 and count & (count - 1) == 0


def peer_ids(axis):
    count = lax.axis_size(axis)
    ids = jnp.arange(count, dtype=jnp.int32)
    return ids ^ lax.axis_index(axis) if direct(axis) else ids


def hop(value, axis, step):
    count = lax.axis_size(axis)
    return lax.ppermute(value, axis, [(i, i ^ step) for i in range(count)])


def spread(value, axis):
    count = lax.axis_size(axis)
    if direct(axis):
        return [value] + [hop(value, axis, step) for step in range(1, count)]
    every = lax.all_gather(value, axis, axis=0)
    return [every[i] for i in range(count)]


def exchange(blocks, axis):
    count = lax.axis_size(axis)
    if direct(axis):
        return [blocks[0]] + [hop(blocks[step], axis, step) for step in range(1, count)]
    swapped = lax.all_to_all(jnp.stack(blocks), axis, 0, 0, tiled=True)
    return [swapped[i] for i in range(count)]


def ordered(pieces, axis):
    count = len(pieces)
    ids = peer_ids(axis)
    rows = pieces[0].shape[0]
    joined = jnp.zeros((count * rows,) + pieces[0].shape[1:], pieces[0].dtype)
    for place in range(count):
        joined = lax.dynamic_update_slice(joined, pieces[place], (ids[place] * rows, 0))
    return joined


def gather_rows(part):
    if direct("expert") and direct("shard"):
        plane = ordered(spread(part, "shard"), "shard")
        return ordered(spread(plane, "expert"), "expert")
    return lax.all_gather(part, ("expert", "shard"), axis=0, tiled=True)


def scatter_rows(whole):
    for axis in ("expert", "shard"):
        count = lax.axis_size(axis)
        rows = whole.shape[0] // count
        ids = peer_ids(axis)
        blocks = [
            lax.dynamic_slice_in_dim(whole, ids[i] * rows, rows, axis=0).astype(BF)
            for i in range(count)
        ]
        whole = sum(block.astype(F32) for block in exchange(blocks, axis))
    return whole


def inverse_rms(value):
    return lax.rsqrt(jnp.mean(value * value, axis=-1, keepdims=True) + EPSILON)


def norm_back(value, gain, grad):
    scale = inverse_rms(value)
    scaled = value * scale
    gained = grad * gain
    back = scale * (gained - scaled * jnp.mean(gained * scaled, axis=-1, keepdims=True))
    return back, jnp.sum(grad * scaled, axis=0)


def gelu_parts(value):
    c = math.sqrt(2.0 / math.pi)
    inner = jnp.tanh(c * (value + 0.044715 * value * value * value))
    grad = 0.5 * (1.0 + inner) + 0.5 * value * (1.0 - inner * inner) * (
        c * (1.0 + 3.0 * 0.044715 * value * value)
    )
    return 0.5 * value * (1.0 + inner), grad


def body(
    feed, segments, routes, rel_bucket, gain_attn, gain_ffn, w_query, w_key, w_value, w_out_attn,
    rel_table, router, expert_in, expert_out,
):
    seq = feed.shape[2]
    width = feed.shape[3]
    experts = lax.axis_size("expert")
    shards = lax.axis_size("shard")
    cap = max(2, 2 * seq // experts)
    own_rows = w_query.shape[1]
    sec = lax.axis_index("section")
    first = sec == 0
    score_scale = 1.0 / math.sqrt(HEAD_DIM)

    table_rows = rel_table.shape[1]
    ext = jnp.concatenate(
        [
            gain_attn[0][:, None],
            gain_ffn[0][:, None],
            jnp.pad(rel_table[0], (0, own_rows - table_rows))[:, None],
            router[0],
            jnp.zeros((own_rows, EXT - 3 - experts), BF),
        ],
        axis=1,
    )
    half_a = jnp.concatenate([w_query[0], w_key[0], ext], axis=1)
    half_b = jnp.concatenate([w_value[0], w_out_attn[0], ext], axis=1)
    came = swap(jnp.where(first, half_b, half_a))
    parts = [jnp.where(first, half_a, came), jnp.where(first, came, half_b)]

    came = swap(jnp.where(first, feed[0, 1], feed[0, 0]))
    layer_x = jnp.where(first, feed[0, 0], came)
    layer_dy = jnp.where(first, came, feed[0, 1])
    came = swap(jnp.where(first, routes[0, 1, 0], routes[0, 0, 0]))
    kept = jnp.where(first, routes[0, 0, 0], routes[0, 1, 0])
    my_routes = jnp.stack([jnp.where(first, kept, came), jnp.where(first, came, kept)])
    seg_ids = jnp.where(first, segments[0, 0], segments[1, 0])
    came_in = swap(expert_in[0, 0])
    came_out = swap(expert_out[0, 0])
    w_in = [jnp.where(first, expert_in[0, 0], came_in), jnp.where(first, came_in, expert_in[0, 0])]
    w_out = [
        jnp.where(first, expert_out[0, 0], came_out),
        jnp.where(first, came_out, expert_out[0, 0]),
    ]

    all_routes = jnp.stack(spread(my_routes, "shard"), axis=1)
    hot = (all_routes[..., None] == peer_ids("expert")).astype(BF)
    positions = jnp.arange(seq, dtype=jnp.int32)
    before = (positions[:, None] > positions[None, :]).astype(BF)
    rank = jnp.einsum("ij,lzje->lzie", before, hot, preferred_element_type=F32)
    slot_in = jnp.arange(cap, dtype=jnp.int32).astype(F32)
    dispatch = (hot[..., None] * (rank[..., None] == slot_in).astype(BF)).reshape(
        2, shards, seq, experts * cap
    )
    chosen = (my_routes[..., None] == jnp.arange(experts, dtype=jnp.int32)).astype(F32)
    bucket_ij = jnp.stack([rel_bucket[seq - 1 - i : 2 * seq - 1 - i] for i in range(seq)])
    bucket_hot = (
        bucket_ij.reshape(1, seq * seq) == jnp.arange(NB, dtype=jnp.int32)[:, None]
    ).astype(BF)
    same_doc = seg_ids[:, None] == seg_ids[None, :]

    weights = []
    for layer in range(2):
        mine = gather_rows(parts[layer])
        other = swap(mine)
        whole_a = jnp.where(first, mine, other)
        whole_b = jnp.where(first, other, mine)
        side = whole_a[:, 2 * width :]
        table = side[:, 2].reshape(-1, own_rows)[:, :table_rows].reshape(NB, HEADS)
        weights.append(
            dict(
                qkv=jnp.concatenate([whole_a[:, : 2 * width], whole_b[:, :width]], axis=1),
                out=whole_b[:, width : 2 * width],
                gain_one=side[:, 0].astype(F32),
                gain_two=side[:, 1].astype(F32),
                router=side[:, 3 : 3 + experts],
                bias=t_dot(table, bucket_hot).reshape(HEADS, seq, seq),
            )
        )

    def to_experts(layer, tokens):
        every = jnp.stack(spread(tokens, "shard"))
        slots = jnp.einsum("zsc,zsd->czd", dispatch[layer], every, preferred_element_type=F32)
        slots = slots.astype(BF).reshape(experts, cap * shards, width)
        return jnp.concatenate(exchange([slots[i] for i in range(experts)], "expert"), axis=0)

    def to_tokens(layer, rows):
        rows = rows.astype(BF).reshape(experts, cap * shards, width)
        back = jnp.stack(exchange([rows[i] for i in range(experts)], "expert"))
        back = back.reshape(experts * cap, shards, width)
        tokens = jnp.einsum("zsc,czd->zsd", dispatch[layer], back, preferred_element_type=F32)
        tokens = tokens.astype(BF)
        return sum(
            piece.astype(F32) for piece in exchange([tokens[i] for i in range(shards)], "shard")
        )

    def heads(value):
        return value.reshape(seq, HEADS, HEAD_DIM)

    def forward(layer, x_low):
        w = weights[layer]
        x = x_low.astype(F32)
        normed_one = (x * inverse_rms(x) * w["gain_one"]).astype(BF)
        qkv = dot(normed_one, w["qkv"]).astype(BF)
        queries, keys_all, values = [heads(qkv[:, i * width : (i + 1) * width]) for i in range(3)]
        scores = jnp.einsum("qhd,khd->hqk", queries, keys_all, preferred_element_type=F32)
        scores = jnp.where(same_doc[None], scores * score_scale + w["bias"], MASK_FILL)
        exp_scores = jnp.exp(scores - jnp.max(scores, axis=-1, keepdims=True))
        probs = exp_scores / jnp.sum(exp_scores, axis=-1, keepdims=True)
        context = jnp.einsum("hqk,khd->qhd", probs.astype(BF), values, preferred_element_type=F32)
        context = context.reshape(seq, width).astype(BF)
        hidden = x + dot(context, w["out"])
        normed_two = (hidden * inverse_rms(hidden) * w["gain_two"]).astype(BF)
        gates = jax.nn.softmax(dot(normed_two, w["router"]), axis=-1)
        gate_value = jnp.sum(gates * chosen[layer], axis=-1, keepdims=True)
        rows = to_experts(layer, normed_two)
        pre_act = dot(rows, w_in[layer])
        activated = gelu_parts(pre_act)[0].astype(BF)
        expert_tok = to_tokens(layer, dot(activated, w_out[layer])).astype(BF).astype(F32)
        out = (hidden + gate_value * expert_tok).astype(BF)
        return out, (
            x, normed_one, queries, keys_all, values, probs, context, hidden, normed_two, gates,
            gate_value, rows, pre_act, activated, expert_tok,
        )

    def backward(layer, dy_low, state):
        (
            x, normed_one, queries, keys_all, values, probs, context, hidden, normed_two, gates,
            gate_value, rows, pre_act, activated, expert_tok,
        ) = state
        w = weights[layer]
        dy = dy_low.astype(F32)
        grad_gate = jnp.sum(dy * expert_tok, axis=-1, keepdims=True)
        spread_rows = to_experts(layer, (gate_value * dy).astype(BF))
        grad_act = dot_t(spread_rows, w_out[layer])
        grad_pre = (grad_act * gelu_parts(pre_act)[1]).astype(BF)
        grad_rows = to_tokens(layer, dot_t(grad_pre, w_in[layer]))
        grad_in = t_dot(rows, grad_pre)
        grad_out = t_dot(activated, spread_rows)
        grad_logits = (grad_gate * gate_value * (chosen[layer] - gates)).astype(BF)
        grad_norm_two = grad_rows.astype(BF).astype(F32) + dot_t(grad_logits, w["router"])
        back, grad_gain_two = norm_back(hidden, w["gain_two"], grad_norm_two)
        grad_hidden = dy + back
        grad_hidden_low = grad_hidden.astype(BF)
        grad_context = heads(dot_t(grad_hidden_low, w["out"]).astype(BF))
        grad_probs = jnp.einsum("qhd,khd->hqk", grad_context, values, preferred_element_type=F32)
        grad_scores = probs * (grad_probs - jnp.sum(probs * grad_probs, axis=-1, keepdims=True))
        grad_scores = grad_scores.astype(BF)
        grad_q = jnp.einsum("hqk,khd->qhd", grad_scores, keys_all, preferred_element_type=F32)
        grad_k = jnp.einsum("hqk,qhd->khd", grad_scores, queries, preferred_element_type=F32)
        grad_v = jnp.einsum(
            "hqk,qhd->khd", probs.astype(BF), grad_context, preferred_element_type=F32
        )
        grad_joint = jnp.concatenate(
            [
                (grad_q * score_scale).reshape(seq, width),
                (grad_k * score_scale).reshape(seq, width),
                grad_v.reshape(seq, width),
            ],
            axis=1,
        ).astype(BF)
        grad_normed = dot_t(grad_joint, w["qkv"])
        back, grad_gain_one = norm_back(x, w["gain_one"], grad_normed)
        dx = (grad_hidden + back).astype(BF)
        grad_table = dot_t(bucket_hot, grad_scores.reshape(HEADS, seq * seq))
        grad_table = jnp.pad(
            grad_table.reshape(-1, table_rows), ((0, 0), (0, own_rows - table_rows))
        ).reshape(width, 1)
        side = jnp.concatenate(
            [
                grad_gain_one[:, None],
                grad_gain_two[:, None],
                grad_table,
                t_dot(normed_two, grad_logits),
                jnp.zeros((width, EXT - 3 - experts), F32),
            ],
            axis=1,
        ).astype(BF)
        grad_qkv = t_dot(normed_one, grad_joint).astype(BF)
        grad_attn = t_dot(context, grad_hidden_low).astype(BF)
        grad_a = jnp.concatenate([grad_qkv[:, : 2 * width], side], axis=1)
        grad_b = jnp.concatenate([grad_qkv[:, 2 * width :], grad_attn, jnp.zeros_like(side)], axis=1)
        kept = jnp.where(first, grad_a, grad_b).astype(F32)
        summed = kept + swap(jnp.where(first, grad_b, grad_a)).astype(F32)
        return dx, scatter_rows(summed), (grad_in, grad_out)

    out_zero, state_zero = forward(0, layer_x)
    out_one, state_one = forward(1, out_zero)
    dx_one, sum_one, experts_one = backward(1, layer_dy, state_one)
    dx_zero, sum_zero, experts_zero = backward(0, dx_one, state_zero)

    came = swap(jnp.where(first, sum_one, sum_zero))
    kept = jnp.where(first, sum_zero, sum_one)
    final_a = jnp.where(first, kept, came)
    final_b = jnp.where(first, came, kept)

    def own_expert(zero, one):
        return jnp.where(first, zero, one) + swap(jnp.where(first, one, zero).astype(BF)).astype(F32)

    def by_batch(zero, one):
        came = swap(jnp.where(first, one, zero))
        kept = jnp.where(first, zero, one)
        return jnp.stack([jnp.where(first, kept, came), jnp.where(first, came, kept)])

    side = final_a[:, 2 * width :]
    return (
        by_batch(out_zero, out_one)[None],
        by_batch(dx_zero, dx_one)[None],
        side[:, 0][None],
        side[:, 1][None],
        final_a[:, :width][None],
        final_a[:, width : 2 * width][None],
        final_b[:, :width][None],
        final_b[:, width : 2 * width][None],
        side[:table_rows, 2][None],
        side[:, 3 : 3 + experts][None],
        own_expert(experts_zero[0], experts_one[0])[None, None],
        own_expert(experts_zero[1], experts_one[1])[None, None],
    )


def solution(mesh):
    rows = ("expert", "shard")
    tokens = P("section", None, rows, None)
    matrix = P("section", rows, None)
    vector = P("section", rows)
    expert_specs = (P("section", "expert", None, "shard"), P("section", "expert", "shard", None))
    in_specs = (
        tokens, P(None, rows, None), tokens, P(), vector, vector, matrix, matrix, matrix, matrix,
        vector, matrix, *expert_specs,
    )
    out_specs = (
        tokens, tokens, vector, vector, matrix, matrix, matrix, matrix, vector, matrix,
        *expert_specs,
    )
    return jax.shard_map(body, mesh=mesh, in_specs=in_specs, out_specs=out_specs, check_vma=False)
```

```python
import functools
import math

import jax
import jax.numpy as jnp
import numpy as np
from jax import lax
from jax.experimental import pallas as pl
from jax.experimental.pallas import tpu as pltpu
from jax.sharding import PartitionSpec as P

HEADS = 12
HEAD_DIM = 64
NB = 32
EXT = 128
LEAD = 3
EPSILON = 1e-06
MASK_FILL = -1e30
BF = jnp.bfloat16
F32 = jnp.float32
VM = pl.BlockSpec(memory_space=pltpu.VMEM)
SM = pl.BlockSpec(memory_space=pltpu.SMEM)
HB = pl.BlockSpec(memory_space=pl.ANY)


def dot(a, b):
    return jnp.dot(a, b, preferred_element_type=F32)


def dot_t(a, b):
    return lax.dot_general(a, b, (((1,), (1,)), ((), ())), preferred_element_type=F32)


def t_dot(a, b):
    return lax.dot_general(a, b, (((0,), (0,)), ((), ())), preferred_element_type=F32)


def swap(value):
    return lax.ppermute(value, "section", [(0, 1), (1, 0)])


def direct(axis):
    count = lax.axis_size(axis)
    return count <= 4 and count & (count - 1) == 0


def peer_ids(axis):
    count = lax.axis_size(axis)
    ids = jnp.arange(count, dtype=jnp.int32)
    return ids ^ lax.axis_index(axis) if direct(axis) else ids


def hop(value, axis, step):
    count = lax.axis_size(axis)
    return lax.ppermute(value, axis, [(i, i ^ step) for i in range(count)])


def spread(value, axis):
    count = lax.axis_size(axis)
    if direct(axis):
        return [value] + [hop(value, axis, step) for step in range(1, count)]
    every = lax.all_gather(value, axis, axis=0)
    return [every[i] for i in range(count)]


def exchange(blocks, axis):
    count = lax.axis_size(axis)
    if direct(axis):
        return [blocks[0]] + [hop(blocks[step], axis, step) for step in range(1, count)]
    swapped = lax.all_to_all(jnp.stack(blocks), axis, 0, 0, tiled=True)
    return [swapped[i] for i in range(count)]


def scatter_rows(whole):
    for axis in ("expert", "shard"):
        count = lax.axis_size(axis)
        rows = whole.shape[0] // count
        ids = peer_ids(axis)
        blocks = [
            lax.dynamic_slice_in_dim(whole, ids[i] * rows, rows, axis=0).astype(BF)
            for i in range(count)
        ]
        whole = sum(block.astype(F32) for block in exchange(blocks, axis))
    return whole


def call(kernel, outs, ins, specs, scratch=(), flops=0):
    moved = sum(math.prod(a.shape) * a.dtype.itemsize for a in (*ins, *outs))
    return pl.pallas_call(
        kernel,
        out_shape=list(outs),
        in_specs=list(specs),
        out_specs=[VM] * len(outs),
        scratch_shapes=list(scratch),
        compiler_params=pltpu.CompilerParams(vmem_limit_bytes=48 * 1024 * 1024),
        cost_estimate=pl.CostEstimate(flops=flops, bytes_accessed=moved, transcendentals=0),
    )(*ins)


def out(shape, kind=BF):
    return jax.ShapeDtypeStruct(shape, kind)


def start_weights(place, pieces, held, sems):
    count = len(pieces) // 2
    rows = pieces[0].shape[0]
    copies = []
    for part in range(2):
        for i in range(count):
            target = place[0] if part == 0 else 1 - place[0]
            first = pl.multiple_of(place[2 + i] * rows, rows) if count > 1 else 0
            copies.append(
                pltpu.make_async_copy(
                    pieces[part * count + i],
                    held.at[target, pl.ds(first, rows), :],
                    sems.at[part * count + i],
                )
            )
    for copy in copies:
        copy.start()
    return copies


def inverse_rms(value):
    return lax.rsqrt(jnp.mean(value * value, axis=-1, keepdims=True) + EPSILON)


def norm_back(value, gain, grad):
    scale = inverse_rms(value)
    scaled = value * scale
    gained = grad * gain
    back = scale * (gained - scaled * jnp.mean(gained * scaled, axis=-1, keepdims=True))
    return back, jnp.sum(grad * scaled, axis=0, keepdims=True)


def gain_rows(side):
    pick = (
        lax.broadcasted_iota(jnp.int32, (16, EXT), 0)
        == lax.broadcasted_iota(jnp.int32, (16, EXT), 1)
    ).astype(BF)
    rows = dot_t(pick, side)
    return rows[0:1], rows[1:2]


def gelu_parts(value):
    c = math.sqrt(2.0 / math.pi)
    square = value * value
    inner = jnp.tanh(c * (value + 0.044715 * square * value))
    grad = 0.5 * (1.0 + inner) + 0.5 * value * (1.0 - inner * inner) * (
        c + (3.0 * 0.044715 * c) * square
    )
    return 0.5 * value * (1.0 + inner), grad


def softmax_lanes(logits, experts):
    lane = lax.broadcasted_iota(jnp.int32, logits.shape, 1)
    valid = (lane >= LEAD) & (lane < LEAD + experts)
    logits = jnp.where(valid, logits, MASK_FILL)
    power = jnp.exp(logits - jnp.max(logits, axis=-1, keepdims=True))
    power = jnp.where(valid, power, 0.0)
    return power / jnp.sum(power, axis=-1, keepdims=True), lane


def pair_rows(value):
    low_lanes = lax.broadcasted_iota(jnp.int32, value.shape, 1) < HEAD_DIM
    zero = jnp.zeros_like(value)
    return jnp.concatenate(
        [jnp.where(low_lanes, value, zero), jnp.where(low_lanes, zero, value)], axis=0
    )


def pair_lanes(value):
    half = value.shape[0] // 2
    low_lanes = lax.broadcasted_iota(jnp.int32, (half, value.shape[1]), 1) < HEAD_DIM
    return jnp.where(low_lanes, value[:half], value[half:])


def attn_forward(layer, seq, width, experts, count, *refs):
    place, route, seg_col, seg_row, bucket, bucket_of, head_sel = refs[:7]
    refs = refs[7:]
    pieces, refs = refs[: 2 * count], refs[2 * count :]
    if layer == 0:
        (x_ref,), refs = refs[:1], refs[1:]
    else:
        (hid_ref, gate_ref), toks, refs = refs[:2], refs[2:-12], refs[-12:]
        (out_ref, tok_ref), refs = refs[:2], refs[2:]
    n2_ref, state, probs_ref, hidden_ref, gates_ref, gv_ref, ext_ref, held, sems, qkv = refs
    copies = start_weights(place, pieces, held, sems)
    if layer == 0:
        x = x_ref[...].astype(F32)
    else:
        tok = sum(t[...].astype(F32) for t in toks).astype(BF)
        tok_ref[...] = tok
        low = (hid_ref[...] + gate_ref[:, 0:1] * tok.astype(F32)).astype(BF)
        out_ref[...] = low
        x = low.astype(F32)
    scaled = x * inverse_rms(x)
    same = seg_col[...] == seg_row[...]
    for copy in copies:
        copy.wait()
    side = held[0, :, 2 * width : 2 * width + EXT]
    ext_ref[...] = side
    gain_one, gain_two = gain_rows(side)
    values = jnp.where(
        bucket_of[...] == bucket[...], side[:, 2:3].astype(F32), 0.0
    ).astype(BF)
    table = dot(head_sel[...], values)
    normed = (scaled * gain_one).astype(BF)
    state[:, :width] = normed
    qkv[:, : 2 * width] = dot(normed, held[0, :, : 2 * width]).astype(BF)
    qkv[:, 2 * width :] = dot(normed, held[1, :, :width]).astype(BF)
    state[:, width : 4 * width] = qkv[...]
    scale = 1.0 / math.sqrt(HEAD_DIM)
    contexts = []
    for p in range(HEADS // 2):
        lanes = slice(128 * p, 128 * p + 128)
        q2 = pair_rows(qkv[:, lanes])
        scores = dot_t(q2, qkv[:, width + 128 * p : width + 128 * p + 128]) * scale
        parts = []
        for h in (2 * p, 2 * p + 1):
            line = jnp.broadcast_to(table[h : h + 1], (seq, 2 * seq))
            bias = pltpu.roll(line, seq + 1, axis=1, stride=1, stride_axis=0)[:, :seq]
            part = scores[seq * (h - 2 * p) : seq * (h - 2 * p) + seq] + bias
            parts.append(jnp.where(same, part, MASK_FILL))
        scores = jnp.concatenate(parts, axis=0)
        power = jnp.exp(scores - jnp.max(scores, axis=-1, keepdims=True))
        probs = power / jnp.sum(power, axis=-1, keepdims=True)
        probs_ref[p] = probs
        vals = qkv[:, 2 * width + 128 * p : 2 * width + 128 * p + 128]
        contexts.append(pair_lanes(dot(probs.astype(BF), vals)))
    context = jnp.concatenate(contexts, axis=1).astype(BF)
    state[:, 4 * width :] = context
    hidden = x + dot(context, held[1, :, width : 2 * width])
    hidden_ref[...] = hidden
    normed_two = (hidden * inverse_rms(hidden) * gain_two).astype(BF)
    n2_ref[...] = normed_two
    gates, lane = softmax_lanes(dot(normed_two, side), experts)
    gates_ref[...] = gates
    value = jnp.sum(jnp.where(lane == route[...] + LEAD, gates, 0.0), axis=-1, keepdims=True)
    gv_ref[...] = jnp.broadcast_to(value, gv_ref.shape)


def dispatch_rows(count, shards, cap, *refs):
    hot = refs[0]
    toks = refs[1 : 1 + shards]
    blocks = refs[1 + shards :]
    for z in range(shards):
        rows = dot(hot[z], toks[z][...]).astype(BF)
        for i in range(count):
            blocks[i][z * cap : (z + 1) * cap, :] = rows[i * cap : (i + 1) * cap]


def combine_rows(count, shards, cap, *refs):
    hot = refs[0]
    blocks = refs[1 : 1 + count]
    toks = refs[1 + count :]
    for z in range(shards):
        rows = jnp.concatenate([b[z * cap : (z + 1) * cap, :] for b in blocks], axis=0)
        toks[z][...] = dot(hot[z], rows).astype(BF)


def start_expert(layer, place, own, came, held, sems):
    def begin(pair):
        for i in range(2):
            pltpu.make_async_copy(pair[i], held.at[i], sems.at[i]).start()

    @pl.when(place[0] == layer)
    def _():
        begin(own)

    @pl.when(place[0] != layer)
    def _():
        begin(came)

    return [pltpu.make_async_copy(own[i], held.at[i], sems.at[i]) for i in range(2)]


def expert_forward(layer, count, *refs):
    place, own, came = refs[0], refs[1:3], refs[3:5]
    blocks = refs[5 : 5 + count]
    results = refs[5 + count : 5 + 2 * count]
    held, sems = refs[5 + 2 * count :]
    copies = start_expert(layer, place, own, came, held, sems)
    for copy in copies:
        copy.wait()
    for i in range(count):
        pre_act = dot(blocks[i][...], held[0])
        activated = gelu_parts(pre_act)[0].astype(BF)
        results[i][...] = dot(activated, held[1]).astype(BF)


def expert_backward(layer, count, experts, with_out, *refs):
    place, own, came, ext = refs[0], refs[1:3], refs[3:5], refs[5]
    blocks = refs[6 : 6 + count]
    dys = refs[6 + count : 6 + 2 * count]
    refs = refs[6 + 2 * count :]
    grads, refs = refs[:count], refs[count:]
    if with_out:
        results, refs = refs[:count], refs[count:]
    keep, held, sems = refs
    copies = start_expert(layer, place, own, came, held, sems)
    rows_each = blocks[0].shape[0]
    for copy in copies:
        copy.wait()
    for i in range(count):
        at = slice(i * rows_each, (i + 1) * rows_each)
        rows = blocks[i][...]
        gates, lane = softmax_lanes(dot(rows, ext[...]), experts)
        mine = (lane == place[1] + LEAD).astype(F32)
        value = jnp.sum(gates * mine, axis=-1, keepdims=True)
        dy = dys[i][...].astype(F32)
        grad_expert = (value * dy).astype(BF)
        act, slope = gelu_parts(dot(rows, held[0]))
        act = act.astype(BF)
        grad_pre = (dot_t(grad_expert, held[1]) * slope).astype(BF)
        grad = dot_t(grad_pre, held[0])
        if with_out:
            result = dot(act, held[1])
            results[i][...] = result.astype(BF)
            grad_gate = jnp.sum(dy * result, axis=-1, keepdims=True)
            grad_logits = (grad_gate * value * (mine - gates)).astype(BF)
            grad = grad + dot_t(grad_logits, ext[...])
        grads[i][...] = grad.astype(BF)
        keep[0, at, :] = rows
        keep[1, at, :] = grad_pre
        keep[2, at, :] = act
        keep[3, at, :] = grad_expert


def attn_backward(layer, seq, width, experts, count, shards, *refs):
    place, route, bucket_back, bucket_of, head_sel = refs[:5]
    pieces, refs = refs[5 : 5 + 2 * count], refs[5 + 2 * count :]
    dy_ref, x_ref, state, probs_ref, hidden_ref, n2_ref, gates_ref, gv_ref, tok_ref = refs[:9]
    parts, refs = refs[9 : 9 + shards], refs[9 + shards :]
    dx_ref, ship, stay, side_grad, held, sems, gj, g_rel = refs
    copies = start_weights(place, pieces, held, sems)
    dy = dy_ref[...].astype(F32)
    grad_norm_two = sum(p[...].astype(F32) for p in parts)
    hidden = hidden_ref[...]
    x = x_ref[...].astype(F32)
    for copy in copies:
        copy.wait()
    side = held[0, :, 2 * width : 2 * width + EXT]
    gain_one, gain_two = gain_rows(side)
    side_grad[...] = jnp.zeros_like(side_grad)
    if layer == 0:
        gates = gates_ref[...]
        lane = lax.broadcasted_iota(jnp.int32, gates.shape, 1)
        hot = (lane == route[...] + LEAD).astype(F32)
        grad_gate = jnp.sum(dy * tok_ref[...].astype(F32), axis=-1, keepdims=True)
        grad_logits = (grad_gate * gv_ref[:, 0:1] * (hot - gates)).astype(BF)
        grad_norm_two = grad_norm_two + dot_t(grad_logits, side)
        router_rows = t_dot(grad_logits, n2_ref[...])
        side_grad[...] = router_rows[: side_grad.shape[0]]
    back, gain_two_grad = norm_back(hidden, gain_two, grad_norm_two)
    grad_hidden = dy + back
    grad_hidden_low = grad_hidden.astype(BF)
    grad_context = dot_t(grad_hidden_low, held[1, :, width : 2 * width]).astype(BF)
    scale = 1.0 / math.sqrt(HEAD_DIM)
    mirror = (
        lax.broadcasted_iota(jnp.int32, (seq, 2 * seq), 0)
        + lax.broadcasted_iota(jnp.int32, (seq, 2 * seq), 1)
        == seq - 1
    ).astype(BF)
    for p in range(HEADS // 2):
        lanes = slice(128 * p, 128 * p + 128)
        q2 = pair_rows(state[:, width + 128 * p : width + 128 * p + 128])
        keys = state[:, 2 * width + 128 * p : 2 * width + 128 * p + 128]
        vals = state[:, 3 * width + 128 * p : 3 * width + 128 * p + 128]
        g2 = pair_rows(grad_context[:, lanes])
        probs = probs_ref[p]
        grad_probs = dot_t(g2, vals)
        grad_scores = probs * (
            grad_probs - jnp.sum(probs * grad_probs, axis=-1, keepdims=True)
        )
        grad_scores = grad_scores.astype(BF)
        gj[:, lanes] = (pair_lanes(dot(grad_scores, keys)) * scale).astype(BF)
        gj[:, width + 128 * p : width + 128 * p + 128] = (t_dot(grad_scores, q2) * scale).astype(BF)
        gj[:, 2 * width + 128 * p : 2 * width + 128 * p + 128] = t_dot(
            probs.astype(BF), g2
        ).astype(BF)
        turned = dot(grad_scores, mirror)
        for h in range(2):
            shifted = pltpu.roll(turned[h * seq : (h + 1) * seq], 0, axis=1, stride=1, stride_axis=0)
            g_rel[2 * p + h : 2 * p + h + 1, :] = jnp.sum(shifted, axis=0, keepdims=True)
    g_rel[HEADS:, :] = jnp.zeros_like(g_rel[HEADS:, :])
    buckets = (bucket_of[...] == bucket_back[...]).astype(BF)
    offsets = g_rel[...]
    high = offsets.astype(BF)
    low = (offsets - high.astype(F32)).astype(BF)
    by_row = dot_t(high, buckets) + dot_t(low, buckets)
    side_grad[2:3, :] = jnp.sum(by_row * head_sel[...].astype(F32), axis=0, keepdims=True)
    side_grad[1:2, :] = gain_two_grad
    grad_normed = dot_t(gj[:, : 2 * width], held[0, :, : 2 * width]) + dot_t(
        gj[:, 2 * width :], held[1, :, :width]
    )
    back, gain_one_grad = norm_back(x, gain_one, grad_normed)
    side_grad[0:1, :] = gain_one_grad
    dx_ref[...] = (grad_hidden + back).astype(BF)
    normed = state[:, :width]
    halves = (ship, stay)
    for core in range(2):

        @pl.when(place[0] == core)
        def _(core=core):
            halves[1 - core][:, :width] = normed
            halves[1 - core][:, width : 3 * width] = gj[:, : 2 * width]
            halves[1 - core][:, 3 * width :] = jnp.zeros_like(normed)
            halves[core][:, :width] = normed
            halves[core][:, width : 2 * width] = gj[:, 2 * width :]
            halves[core][:, 2 * width : 3 * width] = state[:, 4 * width :]
            halves[core][:, 3 * width :] = grad_hidden_low


def last_output(experts, shards, *refs):
    route, dy_ref, hidden_ref, n2_ref, gates_ref, gv_ref, side_in = refs[:7]
    parts, refs = refs[7 : 7 + shards], refs[7 + shards :]
    out_ref, side_grad = refs
    tok = sum(p[...].astype(F32) for p in parts).astype(BF).astype(F32)
    value = gv_ref[:, 0:1]
    out_ref[...] = (hidden_ref[...] + value * tok).astype(BF)
    gates = gates_ref[...]
    lane = lax.broadcasted_iota(jnp.int32, gates.shape, 1)
    hot = (lane == route[...] + LEAD).astype(F32)
    grad_gate = jnp.sum(dy_ref[...].astype(F32) * tok, axis=-1, keepdims=True)
    grad_logits = (grad_gate * value * (hot - gates)).astype(BF)
    side_grad[...] = side_in[...] + t_dot(grad_logits, n2_ref[...])[: side_grad.shape[0]]


def attn_weights(width, count, *refs):
    place, stay, came, side_a, side_b = refs[:5]
    blocks, total = refs[5 : 5 + count], refs[-1]

    def both(first, last):
        return jnp.concatenate([stay[:, first:last], came[:, first:last]], axis=0)

    @pl.when(place[0] == 0)
    def _():
        total[:, : 2 * width] = t_dot(both(0, width), both(width, 3 * width)).astype(BF)
        side = side_a[...] + side_b[...]
        pick = (
            lax.broadcasted_iota(jnp.int32, (side.shape[0], EXT), 0)
            == lax.broadcasted_iota(jnp.int32, (side.shape[0], EXT), 1)
        ).astype(BF)
        total[:, 2 * width :] = t_dot(side.astype(BF), pick).astype(BF)

    @pl.when(place[0] != 0)
    def _():
        total[:, :width] = t_dot(both(0, width), both(width, 2 * width)).astype(BF)
        total[:, width : 2 * width] = t_dot(
            both(2 * width, 3 * width), both(3 * width, 4 * width)
        ).astype(BF)
        total[:, 2 * width :] = jnp.zeros_like(total[:, 2 * width :])

    rows = blocks[0].shape[0]
    for i in range(count):
        first = pl.multiple_of(place[2 + i] * rows, rows) if count > 1 else 0
        blocks[i][...] = total[pl.ds(first, rows), :]


def sum_blocks(count, at, *refs):
    place, parts = refs[0], refs[1 : 1 + count]
    blocks, total = refs[1 + count : -1], refs[-1]
    total[...] = sum(p[...].astype(F32) for p in parts)
    rows = blocks[0].shape[0]
    for i, block in enumerate(blocks):
        first = pl.multiple_of(place[at + i] * rows, rows) if len(blocks) > 1 else 0
        block[...] = total[pl.ds(first, rows), :].astype(block.dtype)


def join_rows(count, first_id, *refs):
    place, parts, whole, sems = refs[0], refs[1 : 1 + count], refs[1 + count], refs[2 + count]
    rows = parts[0].shape[0]
    copies = []
    for i in range(count):
        first = pl.multiple_of(place[first_id + i] * rows, rows)
        copies.append(pltpu.make_async_copy(parts[i], whole.at[pl.ds(first, rows), :], sems.at[i]))
    for copy in copies:
        copy.start()
    for copy in copies:
        copy.wait()


def expert_weights(other, *refs):
    place, keeps, refs = refs[0], refs[1:3], refs[3:]
    if other:
        in_ref, out_ref, held, sem = refs
    else:
        came_in, came_out, in_ref, out_ref, held, sem = refs
    for layer in range(2):

        @pl.when((place[0] == layer) != other)
        def _(layer=layer):
            pltpu.make_async_copy(keeps[layer], held, sem).start()

    pltpu.make_async_copy(keeps[0], held, sem).wait()
    grad_in = t_dot(held[0], held[1])
    grad_out = t_dot(held[2], held[3])
    if not other:
        grad_in = grad_in + came_in[...].astype(F32)
        grad_out = grad_out + came_out[...].astype(F32)
    in_ref[...] = grad_in.astype(in_ref.dtype)
    out_ref[...] = grad_out.astype(out_ref.dtype)


def body(
    feed, segments, routes, rel_bucket, gain_attn, gain_ffn, w_query, w_key, w_value, w_out_attn,
    rel_table, router, expert_in, expert_out,
):
    seq = feed.shape[2]
    width = feed.shape[3]
    experts = lax.axis_size("expert")
    shards = lax.axis_size("shard")
    cap = max(2, 2 * seq // experts)
    own_rows = w_query.shape[1]
    table_rows = rel_table.shape[1]
    quick = direct("expert") and direct("shard")
    blocks_count = experts if quick else 1
    wide = 2 * width + EXT
    side_rows = -(-(LEAD + experts) // 16) * 16
    sec = lax.axis_index("section")
    first = sec == 0
    place = jnp.concatenate(
        [
            jnp.stack([sec, lax.axis_index("expert")]).astype(jnp.int32),
            peer_ids("expert"),
            peer_ids("shard"),
        ]
    )
    spots = np.arange(width)
    flat = spots // own_rows * table_rows + spots % own_rows
    real = spots % own_rows < table_rows
    bucket_of = jnp.asarray(np.where(real, flat // HEADS, -1)[:, None].astype(np.int32))
    head_sel = jnp.asarray(
        (real[None, :] & (flat % HEADS == np.arange(16)[:, None])).astype(np.float32)
    ).astype(BF)
    spare = jnp.full((1,), -2, jnp.int32)
    bucket = jnp.concatenate([rel_bucket, spare])[None, :]
    bucket_back = jnp.concatenate([rel_bucket[::-1], spare])[None, :]

    ext = jnp.concatenate(
        [
            gain_attn[0][:, None],
            gain_ffn[0][:, None],
            jnp.pad(rel_table[0], (0, own_rows - table_rows))[:, None],
            router[0],
            jnp.zeros((own_rows, EXT - LEAD - experts), BF),
        ],
        axis=1,
    )
    half_a = jnp.concatenate([w_query[0], w_key[0], ext], axis=1)
    half_b = jnp.concatenate([w_value[0], w_out_attn[0], ext], axis=1)
    came = swap(jnp.where(first, half_b, half_a))
    parts = [jnp.where(first, half_a, came), jnp.where(first, came, half_b)]

    def gather(part):
        if not quick:
            mine = [lax.all_gather(part, ("expert", "shard"), axis=0, tiled=True)]
        else:
            plane = pl.pallas_call(
                functools.partial(join_rows, shards, 2 + experts),
                out_shape=out((shards * own_rows, wide)),
                in_specs=[SM] + [HB] * shards,
                out_specs=HB,
                scratch_shapes=[pltpu.SemaphoreType.DMA((shards,))],
            )(place, *spread(part, "shard"))
            mine = spread(plane, "expert")
        return mine + [swap(piece) for piece in mine]

    weights = [gather(parts[0]), None]

    came = swap(jnp.where(first, feed[0, 1], feed[0, 0]))
    layer_x = jnp.where(first, feed[0, 0], came)
    layer_dy = jnp.where(first, came, feed[0, 1])
    came = swap(jnp.where(first, routes[0, 1, 0], routes[0, 0, 0]))
    kept = jnp.where(first, routes[0, 0, 0], routes[0, 1, 0])
    my_routes = jnp.stack([jnp.where(first, kept, came), jnp.where(first, came, kept)])
    seg_ids = jnp.where(first, segments[0, 0], segments[1, 0])
    own_experts = [expert_in[0, 0], expert_out[0, 0]]
    came_experts = [swap(expert_in[0, 0]), swap(expert_out[0, 0])]

    all_routes = jnp.stack(spread(my_routes, "shard"), axis=1)
    hot = (all_routes[..., None] == peer_ids("expert")).astype(BF)
    positions = jnp.arange(seq, dtype=jnp.int32)
    before = (positions[:, None] > positions[None, :]).astype(BF)
    rank = jnp.einsum("ij,lzje->lzie", before, hot, preferred_element_type=F32)
    slot_in = jnp.arange(cap, dtype=jnp.int32).astype(F32)
    back_hot = (hot[..., None] * (rank[..., None] == slot_in).astype(BF)).reshape(
        2, shards, seq, experts * cap
    )
    to_hot = jnp.swapaxes(back_hot, 2, 3)
    route_cols = my_routes[:, :, None]
    seg_col, seg_row = seg_ids[:, None], seg_ids[None, :]

    row = out((seq, width))
    block = out((shards * cap * experts // blocks_count, width))
    sems = pltpu.SemaphoreType.DMA
    weight_count = experts if quick else 1
    weight_scratch = [pltpu.VMEM((2, width, wide), BF), sems((2 * weight_count,))]
    expert_scratch = [pltpu.VMEM((2, expert_in.shape[2], expert_in.shape[3]), BF), sems((2,))]
    expert_specs = [SM] + [HB] * 4

    def to_experts(layer, tokens):
        every = spread(tokens, "shard")
        if not quick:
            slots = jnp.einsum(
                "zcs,zsd->czd", to_hot[layer], jnp.stack(every), preferred_element_type=F32
            )
            slots = slots.astype(BF).reshape(experts, cap * shards, width)
            moved = exchange([slots[i] for i in range(experts)], "expert")
            return [jnp.concatenate(moved, axis=0)]
        blocks = call(
            functools.partial(dispatch_rows, experts, shards, cap),
            [block] * experts,
            [to_hot[layer], *every],
            [VM] * (1 + shards),
        )
        return exchange(blocks, "expert")

    def to_tokens(layer, blocks):
        if not quick:
            rows = blocks[0].reshape(experts, cap * shards, width)
            back = jnp.stack(exchange([rows[i] for i in range(experts)], "expert"))
            back = back.reshape(experts * cap, shards, width)
            tokens = jnp.einsum(
                "zsc,czd->zsd", back_hot[layer], back, preferred_element_type=F32
            ).astype(BF)
            return exchange([tokens[i] for i in range(shards)], "shard")
        back = exchange(blocks, "expert")
        tokens = call(
            functools.partial(combine_rows, experts, shards, cap),
            [row] * shards,
            [back_hot[layer], *back],
            [VM] * (1 + experts),
        )
        return exchange(tokens, "shard")

    def attention(layer, ins, in_specs):
        state_outs = [
            row,
            out((seq, 5 * width)),
            out((HEADS // 2, 2 * seq, seq), F32),
            out((seq, width), F32),
            out((seq, EXT), F32),
            out((seq, EXT), F32),
            out((width, EXT)),
        ]
        return call(
            functools.partial(attn_forward, layer, seq, width, experts, weight_count),
            ([row, row] if layer else []) + state_outs,
            [
                place, route_cols[layer], seg_col, seg_row, bucket, bucket_of, head_sel,
                *weights[layer], *ins,
            ],
            [SM] + [VM] * 6 + [HB] * (2 * weight_count) + in_specs,
            weight_scratch + [pltpu.VMEM((seq, 3 * width), BF)],
        )

    def attention_back(layer, dy, x, state, tok, parts):
        n2, acts, probs, hidden, gates, gv, _ = state
        return call(
            functools.partial(attn_backward, layer, seq, width, experts, weight_count, shards),
            [
                row,
                out((seq, 4 * width)),
                out((seq, 4 * width)),
                out((side_rows, width), F32),
            ],
            [
                place, route_cols[layer], bucket_back, bucket_of, head_sel, *weights[layer],
                dy, x, acts, probs, hidden, n2, gates, gv, tok, *parts,
            ],
            [SM] + [VM] * 4 + [HB] * (2 * weight_count) + [VM] * (9 + shards),
            weight_scratch + [pltpu.VMEM((seq, 3 * width), BF), pltpu.VMEM((16, 2 * seq), F32)],
        )

    def back_expert(layer, rows, dys, ext_side, with_out):
        results = call(
            functools.partial(expert_backward, layer, blocks_count, experts, with_out),
            [block] * (blocks_count * (2 if with_out else 1))
            + [out((4, shards * cap * experts, width))],
            [place, *own_experts, *came_experts, ext_side, *rows, *dys],
            expert_specs + [VM] * (1 + 2 * blocks_count),
            expert_scratch,
        )
        return results[:blocks_count], results[blocks_count:-1], results[-1]

    def reduce_weights(ship, stay, side):
        came = swap(ship)
        side_came = swap(side)
        blocks = call(
            functools.partial(attn_weights, width, weight_count),
            [out((width // weight_count, wide))] * weight_count,
            [place, stay, came, side, side_came],
            [SM] + [VM] * 4,
            [pltpu.VMEM((width, wide), BF)],
        )
        if not quick:
            return scatter_rows(blocks[0])
        blocks = call(
            functools.partial(sum_blocks, experts, 2 + experts),
            [out((own_rows, wide))] * shards,
            [place, *exchange(blocks, "expert")],
            [SM] + [VM] * experts,
            [pltpu.VMEM((shards * own_rows, wide), F32)],
        )
        (total,) = call(
            functools.partial(sum_blocks, shards, 0),
            [out((own_rows, wide), F32)],
            [place, *exchange(blocks, "shard")],
            [SM] + [VM] * shards,
            [pltpu.VMEM((own_rows, wide), F32)],
        )
        return total

    state_zero = attention(0, [layer_x], [VM])
    rows_zero = to_experts(0, state_zero[0])
    weights[1] = gather(parts[1])
    dys_one = to_experts(1, layer_dy)
    results = call(
        functools.partial(expert_forward, 0, blocks_count),
        [block] * blocks_count,
        [place, *own_experts, *came_experts, *rows_zero],
        expert_specs + [VM] * blocks_count,
        expert_scratch,
    )
    toks = to_tokens(0, results)
    results = attention(1, [state_zero[3], state_zero[5], *toks], [VM] * (2 + shards))
    (out_zero, tok_zero), state_one = results[:2], results[2:]
    rows_one = to_experts(1, state_one[0])
    grads, results, keep_one = back_expert(1, rows_one, dys_one, state_one[6], True)
    parts_one = to_tokens(1, grads)
    dx_one, ship_one, stay_one, side_one = attention_back(
        1, layer_dy, out_zero, state_one, out_zero, parts_one
    )
    dys_zero = to_experts(0, dx_one)
    toks_one = to_tokens(1, results)
    grads, _, keep_zero = back_expert(0, rows_zero, dys_zero, state_zero[6], False)
    out_one, side_one = call(
        functools.partial(last_output, experts, shards),
        [row, out((side_rows, width), F32)],
        [
            route_cols[1], layer_dy, state_one[3], state_one[0], state_one[4], state_one[5],
            side_one, *toks_one,
        ],
        [VM] * (7 + shards),
    )
    sum_one = reduce_weights(ship_one, stay_one, side_one)
    matrix = (expert_in.shape[2], expert_in.shape[3])
    keep_scratch = [pltpu.VMEM(keep_one.shape, BF), sems(())]
    sent = call(
        functools.partial(expert_weights, True),
        [out(matrix)] * 2,
        [place, keep_zero, keep_one],
        [SM, HB, HB],
        keep_scratch,
    )
    came_grads = [swap(grad) for grad in sent]
    parts_zero = to_tokens(0, grads)
    dx_zero, ship_zero, stay_zero, side_zero = attention_back(
        0, dx_one, layer_x, state_zero, tok_zero, parts_zero
    )
    sum_zero = reduce_weights(ship_zero, stay_zero, side_zero)
    own_grads = call(
        functools.partial(expert_weights, False),
        [out(matrix, F32)] * 2,
        [place, keep_zero, keep_one, *came_grads],
        [SM, HB, HB, VM, VM],
        keep_scratch,
    )

    came = swap(jnp.where(first, sum_one, sum_zero))
    kept = jnp.where(first, sum_zero, sum_one)
    final_a = jnp.where(first, kept, came)
    final_b = jnp.where(first, came, kept)

    def by_batch(zero, one):
        came = swap(jnp.where(first, one, zero))
        kept = jnp.where(first, zero, one)
        return jnp.stack([jnp.where(first, kept, came), jnp.where(first, came, kept)])

    side = final_a[:, 2 * width :]
    return (
        by_batch(out_zero, out_one)[None],
        by_batch(dx_zero, dx_one)[None],
        side[:, 0][None],
        side[:, 1][None],
        final_a[:, :width][None],
        final_a[:, width : 2 * width][None],
        final_b[:, :width][None],
        final_b[:, width : 2 * width][None],
        side[:table_rows, 2][None],
        side[:, LEAD : LEAD + experts][None],
        own_grads[0][None, None],
        own_grads[1][None, None],
    )


def solution(mesh):
    rows = ("expert", "shard")
    tokens = P("section", None, rows, None)
    matrix = P("section", rows, None)
    vector = P("section", rows)
    expert_specs = (P("section", "expert", None, "shard"), P("section", "expert", "shard", None))
    in_specs = (
        tokens, P(None, rows, None), tokens, P(), vector, vector, matrix, matrix, matrix, matrix,
        vector, matrix, *expert_specs,
    )
    out_specs = (
        tokens, tokens, vector, vector, matrix, matrix, matrix, matrix, vector, matrix,
        *expert_specs,
    )
    return jax.shard_map(body, mesh=mesh, in_specs=in_specs, out_specs=out_specs, check_vma=False)
```

```python
import functools
import math

import jax
import jax.numpy as jnp
import numpy as np
from jax import lax
from jax.experimental import pallas as pl
from jax.experimental.pallas import tpu as pltpu
from jax.sharding import PartitionSpec as P

HEADS = 12
HEAD_DIM = 64
NB = 32
EXT = 128
LEAD = 3
EPSILON = 1e-06
MASK_FILL = -1e30
BF = jnp.bfloat16
F32 = jnp.float32
VM = pl.BlockSpec()
SM = pl.BlockSpec(memory_space=pltpu.SMEM)
HB = pl.BlockSpec(memory_space=pltpu.HBM)
AN = pl.BlockSpec(memory_space=pl.ANY)


def dot(a, b):
    return jnp.dot(a, b, preferred_element_type=F32)


def dot_t(a, b):
    return lax.dot_general(a, b, (((1,), (1,)), ((), ())), preferred_element_type=F32)


def t_dot(a, b):
    return lax.dot_general(a, b, (((0,), (0,)), ((), ())), preferred_element_type=F32)


def swap(value):
    return lax.ppermute(value, "section", [(0, 1), (1, 0)])


def direct(axis):
    count = lax.axis_size(axis)
    return count <= 4 and count & (count - 1) == 0


def peer_ids(axis):
    count = lax.axis_size(axis)
    ids = jnp.arange(count, dtype=jnp.int32)
    return ids ^ lax.axis_index(axis) if direct(axis) else ids


def hop(value, axis, step):
    count = lax.axis_size(axis)
    return lax.ppermute(value, axis, [(i, i ^ step) for i in range(count)])


def spread(value, axis):
    count = lax.axis_size(axis)
    if direct(axis):
        return [value] + [hop(value, axis, step) for step in range(1, count)]
    every = lax.all_gather(value, axis, axis=0)
    return [every[i] for i in range(count)]


def exchange(blocks, axis):
    count = lax.axis_size(axis)
    if direct(axis):
        return [blocks[0]] + [hop(blocks[step], axis, step) for step in range(1, count)]
    swapped = lax.all_to_all(jnp.stack(blocks), axis, 0, 0, tiled=True)
    return [swapped[i] for i in range(count)]


def scatter_rows(whole):
    for axis in ("expert", "shard"):
        count = lax.axis_size(axis)
        rows = whole.shape[0] // count
        ids = peer_ids(axis)
        blocks = [
            lax.dynamic_slice_in_dim(whole, ids[i] * rows, rows, axis=0).astype(BF)
            for i in range(count)
        ]
        whole = sum(block.astype(F32) for block in exchange(blocks, axis))
    return whole


def call(kernel, outs, ins, specs, scratch=(), flops=0, out_specs=None, after=()):
    count = len(ins)
    moved = sum(math.prod(a.shape) * a.dtype.itemsize for a in (*ins, *outs))

    def run(*refs):
        kernel(*refs[:count], *refs[count + len(after) :])

    return pl.pallas_call(
        run,
        out_shape=list(outs),
        in_specs=list(specs) + [AN] * len(after),
        out_specs=list(out_specs or [VM] * len(outs)),
        scratch_shapes=list(scratch),
        compiler_params=pltpu.CompilerParams(vmem_limit_bytes=28 * 1024 * 1024),
        cost_estimate=pl.CostEstimate(flops=flops, bytes_accessed=moved, transcendentals=0),
    )(*ins, *after)


def out(shape, kind=BF):
    return jax.ShapeDtypeStruct(shape, kind)


def begin(copies):
    for copy in copies:
        copy.start()
    return copies


def finish(copies):
    for copy in copies:
        copy.wait()


def join_weights(place, pieces, held, layout, shards):
    peers = len(pieces) // (2 * len(layout))
    for part in range(2):
        target = place[0] if part == 0 else 1 - place[0]
        for i, (zs, column) in enumerate(layout):
            for e in range(peers):
                piece = pieces[(part * len(layout) + i) * peers + e]
                rows = piece.shape[0] // len(zs)
                for at, z in enumerate(zs):
                    first = (place[2 + e] * shards + place[2 + peers + z]) * rows
                    held[
                        target,
                        pl.ds(pl.multiple_of(first, rows), rows),
                        column : column + piece.shape[1],
                    ] = piece[at * rows : (at + 1) * rows, :]


def as_column(row, turned=None):
    n = row.shape[1]
    across = lax.broadcasted_iota(jnp.int32, (n, n), 1)
    down = lax.broadcasted_iota(jnp.int32, (n, n), 0)
    if turned is not None:
        down = turned - down
    return jnp.sum(jnp.where(across == down, row, jnp.zeros_like(row)), axis=1, keepdims=True)


def table_places(width, own_rows, table_rows):
    spot = lax.broadcasted_iota(jnp.int32, (16, width), 1).astype(F32)
    owner = jnp.floor((spot + 0.5) * (1.0 / own_rows))
    rest = spot - owner * own_rows
    flat = owner * table_rows + rest
    bucket = jnp.floor((flat + 0.5) * (1.0 / HEADS))
    head = flat - bucket * HEADS
    real = rest < table_rows
    row = lax.broadcasted_iota(jnp.int32, (16, width), 0).astype(F32)
    return jnp.where(real, bucket, -1.0)[0:1], (real & (head == row)).astype(F32)


def inverse_rms(value):
    return lax.rsqrt(jnp.mean(value * value, axis=-1, keepdims=True) + EPSILON)


def norm_back(value, gain, grad):
    scale = inverse_rms(value)
    scaled = value * scale
    gained = grad * gain
    back = scale * (gained - scaled * jnp.mean(gained * scaled, axis=-1, keepdims=True))
    return back, jnp.sum(grad * scaled, axis=0, keepdims=True)


def gain_rows(side):
    pick = (
        lax.broadcasted_iota(jnp.int32, (16, EXT), 0)
        == lax.broadcasted_iota(jnp.int32, (16, EXT), 1)
    ).astype(BF)
    rows = dot_t(pick, side)
    return rows[0:1], rows[1:2], rows[2:3]


def gelu_parts(value):
    c = math.sqrt(2.0 / math.pi)
    square = value * value
    inner = jnp.tanh(c * (value + 0.044715 * square * value))
    grad = 0.5 * (1.0 + inner) + 0.5 * value * (1.0 - inner * inner) * (
        c + (3.0 * 0.044715 * c) * square
    )
    return 0.5 * value * (1.0 + inner), grad


def softmax_lanes(logits, experts):
    lane = lax.broadcasted_iota(jnp.int32, logits.shape, 1)
    valid = (lane >= LEAD) & (lane < LEAD + experts)
    logits = jnp.where(valid, logits, MASK_FILL)
    power = jnp.exp(logits - jnp.max(logits, axis=-1, keepdims=True))
    power = jnp.where(valid, power, 0.0)
    return power / jnp.sum(power, axis=-1, keepdims=True), lane


def pair_rows(value):
    low_lanes = lax.broadcasted_iota(jnp.int32, value.shape, 1) < HEAD_DIM
    zero = jnp.zeros_like(value)
    return jnp.concatenate(
        [jnp.where(low_lanes, value, zero), jnp.where(low_lanes, zero, value)], axis=0
    )


def pair_lanes(value):
    half = value.shape[0] // 2
    low_lanes = lax.broadcasted_iota(jnp.int32, (half, value.shape[1]), 1) < HEAD_DIM
    return jnp.where(low_lanes, value[:half], value[half:])


def attn_forward(layer, seq, width, experts, layout, count, shards, own_rows, table_rows, *refs):
    place, info = refs[:2]
    refs = refs[2:]
    pieces, refs = refs[:count], refs[count:]
    if layer == 0:
        (x_ref,), refs = refs[:1], refs[1:]
        n2_ref, refs = refs[0], refs[1:]
        extra = []
    else:
        (hid_ref,), toks, refs = refs[:1], refs[1:-16], refs[-16:]
        out_ref, n2_ref, tok_out = refs[:3]
        refs = refs[3:]
    acts_out, probs_out, floats_out, ext_out, held_out = refs[:5]
    held, sem, acts, probs_keep, floats, ext_keep, low_keep, out_sems = refs[5:]
    if layer == 0:
        low = x_ref[...]
    else:
        coming = pltpu.make_async_copy(hid_ref, floats, out_sems.at[0])
        coming.start()
        tok = sum(t[...].astype(F32) for t in toks).astype(BF)
        low_keep[...] = tok
        coming.wait()
        gate = floats[:, width + EXT : width + EXT + 1]
        low = (floats[:, :width] + gate * tok.astype(F32)).astype(BF)
        out_ref[...] = low
        extra = begin([pltpu.make_async_copy(low_keep, tok_out, out_sems.at[0])])
    acts[:, 6 * width :] = low
    x = low.astype(F32)
    scaled = x * inverse_rms(x)
    seg_row = info[0:1, :seq]
    same = as_column(seg_row) == seg_row
    route = as_column(info[1 + layer : 2 + layer, :seq])
    bucket = as_column(info[3:4, :]).astype(F32)
    bucket_row, head_sel = table_places(width, own_rows, table_rows)
    buckets = (bucket == bucket_row).astype(BF)
    if layout:
        join_weights(place, pieces, held, layout, shards)
    else:
        held[place[0]] = pieces[0][...]
        held[1 - place[0]] = pieces[1][...]
    extra = extra + begin([pltpu.make_async_copy(held, held_out, sem)])
    side = held[0, :, 2 * width : 2 * width + EXT]
    ext_keep[...] = side
    extra = extra + begin([pltpu.make_async_copy(ext_keep, ext_out, out_sems.at[1])])
    gain_one, gain_two, table_row = gain_rows(side)
    table = dot_t((head_sel * table_row).astype(BF), buckets)
    normed = (scaled * gain_one).astype(BF)
    acts[:, :width] = normed
    acts[:, width : 3 * width] = dot(normed, held[0, :, : 2 * width]).astype(BF)
    acts[:, 3 * width : 4 * width] = dot(normed, held[1, :, :width]).astype(BF)
    scale = 1.0 / math.sqrt(HEAD_DIM)
    contexts = []
    for p in range(HEADS // 2):
        at = [(1 + i) * width + 128 * p for i in range(3)]
        q2 = pair_rows(acts[:, at[0] : at[0] + 128])
        scores = dot_t(q2, acts[:, at[1] : at[1] + 128]) * scale
        parts = []
        for h in (2 * p, 2 * p + 1):
            line = jnp.broadcast_to(table[h : h + 1], (seq, 2 * seq))
            bias = pltpu.roll(line, seq + 1, axis=1, stride=1, stride_axis=0)[:, :seq]
            part = scores[seq * (h - 2 * p) : seq * (h - 2 * p) + seq] + bias
            parts.append(jnp.where(same, part, MASK_FILL))
        scores = jnp.concatenate(parts, axis=0)
        power = jnp.exp(scores - jnp.max(scores, axis=-1, keepdims=True))
        probs = power / jnp.sum(power, axis=-1, keepdims=True)
        probs_keep[p] = probs
        contexts.append(pair_lanes(dot(probs.astype(BF), acts[:, at[2] : at[2] + 128])))
    extra = extra + begin([pltpu.make_async_copy(probs_keep, probs_out, out_sems.at[2])])
    context = jnp.concatenate(contexts, axis=1).astype(BF)
    acts[:, 4 * width : 5 * width] = context
    hidden = x + dot(context, held[1, :, width : 2 * width])
    floats[:, :width] = hidden
    normed_two = (hidden * inverse_rms(hidden) * gain_two).astype(BF)
    n2_ref[...] = normed_two
    acts[:, 5 * width : 6 * width] = normed_two
    extra = extra + begin([pltpu.make_async_copy(acts, acts_out, out_sems.at[3])])
    gates, lane = softmax_lanes(dot(normed_two, side), experts)
    floats[:, width : width + EXT] = gates
    value = jnp.sum(jnp.where(lane == route + LEAD, gates, 0.0), axis=-1, keepdims=True)
    floats[:, width + EXT :] = jnp.broadcast_to(value, gates.shape)
    finish(extra + begin([pltpu.make_async_copy(floats, floats_out, out_sems.at[4])]))


def pick_inputs(seq, *refs):
    place, own_feed, came_feed, segments, own_routes, came_routes, buckets = refs[:7]
    x_ref, dy_ref, info, sems = refs[7:]
    sec = place[0]
    for core in range(2):

        @pl.when(sec == core)
        def _(core=core):
            sources = (own_feed, came_feed) if core == 0 else (came_feed, own_feed)
            finish(
                begin(
                    [
                        pltpu.make_async_copy(sources[0].at[core], x_ref, sems.at[0]),
                        pltpu.make_async_copy(sources[1].at[core], dy_ref, sems.at[1]),
                    ]
                )
            )
            info[...] = jnp.full(info.shape, -2, jnp.int32)
            info[0:1, :seq] = segments[core : core + 1, :]
            info[1 + core : 2 + core, :seq] = own_routes[core : core + 1, :]
            info[2 - core : 3 - core, :seq] = came_routes[core : core + 1, :]
            info[3:4, : 2 * seq - 1] = buckets[...]


def routing_slots(shards, seq, experts, cap, *refs):
    place, infos, slots = refs[0], refs[1 : 1 + shards], refs[1 + shards]
    before = (
        lax.broadcasted_iota(jnp.int32, (seq, seq), 0)
        < lax.broadcasted_iota(jnp.int32, (seq, seq), 1)
    ).astype(BF)
    routes = jnp.concatenate(
        [info[1 + layer : 2 + layer, :seq] for layer in range(2) for info in infos], axis=0
    )
    rank = jnp.zeros(routes.shape, F32)
    for e in range(experts):
        mine = (routes == e).astype(F32)
        rank = rank + mine * dot(mine.astype(BF), before)
    slots[...] = (routes ^ place[1]) * cap + rank.astype(jnp.int32)


def slot_hot(slots, layer, shards, z, total):
    row = slots[layer * shards + z : layer * shards + z + 1, :]
    return (lax.broadcasted_iota(jnp.int32, (total, row.shape[1]), 0) == row).astype(BF)


def dispatch_rows(layer, count, shards, cap, *refs):
    slots = refs[0]
    toks = refs[1 : 1 + shards]
    blocks = refs[1 + shards :]
    for z in range(shards):
        rows = dot(slot_hot(slots, layer, shards, z, count * cap), toks[z][...]).astype(BF)
        for i in range(count):
            blocks[i][z * cap : (z + 1) * cap, :] = rows[i * cap : (i + 1) * cap]


def combine_rows(layer, count, shards, cap, *refs):
    slots = refs[0]
    blocks, refs = refs[1 : 1 + count], refs[1 + count :]
    more = (len(refs) - shards) // 2
    handed, toks, given = refs[:more], refs[more : more + shards], refs[more + shards :]
    for z in range(shards):
        rows = jnp.concatenate([b[z * cap : (z + 1) * cap, :] for b in blocks], axis=0)
        toks[z][...] = t_dot(slot_hot(slots, layer, shards, z, count * cap), rows).astype(BF)
    for source, target in zip(handed, given):
        target[...] = source[...]


def start_expert(layer, place, own, came, held, sems):
    def begin(pair):
        for i in range(2):
            pltpu.make_async_copy(pair[i], held.at[i], sems.at[i]).start()

    @pl.when(place[0] == layer)
    def _():
        begin(own)

    @pl.when(place[0] != layer)
    def _():
        begin(came)

    return [pltpu.make_async_copy(own[i], held.at[i], sems.at[i]) for i in range(2)]


def expert_forward(layer, count, *refs):
    place, own, came = refs[0], refs[1:3], refs[3:5]
    blocks = refs[5 : 5 + count]
    results, rows_out = refs[5 + count : 5 + 2 * count], refs[5 + 2 * count]
    held, sems, rows, out_sem = refs[6 + 2 * count :]
    copies = start_expert(layer, place, own, came, held, sems)
    each = blocks[0].shape[0]
    for i in range(count):
        rows[i * each : (i + 1) * each, :] = blocks[i][...]
    leaving = begin([pltpu.make_async_copy(rows, rows_out, out_sem)])
    finish(copies)
    for i in range(count):
        activated = gelu_parts(dot(blocks[i][...], held[0]))[0].astype(BF)
        results[i][...] = dot(activated, held[1]).astype(BF)
    finish(leaving)


def expert_backward(layer, count, experts, with_out, *refs):
    place, own, came, ext_in = refs[0], refs[1:3], refs[3:5], refs[5]
    if with_out:
        blocks, dy_in, refs = refs[6 : 6 + count], refs[6 + count : 6 + 2 * count], refs[6 + 2 * count :]
    else:
        rows_in, dys, refs = refs[6], refs[7 : 7 + count], refs[7 + count :]
    grads, refs = refs[:count], refs[count:]
    if with_out:
        results, refs = refs[:count], refs[count:]
    keep_out, held, sems, keep, ext, late, more_sems = refs
    copies = start_expert(layer, place, own, came, held, sems)
    each = grads[0].shape[0]
    loads = [pltpu.make_async_copy(ext_in, ext, more_sems.at[0])]
    if with_out:
        loads += [
            pltpu.make_async_copy(dy_in[i], late.at[pl.ds(i * each, each), :], more_sems.at[1 + i])
            for i in range(count)
        ]
    else:
        loads += [pltpu.make_async_copy(rows_in, late, more_sems.at[1])]
    begin(loads)
    finish(loads + copies)
    leaving = []
    for i in range(count):
        at = slice(i * each, (i + 1) * each)
        if with_out:
            rows, dy = blocks[i][...], late[at, :]
        else:
            rows, dy = late[at, :], dys[i][...]
        dy = dy.astype(F32)
        gates, lane = softmax_lanes(dot(rows, ext[...]), experts)
        mine = (lane == place[1] + LEAD).astype(F32)
        value = jnp.sum(gates * mine, axis=-1, keepdims=True)
        grad_expert = (value * dy).astype(BF)
        act, slope = gelu_parts(dot(rows, held[0]))
        act = act.astype(BF)
        grad_pre = (dot_t(grad_expert, held[1]) * slope).astype(BF)
        grad = dot_t(grad_pre, held[0])
        if with_out:
            result = dot(act, held[1])
            results[i][...] = result.astype(BF)
            grad_gate = jnp.sum(dy * result, axis=-1, keepdims=True)
            grad_logits = (grad_gate * value * (mine - gates)).astype(BF)
            grad = grad + dot_t(grad_logits, ext[...])
        grads[i][...] = grad.astype(BF)
        keep[0, at, :] = rows
        keep[1, at, :] = grad_pre
        keep[2, at, :] = act
        keep[3, at, :] = grad_expert
        leaving += begin(
            [
                pltpu.make_async_copy(
                    keep.at[:, pl.ds(i * each, each), :],
                    keep_out.at[:, pl.ds(i * each, each), :],
                    more_sems.at[1 + count + i],
                )
            ]
        )
    finish(leaving)


def attn_backward(layer, seq, width, experts, shards, own_rows, table_rows, *refs):
    place, info, held_in = refs[:3]
    refs = refs[3:]
    dy_ref, acts_in, probs_in, floats_in = refs[:4]
    refs = refs[4:]
    if layer == 0:
        tok_in, refs = refs[0], refs[1:]
    parts, refs = refs[:shards], refs[shards:]
    dx_ref, ship, stay, side_grad = refs[:4]
    held, sem, acts, probs_all, floats, tok_keep, gj, g_rel, in_sems = refs[4:]
    loads = [
        pltpu.make_async_copy(floats_in, floats, in_sems.at[0]),
        pltpu.make_async_copy(acts_in, acts, in_sems.at[1]),
        pltpu.make_async_copy(probs_in, probs_all, in_sems.at[2]),
    ]
    if layer == 0:
        loads.append(pltpu.make_async_copy(tok_in, tok_keep, in_sems.at[3]))
    begin(loads)
    copies = begin([pltpu.make_async_copy(held_in, held, sem)])
    dy = dy_ref[...].astype(F32)
    grad_norm_two = sum(p[...].astype(F32) for p in parts)
    route = as_column(info[1 + layer : 2 + layer, :seq])
    bucket = as_column(info[3:4, :], 2 * seq - 2).astype(F32)
    bucket_row, head_sel = table_places(width, own_rows, table_rows)
    buckets = (bucket == bucket_row).astype(BF)
    finish(loads)
    hidden = floats[:, :width]
    x = acts[:, 6 * width :].astype(F32)
    state = acts
    finish(copies)
    side = held[0, :, 2 * width : 2 * width + EXT]
    gain_one, gain_two, _ = gain_rows(side)
    side_grad[...] = jnp.zeros_like(side_grad)
    if layer == 0:
        gates = floats[:, width : width + EXT]
        lane = lax.broadcasted_iota(jnp.int32, gates.shape, 1)
        hot = (lane == route + LEAD).astype(F32)
        grad_gate = jnp.sum(dy * tok_keep[...].astype(F32), axis=-1, keepdims=True)
        value = floats[:, width + EXT : width + EXT + 1]
        grad_logits = (grad_gate * value * (hot - gates)).astype(BF)
        grad_norm_two = grad_norm_two + dot_t(grad_logits, side)
        router_rows = t_dot(grad_logits, acts[:, 5 * width : 6 * width])
        side_grad[...] = router_rows[: side_grad.shape[0]]
    back, gain_two_grad = norm_back(hidden, gain_two, grad_norm_two)
    grad_hidden = dy + back
    grad_hidden_low = grad_hidden.astype(BF)
    grad_context = dot_t(grad_hidden_low, held[1, :, width : 2 * width]).astype(BF)
    scale = 1.0 / math.sqrt(HEAD_DIM)
    mirror = (
        lax.broadcasted_iota(jnp.int32, (seq, 2 * seq), 0)
        + lax.broadcasted_iota(jnp.int32, (seq, 2 * seq), 1)
        == seq - 1
    ).astype(BF)
    for p in range(HEADS // 2):
        lanes = slice(128 * p, 128 * p + 128)
        q2 = pair_rows(state[:, width + 128 * p : width + 128 * p + 128])
        keys = state[:, 2 * width + 128 * p : 2 * width + 128 * p + 128]
        vals = state[:, 3 * width + 128 * p : 3 * width + 128 * p + 128]
        g2 = pair_rows(grad_context[:, lanes])
        probs = probs_all[p]
        grad_probs = dot_t(g2, vals)
        grad_scores = probs * (
            grad_probs - jnp.sum(probs * grad_probs, axis=-1, keepdims=True)
        )
        grad_scores = grad_scores.astype(BF)
        gj[:, lanes] = (pair_lanes(dot(grad_scores, keys)) * scale).astype(BF)
        gj[:, width + 128 * p : width + 128 * p + 128] = (t_dot(grad_scores, q2) * scale).astype(BF)
        gj[:, 2 * width + 128 * p : 2 * width + 128 * p + 128] = t_dot(
            probs.astype(BF), g2
        ).astype(BF)
        turned = dot(grad_scores, mirror)
        for h in range(2):
            shifted = pltpu.roll(turned[h * seq : (h + 1) * seq], 0, axis=1, stride=1, stride_axis=0)
            g_rel[2 * p + h : 2 * p + h + 1, :] = jnp.sum(shifted, axis=0, keepdims=True)
    g_rel[HEADS:, :] = jnp.zeros_like(g_rel[HEADS:, :])
    offsets = g_rel[...]
    high = offsets.astype(BF)
    low = (offsets - high.astype(F32)).astype(BF)
    by_row = dot(high, buckets) + dot(low, buckets)
    side_grad[2:3, :] = jnp.sum(by_row * head_sel, axis=0, keepdims=True)
    side_grad[1:2, :] = gain_two_grad
    grad_normed = dot_t(gj[:, : 2 * width], held[0, :, : 2 * width]) + dot_t(
        gj[:, 2 * width :], held[1, :, :width]
    )
    back, gain_one_grad = norm_back(x, gain_one, grad_normed)
    side_grad[0:1, :] = gain_one_grad
    dx_ref[...] = (grad_hidden + back).astype(BF)
    normed = state[:, :width]
    halves = (ship, stay)
    for core in range(2):

        @pl.when(place[0] == core)
        def _(core=core):
            halves[1 - core][:, :width] = normed
            halves[1 - core][:, width : 3 * width] = gj[:, : 2 * width]
            halves[1 - core][:, 3 * width :] = jnp.zeros_like(normed)
            halves[core][:, :width] = normed
            halves[core][:, width : 2 * width] = gj[:, 2 * width :]
            halves[core][:, 2 * width : 3 * width] = state[:, 4 * width : 5 * width]
            halves[core][:, 3 * width :] = grad_hidden_low


def last_output(seq, width, experts, shards, *refs):
    info, dy_ref, acts_in, floats_in, side_in = refs[:5]
    parts, refs = refs[5 : 5 + shards], refs[5 + shards :]
    out_ref, side_grad, normed, floats, sems = refs
    loads = begin(
        [
            pltpu.make_async_copy(floats_in, floats, sems.at[0]),
            pltpu.make_async_copy(acts_in.at[:, pl.ds(5 * width, width)], normed, sems.at[1]),
        ]
    )
    tok = sum(p[...].astype(F32) for p in parts).astype(BF).astype(F32)
    finish(loads)
    value = floats[:, width + EXT : width + EXT + 1]
    out_ref[...] = (floats[:, :width] + value * tok).astype(BF)
    gates = floats[:, width : width + EXT]
    lane = lax.broadcasted_iota(jnp.int32, gates.shape, 1)
    hot = (lane == as_column(info[2:3, :seq]) + LEAD).astype(F32)
    grad_gate = jnp.sum(dy_ref[...].astype(F32) * tok, axis=-1, keepdims=True)
    grad_logits = (grad_gate * value * (hot - gates)).astype(BF)
    side_grad[...] = side_in[...] + t_dot(grad_logits, normed[...])[: side_grad.shape[0]]


def attn_weights(width, count, parts, *refs):
    place, stay, came = refs[:3]
    total = refs[-1]
    blocks = refs[-1 - count : -1]
    sides = refs[3 : -1 - count]

    def both(first, last):
        return jnp.concatenate([stay[:, first:last], came[:, first:last]], axis=0)

    for i, part in enumerate(parts):
        at = slice(i * width, (i + 1) * width)

        @pl.when(place[0] == 0)
        def _(part=part, at=at):
            total[:, at] = t_dot(
                both(0, width), both((1 + part) * width, (2 + part) * width)
            ).astype(BF)

        @pl.when(place[0] != 0)
        def _(part=part, at=at):
            total[:, at] = t_dot(
                both(2 * part * width, (2 * part + 1) * width),
                both((2 * part + 1) * width, (2 * part + 2) * width),
            ).astype(BF)

    if sides:
        block = jnp.zeros((width, EXT), F32)
        for layer in range(2):
            rows = sides[2 * layer][...] + sides[2 * layer + 1][...]
            pick = (
                lax.broadcasted_iota(jnp.int32, (rows.shape[0], EXT), 0) + layer * (EXT // 2)
                == lax.broadcasted_iota(jnp.int32, (rows.shape[0], EXT), 1)
            ).astype(BF)
            block = block + t_dot(rows.astype(BF), pick)
        total[:, len(parts) * width :] = block.astype(BF)

    rows = blocks[0].shape[0]
    for i in range(count):
        first = pl.multiple_of(place[2 + i] * rows, rows) if count > 1 else 0
        blocks[i][...] = total[pl.ds(first, rows), :]


def last_swap(width, *refs):
    place, zero, one_left, one_right, send = refs

    @pl.when(place[0] == 0)
    def _():
        send[:, :width] = one_left[...]
        send[:, width : 2 * width] = one_right[...]
        send[:, 2 * width :] = zero[:, 2 * width :]

    @pl.when(place[0] != 0)
    def _():
        send[...] = zero[...]


def last_grads(width, experts, *refs):
    place, zero, one_left, one_right, came = refs[:5]
    query, key, value, out_proj, gain_a, gain_f, table, router = refs[5:]

    def put(half_a, side_at, values, outs):
        query[...] = half_a[:, :width]
        key[...] = half_a[:, width : 2 * width]
        value[...] = values
        out_proj[...] = outs
        side = half_a[:, 2 * width + side_at : 2 * width + side_at + EXT // 2]
        n = side.shape[0]
        across = lax.broadcasted_iota(jnp.int32, (n, n), 1)
        down = lax.broadcasted_iota(jnp.int32, (n, n), 0)

        def turned(i):
            return jnp.sum(
                jnp.where(across == down, side[:, i : i + 1], 0.0), axis=0, keepdims=True
            )

        for i, target in enumerate((gain_a, gain_f, table)):
            target[...] = turned(i)[:, : target.shape[1]]
        for e in range(experts):
            router[e : e + 1, :] = turned(LEAD + e)

    @pl.when(place[0] == 0)
    def _():
        put(zero, 0, came[:, :width], came[:, width : 2 * width])

    @pl.when(place[0] != 0)
    def _():
        put(came, EXT // 2, one_left[...], one_right[...])


def sum_blocks(count, at, *refs):
    place, parts = refs[0], refs[1 : 1 + count]
    blocks, total = refs[1 + count : -1], refs[-1]
    total[...] = sum(p[...].astype(F32) for p in parts)
    rows = blocks[0].shape[0]
    for i, block in enumerate(blocks):
        first = pl.multiple_of(place[at + i] * rows, rows) if len(blocks) > 1 else 0
        block[...] = total[pl.ds(first, rows), :].astype(block.dtype)


def join_rows(*refs):
    place, kept, came, dy = refs[:4]
    parts, (whole, later, dy_out) = refs[4:-3], refs[-3:]
    rows = parts[0].shape[0]
    for i, part in enumerate(parts):
        whole[i * rows : (i + 1) * rows, :] = part[...]
    dy_out[...] = dy[...]

    @pl.when(place[0] == 0)
    def _():
        later[...] = came[...]

    @pl.when(place[0] != 0)
    def _():
        later[...] = kept[...]


def join_columns(cut, *refs):
    parts, (left, right) = refs[:-2], refs[-2:]
    rows = parts[0].shape[0]
    for i, part in enumerate(parts):
        left[i * rows : (i + 1) * rows, :] = part[:, :cut]
        right[i * rows : (i + 1) * rows, :] = part[:, cut:]


def pack_weights(width, experts, table_rows, *refs):
    place, query, key, value, out_proj, gain_a, gain_f, table, router = refs[:9]
    send, keep, row_a, row_f, row_t, rows_r, sems = refs[9:]
    own_rows = row_a.shape[1]
    small = begin(
        [
            pltpu.make_async_copy(source, target, sems.at[4 + i])
            for i, (source, target) in enumerate(
                ((gain_a, row_a), (gain_f, row_f), (table, row_t), (router, rows_r))
            )
        ]
    )
    halves = (keep, send)
    for core in range(2):

        @pl.when(place[0] == core)
        def _(core=core):
            begin(
                [
                    pltpu.make_async_copy(
                        source,
                        halves[(core + i // 2) % 2].at[:, pl.ds(i % 2 * width, width)],
                        sems.at[i],
                    )
                    for i, source in enumerate((query, key, value, out_proj))
                ]
            )

    finish(small)
    columns = [as_column(row_a[...].astype(F32)), as_column(row_f[...].astype(F32))]
    line = row_t[...].astype(F32)
    down = lax.broadcasted_iota(jnp.int32, (own_rows, table_rows), 0)
    across = lax.broadcasted_iota(jnp.int32, (own_rows, table_rows), 1)
    columns.append(jnp.sum(jnp.where(down == across, line, 0.0), axis=1, keepdims=True))
    lines = rows_r[...].astype(F32)
    columns += [as_column(lines[e : e + 1]) for e in range(experts)]
    lane = lax.broadcasted_iota(jnp.int32, (own_rows, EXT), 1)
    block = jnp.zeros((own_rows, EXT), F32)
    for i, column in enumerate(columns):
        block = jnp.where(lane == i, column, block)
    keep[:, 2 * width :] = block.astype(BF)
    send[:, 2 * width :] = block.astype(BF)
    finish(
        [
            pltpu.make_async_copy(source, keep.at[:, pl.ds(0, width)], sems.at[i])
            for i, source in enumerate((query, key, value, out_proj))
        ]
    )


def expert_weights(other, *refs):
    place, keeps, refs = refs[0], refs[1:3], refs[3:]
    if other:
        in_ref, out_ref, held, sem = refs
    else:
        came_in, came_out, in_ref, out_ref, held, sem = refs
    for layer in range(2):

        @pl.when((place[0] == layer) != other)
        def _(layer=layer):
            pltpu.make_async_copy(keeps[layer], held, sem).start()

    pltpu.make_async_copy(keeps[0], held, sem).wait()
    grad_in = t_dot(held[0], held[1])
    grad_out = t_dot(held[2], held[3])
    if not other:
        grad_in = grad_in + came_in[...].astype(F32)
        grad_out = grad_out + came_out[...].astype(F32)
    in_ref[...] = grad_in.astype(in_ref.dtype)
    out_ref[...] = grad_out.astype(out_ref.dtype)


def body(
    feed, segments, routes, rel_bucket, gain_attn, gain_ffn, w_query, w_key, w_value, w_out_attn,
    rel_table, router, expert_in, expert_out,
):
    seq = feed.shape[2]
    width = feed.shape[3]
    experts = lax.axis_size("expert")
    shards = lax.axis_size("shard")
    cap = max(2, 2 * seq // experts)
    own_rows = w_query.shape[1]
    table_rows = rel_table.shape[1]
    quick = direct("expert") and direct("shard")
    blocks_count = experts if quick else 1
    wide = 2 * width + EXT
    side_rows = -(-(LEAD + experts) // 16) * 16
    sec = lax.axis_index("section")
    first = sec == 0
    place = jnp.concatenate(
        [
            jnp.stack([sec, lax.axis_index("expert")]).astype(jnp.int32),
            peer_ids("expert"),
            peer_ids("shard"),
        ]
    )
    row = out((seq, width))
    sems = pltpu.SemaphoreType.DMA

    small = [gain_attn, gain_ffn, rel_table, router[0].T]
    send, kept = call(
        functools.partial(pack_weights, width, experts, table_rows),
        [out((own_rows, wide))] * 2,
        [place, w_query[0], w_key[0], w_value[0], w_out_attn[0], *small],
        [SM] + [HB] * 8,
        [pltpu.VMEM(one.shape, BF) for one in small] + [sems((8,))],
    )
    came = swap(send)
    part_zero = jnp.where(first, kept, came)

    feed_own = feed[0]
    routes_own = routes[0, :, 0]
    layer_x, layer_dy, info = call(
        functools.partial(pick_inputs, seq),
        [row, row, out((8, 2 * seq), jnp.int32)],
        [
            place, feed_own, swap(feed_own), segments[:, 0], routes_own, swap(routes_own),
            rel_bucket[None, :],
        ],
        [SM, HB, AN] + [VM] * 4,
        [sems((2,))],
    )

    def both_halves(mine):
        return mine + [swap(piece) for piece in mine]

    shard_all = tuple(range(shards))
    cut = 8 * EXT
    if quick:
        own, *others = spread(part_zero, "shard")
        joined, part_one, dy_late = call(
            join_rows,
            [out(((shards - 1) * own_rows, wide)), out((own_rows, wide)), row],
            [place, kept, came, layer_dy, *others],
            [SM] + [VM] * (2 + shards),
        )
        weights_zero = both_halves(spread(own, "expert") + spread(joined, "expert"))
        columns = call(
            functools.partial(join_columns, cut),
            [out((shards * own_rows, cut)), out((shards * own_rows, wide - cut))],
            spread(part_one, "shard"),
            [VM] * shards,
            after=weights_zero[-1:],
        )
        layouts = [
            (((0,), 0), (shard_all[1:], 0)),
            ((shard_all, 0), (shard_all, cut)),
        ]
    else:
        part_one = jnp.where(first, came, kept)
        dy_late = layer_dy
        weights_zero, weights_one = [
            both_halves([lax.all_gather(part, ("expert", "shard"), axis=0, tiled=True)])
            for part in (part_zero, part_one)
        ]
        layouts = [(), ()]

    own_experts = [expert_in[0, 0], expert_out[0, 0]]
    came_experts = [swap(expert_in[0, 0]), swap(expert_out[0, 0])]

    infos = spread(info, "shard")
    if quick:
        (slots,) = call(
            functools.partial(routing_slots, shards, seq, experts, cap),
            [out((2 * shards, seq), jnp.int32)],
            [place, *infos],
            [SM] + [VM] * shards,
        )
    else:
        all_routes = jnp.stack([one[1:3, :seq] for one in infos], axis=1)
        hot = (all_routes[..., None] == peer_ids("expert")).astype(BF)
        positions = jnp.arange(seq, dtype=jnp.int32)
        before = (positions[:, None] > positions[None, :]).astype(BF)
        rank = jnp.einsum("ij,lzje->lzie", before, hot, preferred_element_type=F32)
        slot_in = jnp.arange(cap, dtype=jnp.int32).astype(F32)
        back_hot = (hot[..., None] * (rank[..., None] == slot_in).astype(BF)).reshape(
            2, shards, seq, experts * cap
        )
        to_hot = jnp.swapaxes(back_hot, 2, 3)

    block = out((shards * cap * experts // blocks_count, width))
    acts_kind = out((seq, 7 * width))
    probs_kind = out((HEADS // 2, 2 * seq, seq), F32)
    floats_kind = out((seq, width + 2 * EXT), F32)

    def buffer(kind):
        return pltpu.VMEM(kind.shape, kind.dtype)

    expert_scratch = [pltpu.VMEM((2, expert_in.shape[2], expert_in.shape[3]), BF), sems((2,))]
    expert_specs = [SM] + [AN] * 4

    def to_experts(layer, tokens, after=()):
        every = spread(tokens, "shard")
        if not quick:
            slot_rows = jnp.einsum(
                "zcs,zsd->czd", to_hot[layer], jnp.stack(every), preferred_element_type=F32
            )
            slot_rows = slot_rows.astype(BF).reshape(experts, cap * shards, width)
            moved = exchange([slot_rows[i] for i in range(experts)], "expert")
            return [jnp.concatenate(moved, axis=0)]
        blocks = call(
            functools.partial(dispatch_rows, layer, experts, shards, cap),
            [block] * experts,
            [slots, *every],
            [VM] * (1 + shards),
            after=after,
        )
        return exchange(blocks, "expert")

    def to_tokens(layer, blocks, later=()):
        if not quick:
            rows = blocks[0].reshape(experts, cap * shards, width)
            back = jnp.stack(exchange([rows[i] for i in range(experts)], "expert"))
            back = back.reshape(experts * cap, shards, width)
            tokens = jnp.einsum(
                "zsc,czd->zsd", back_hot[layer], back, preferred_element_type=F32
            ).astype(BF)
            return exchange([tokens[i] for i in range(shards)], "shard"), list(later)
        back = exchange(blocks, "expert")
        results = call(
            functools.partial(combine_rows, layer, experts, shards, cap),
            [row] * shards + [out(one.shape, one.dtype) for one in later],
            [slots, *back, *later],
            [VM] * (1 + experts + len(later)),
        )
        return exchange(results[:shards], "shard"), results[shards:]

    held_kind = out((2, width, wide))

    def attention(layer, pieces, ins, in_specs):
        count = len(pieces)
        first_outs = [row, row, row] if layer else [row]
        return call(
            functools.partial(
                attn_forward, layer, seq, width, experts, layouts[layer], count, shards, own_rows,
                table_rows,
            ),
            first_outs + [acts_kind, probs_kind, floats_kind, out((width, EXT)), held_kind],
            [place, info, *pieces, *ins],
            [SM, VM] + [VM] * count + in_specs,
            [
                buffer(held_kind), sems(()), buffer(acts_kind),
                buffer(probs_kind), buffer(floats_kind), pltpu.VMEM((width, EXT), BF), buffer(row),
                sems((5,)),
            ],
            out_specs=([VM, VM, HB] if layer else [VM]) + [HB] * 5,
        )

    def attention_back(layer, dy, state, tok, parts, after=()):
        acts, probs, floats, _, held = state
        return call(
            functools.partial(
                attn_backward, layer, seq, width, experts, shards, own_rows, table_rows,
            ),
            [
                row,
                out((seq, 4 * width)),
                out((seq, 4 * width)),
                out((side_rows, width), F32),
            ],
            [place, info, held, dy, acts, probs, floats, *tok, *parts],
            [SM, VM, HB, VM] + [HB] * (3 + len(tok)) + [VM] * shards,
            [
                buffer(held_kind), sems(()), buffer(acts_kind),
                buffer(probs_kind), buffer(floats_kind), buffer(row),
                pltpu.VMEM((seq, 3 * width), BF), pltpu.VMEM((16, 2 * seq), F32), sems((4,)),
            ],
            after=after,
        )

    keep_kind = out((4, shards * cap * experts, width))

    def back_expert(layer, rows, dys, ext_side, with_out):
        results = call(
            functools.partial(expert_backward, layer, blocks_count, experts, with_out),
            [block] * (blocks_count * (2 if with_out else 1)) + [keep_kind],
            [place, *own_experts, *came_experts, ext_side, *rows, *dys],
            expert_specs + [HB]
            + ([VM] * blocks_count + [AN] * blocks_count if with_out else [HB] + [VM] * blocks_count),
            expert_scratch + [
                buffer(keep_kind), pltpu.VMEM((width, EXT), BF),
                pltpu.VMEM(keep_kind.shape[1:], BF), sems((1 + 2 * blocks_count,)),
            ],
            out_specs=[VM] * (blocks_count * (2 if with_out else 1)) + [HB],
        )
        return results[:blocks_count], results[blocks_count:-1], results[-1]

    row_parts = experts if quick else 1

    def weight_blocks(stay, came, parts, sides=(), after=()):
        columns = len(parts) * width + (EXT if sides else 0)
        return call(
            functools.partial(attn_weights, width, row_parts, parts),
            [out((width // row_parts, columns))] * row_parts,
            [place, stay, came, *sides],
            [SM] + [VM] * (2 + len(sides)),
            [pltpu.VMEM((width, columns), BF)],
            after=after,
        )

    def sum_planes(blocks):
        if not quick:
            return blocks
        columns = blocks[0].shape[1]
        return call(
            functools.partial(sum_blocks, experts, 2 + experts),
            [out((own_rows, columns))] * shards,
            [place, *exchange(blocks, "expert")],
            [SM] + [VM] * experts,
            [pltpu.VMEM((shards * own_rows, columns), F32)],
        )

    def sum_rows(blocks):
        if not quick:
            return scatter_rows(blocks[0])
        columns = blocks[0].shape[1]
        (total,) = call(
            functools.partial(sum_blocks, shards, 0),
            [out((own_rows, columns), F32)],
            [place, *exchange(blocks, "shard")],
            [SM] + [VM] * shards,
            [pltpu.VMEM((own_rows, columns), F32)],
        )
        return total

    n2_zero, *state_zero = attention(0, weights_zero, [layer_x], [VM])
    if quick:
        weights_one = both_halves(spread(columns[0], "expert"))
    rows_zero = to_experts(0, n2_zero)
    *results, rows_zero = call(
        functools.partial(expert_forward, 0, blocks_count),
        [block] * blocks_count + [out(keep_kind.shape[1:])],
        [place, *own_experts, *came_experts, *rows_zero],
        expert_specs + [VM] * blocks_count,
        expert_scratch + [pltpu.VMEM(keep_kind.shape[1:], BF), sems(())],
        out_specs=[VM] * blocks_count + [HB],
    )
    toks, later = to_tokens(0, results, columns[1:] if quick else ())
    if quick:
        more = both_halves(spread(later[0], "expert"))
        half = len(more) // 2
        weights_one = weights_one[:half] + more[:half] + weights_one[half:] + more[half:]
    out_zero, n2_one, tok_zero, *state_one = attention(
        1, weights_one, [state_zero[2], *toks], [HB] + [VM] * shards
    )
    dys_one = to_experts(1, dy_late)
    rows_one = to_experts(1, n2_one)
    grads, results, keep_one = back_expert(1, rows_one, dys_one, state_one[3], True)
    parts_one, results = to_tokens(1, grads, results)
    toks_one, _ = to_tokens(1, results)
    dx_one, ship_one, stay_one, side_one = attention_back(
        1, layer_dy, state_one, [], parts_one, after=toks_one[:1]
    )
    came_one = swap(ship_one)
    left_one = weight_blocks(stay_one, came_one, (0,))
    dys_zero = to_experts(0, dx_one, after=left_one)
    out_one, side_one = call(
        functools.partial(last_output, seq, width, experts, shards),
        [row, out((side_rows, width), F32)],
        [info, layer_dy, state_one[0], state_one[2], side_one, *toks_one],
        [VM, VM, HB, HB, VM] + [VM] * shards,
        [buffer(row), buffer(floats_kind), sems((2,))],
    )
    side_one_came = swap(side_one)
    grads, _, keep_zero = back_expert(0, [rows_zero], dys_zero, state_zero[3], False)
    left_one = sum_planes(left_one)
    matrix = (expert_in.shape[2], expert_in.shape[3])
    keep_scratch = [pltpu.VMEM(keep_one.shape, BF), sems(())]
    sent = call(
        functools.partial(expert_weights, True),
        [out(matrix)] * 2,
        [place, keep_zero, keep_one],
        [SM, HB, HB],
        keep_scratch,
    )
    came_grads = [swap(grad) for grad in sent]
    parts_zero, _ = to_tokens(0, grads)
    right_one = weight_blocks(stay_one, came_one, (1,), after=parts_zero[:1])
    dx_zero, ship_zero, stay_zero, side_zero = attention_back(
        0, dx_one, state_zero, [tok_zero], parts_zero, after=left_one + right_one
    )
    blocks_zero = weight_blocks(
        stay_zero, swap(ship_zero), (0, 1), (side_zero, swap(side_zero), side_one, side_one_came)
    )
    sum_left = sum_rows(left_one)
    planes_right = sum_planes(right_one)
    planes_zero = sum_planes(blocks_zero)
    sum_right = sum_rows(planes_right)
    sum_zero = sum_rows(planes_zero)
    own_grads = call(
        functools.partial(expert_weights, False),
        [out(matrix, F32)] * 2,
        [place, keep_zero, keep_one, *came_grads],
        [SM, HB, HB, VM, VM],
        keep_scratch,
        after=blocks_zero[:1],
    )

    (send,) = call(
        functools.partial(last_swap, width),
        [out((own_rows, wide), F32)],
        [place, sum_zero, sum_left, sum_right],
        [SM, VM, VM, VM],
    )
    matrix_kind = out((own_rows, width), F32)
    weight_grads = call(
        functools.partial(last_grads, width, experts),
        [matrix_kind] * 4
        + [out((1, own_rows), F32)] * 2
        + [out((1, table_rows), F32), out((experts, own_rows), F32)],
        [place, sum_zero, sum_left, sum_right, swap(send)],
        [SM] + [VM] * 4,
    )

    def by_batch(zero, one):
        came = swap(jnp.where(first, one, zero))
        kept = jnp.where(first, zero, one)
        return jnp.stack([jnp.where(first, kept, came), jnp.where(first, came, kept)])

    grad_query, grad_key, grad_value, grad_out, grad_a, grad_f, grad_table, grad_router = weight_grads
    return (
        by_batch(out_zero, out_one)[None],
        by_batch(dx_zero, dx_one)[None],
        grad_a,
        grad_f,
        grad_query[None],
        grad_key[None],
        grad_value[None],
        grad_out[None],
        grad_table,
        grad_router.T[None],
        own_grads[0][None, None],
        own_grads[1][None, None],
    )


def solution(mesh):
    rows = ("expert", "shard")
    tokens = P("section", None, rows, None)
    matrix = P("section", rows, None)
    vector = P("section", rows)
    expert_specs = (P("section", "expert", None, "shard"), P("section", "expert", "shard", None))
    in_specs = (
        tokens, P(None, rows, None), tokens, P(), vector, vector, matrix, matrix, matrix, matrix,
        vector, matrix, *expert_specs,
    )
    out_specs = (
        tokens, tokens, vector, vector, matrix, matrix, matrix, matrix, vector, matrix,
        *expert_specs,
    )
    return jax.shard_map(body, mesh=mesh, in_specs=in_specs, out_specs=out_specs, check_vma=False)
```

```python
import functools
import math

import jax
import jax.numpy as jnp
import numpy as np
from jax import lax
from jax.experimental import pallas as pl
from jax.experimental.pallas import tpu as pltpu
from jax.sharding import PartitionSpec as P

HEADS = 12
HEAD_DIM = 64
NB = 32
EXT = 128
LEAD = 3
EPSILON = 1e-06
MASK_FILL = -1e30
BF = jnp.bfloat16
F32 = jnp.float32
VM = pl.BlockSpec()
SM = pl.BlockSpec(memory_space=pltpu.SMEM)
HB = pl.BlockSpec(memory_space=pltpu.HBM)
AN = pl.BlockSpec(memory_space=pl.ANY)


def dot(a, b):
    return jnp.dot(a, b, preferred_element_type=F32)


def dot_t(a, b):
    return lax.dot_general(a, b, (((1,), (1,)), ((), ())), preferred_element_type=F32)


def t_dot(a, b):
    return lax.dot_general(a, b, (((0,), (0,)), ((), ())), preferred_element_type=F32)


def swap(value):
    return lax.ppermute(value, "section", [(0, 1), (1, 0)])


def direct(axis):
    count = lax.axis_size(axis)
    return count <= 4 and count & (count - 1) == 0


def peer_ids(axis):
    count = lax.axis_size(axis)
    ids = jnp.arange(count, dtype=jnp.int32)
    return ids ^ lax.axis_index(axis) if direct(axis) else ids


def hop(value, axis, step):
    count = lax.axis_size(axis)
    return lax.ppermute(value, axis, [(i, i ^ step) for i in range(count)])


def spread(value, axis):
    count = lax.axis_size(axis)
    if direct(axis):
        return [value] + [hop(value, axis, step) for step in range(1, count)]
    every = lax.all_gather(value, axis, axis=0)
    return [every[i] for i in range(count)]


def exchange(blocks, axis):
    count = lax.axis_size(axis)
    if direct(axis):
        return [blocks[0]] + [hop(blocks[step], axis, step) for step in range(1, count)]
    swapped = lax.all_to_all(jnp.stack(blocks), axis, 0, 0, tiled=True)
    return [swapped[i] for i in range(count)]


def scatter_rows(whole):
    for axis in ("expert", "shard"):
        count = lax.axis_size(axis)
        rows = whole.shape[0] // count
        ids = peer_ids(axis)
        blocks = [
            lax.dynamic_slice_in_dim(whole, ids[i] * rows, rows, axis=0).astype(BF)
            for i in range(count)
        ]
        whole = sum(block.astype(F32) for block in exchange(blocks, axis))
    return whole


def call(kernel, outs, ins, specs, scratch=(), flops=0, out_specs=None, after=(), limit=28):
    count = len(ins)
    moved = sum(math.prod(a.shape) * a.dtype.itemsize for a in (*ins, *outs))

    def run(*refs):
        kernel(*refs[:count], *refs[count + len(after) :])

    return pl.pallas_call(
        run,
        out_shape=list(outs),
        in_specs=list(specs) + [AN] * len(after),
        out_specs=list(out_specs or [VM] * len(outs)),
        scratch_shapes=list(scratch),
        compiler_params=pltpu.CompilerParams(vmem_limit_bytes=limit * 1024 * 1024),
        cost_estimate=pl.CostEstimate(flops=flops, bytes_accessed=moved, transcendentals=0),
    )(*ins, *after)


def out(shape, kind=BF):
    return jax.ShapeDtypeStruct(shape, kind)


def begin(copies):
    for copy in copies:
        copy.start()
    return copies


def finish(copies):
    for copy in copies:
        copy.wait()


def join_weights(place, pieces, held, layout):
    plane = pieces[0].shape[0]
    for part in range(2):
        target = place[0] if part == 0 else 1 - place[0]
        for i, (peer, first) in enumerate(layout):
            piece = pieces[part * len(layout) + i]
            at = pl.multiple_of(place[2 + peer] * plane + first, piece.shape[0])
            held[target, pl.ds(at, piece.shape[0]), :] = piece[...]


def as_column(row, turned=None):
    n = row.shape[1]
    across = lax.broadcasted_iota(jnp.int32, (n, n), 1)
    down = lax.broadcasted_iota(jnp.int32, (n, n), 0)
    if turned is not None:
        down = turned - down
    return jnp.sum(jnp.where(across == down, row, jnp.zeros_like(row)), axis=1, keepdims=True)


def table_places(width, own_rows, table_rows):
    spot = lax.broadcasted_iota(jnp.int32, (16, width), 1).astype(F32)
    owner = jnp.floor((spot + 0.5) * (1.0 / own_rows))
    rest = spot - owner * own_rows
    flat = owner * table_rows + rest
    bucket = jnp.floor((flat + 0.5) * (1.0 / HEADS))
    head = flat - bucket * HEADS
    real = rest < table_rows
    row = lax.broadcasted_iota(jnp.int32, (16, width), 0).astype(F32)
    return jnp.where(real, bucket, -1.0)[0:1], (real & (head == row)).astype(F32)


def inverse_rms(value):
    return lax.rsqrt(jnp.mean(value * value, axis=-1, keepdims=True) + EPSILON)


def norm_back(value, gain, grad):
    scale = inverse_rms(value)
    scaled = value * scale
    gained = grad * gain
    back = scale * (gained - scaled * jnp.mean(gained * scaled, axis=-1, keepdims=True))
    return back, jnp.sum(grad * scaled, axis=0, keepdims=True)


def gain_rows(side):
    pick = (
        lax.broadcasted_iota(jnp.int32, (16, EXT), 0)
        == lax.broadcasted_iota(jnp.int32, (16, EXT), 1)
    ).astype(BF)
    rows = dot_t(pick, side)
    return rows[0:1], rows[1:2], rows[2:3]


def gelu_parts(value):
    c = math.sqrt(2.0 / math.pi)
    square = value * value
    inner = jnp.tanh(c * (value + 0.044715 * square * value))
    grad = 0.5 * (1.0 + inner) + 0.5 * value * (1.0 - inner * inner) * (
        c + (3.0 * 0.044715 * c) * square
    )
    return 0.5 * value * (1.0 + inner), grad


def softmax_lanes(logits, experts):
    lane = lax.broadcasted_iota(jnp.int32, logits.shape, 1)
    valid = (lane >= LEAD) & (lane < LEAD + experts)
    logits = jnp.where(valid, logits, MASK_FILL)
    power = jnp.exp(logits - jnp.max(logits, axis=-1, keepdims=True))
    power = jnp.where(valid, power, 0.0)
    return power / jnp.sum(power, axis=-1, keepdims=True), lane


def pair_rows(value):
    low_lanes = lax.broadcasted_iota(jnp.int32, value.shape, 1) < HEAD_DIM
    zero = jnp.zeros_like(value)
    return jnp.concatenate(
        [jnp.where(low_lanes, value, zero), jnp.where(low_lanes, zero, value)], axis=0
    )


def pair_lanes(value):
    half = value.shape[0] // 2
    low_lanes = lax.broadcasted_iota(jnp.int32, (half, value.shape[1]), 1) < HEAD_DIM
    return jnp.where(low_lanes, value[:half], value[half:])


def attn_forward(layer, seq, width, experts, layout, count, shards, own_rows, table_rows, *refs):
    place, info = refs[:2]
    refs = refs[2:]
    pieces, refs = refs[:count], refs[count:]
    if layer == 0:
        (x_ref,), refs = refs[:1], refs[1:]
        n2_ref, refs = refs[0], refs[1:]
        extra = []
    else:
        (hid_ref,), toks, refs = refs[:1], refs[1:-16], refs[-16:]
        out_ref, n2_ref, tok_out = refs[:3]
        refs = refs[3:]
    acts_out, probs_out, floats_out, ext_out, held_out = refs[:5]
    held, sem, acts, probs_keep, floats, ext_keep, low_keep, out_sems = refs[5:]
    if layer == 0:
        low = x_ref[...]
    else:
        coming = pltpu.make_async_copy(hid_ref, floats, out_sems.at[0])
        coming.start()
        tok = sum(t[...].astype(F32) for t in toks).astype(BF)
        low_keep[...] = tok
        coming.wait()
        gate = floats[:, width + EXT : width + EXT + 1]
        low = (floats[:, :width] + gate * tok.astype(F32)).astype(BF)
        out_ref[...] = low
        extra = begin([pltpu.make_async_copy(low_keep, tok_out, out_sems.at[0])])
    acts[:, 6 * width :] = low
    x = low.astype(F32)
    scaled = x * inverse_rms(x)
    seg_row = info[0:1, :seq]
    same = as_column(seg_row) == seg_row
    route = as_column(info[1 + layer : 2 + layer, :seq])
    bucket = as_column(info[3:4, :]).astype(F32)
    bucket_row, head_sel = table_places(width, own_rows, table_rows)
    buckets = (bucket == bucket_row).astype(BF)
    if layout:
        join_weights(place, pieces, held, layout)
    else:
        held[place[0]] = pieces[0][...]
        held[1 - place[0]] = pieces[1][...]
    extra = extra + begin([pltpu.make_async_copy(held, held_out, sem)])
    side = held[0, :, 2 * width : 2 * width + EXT]
    ext_keep[...] = side
    extra = extra + begin([pltpu.make_async_copy(ext_keep, ext_out, out_sems.at[1])])
    gain_one, gain_two, table_row = gain_rows(side)
    table = dot_t((head_sel * table_row).astype(BF), buckets)
    normed = (scaled * gain_one).astype(BF)
    acts[:, :width] = normed
    acts[:, width : 3 * width] = dot(normed, held[0, :, : 2 * width]).astype(BF)
    acts[:, 3 * width : 4 * width] = dot(normed, held[1, :, :width]).astype(BF)
    scale = 1.0 / math.sqrt(HEAD_DIM)
    contexts = []
    for p in range(HEADS // 2):
        at = [(1 + i) * width + 128 * p for i in range(3)]
        q2 = pair_rows(acts[:, at[0] : at[0] + 128])
        scores = dot_t(q2, acts[:, at[1] : at[1] + 128]) * scale
        parts = []
        for h in (2 * p, 2 * p + 1):
            line = jnp.broadcast_to(table[h : h + 1], (seq, 2 * seq))
            bias = pltpu.roll(line, seq + 1, axis=1, stride=1, stride_axis=0)[:, :seq]
            part = scores[seq * (h - 2 * p) : seq * (h - 2 * p) + seq] + bias
            parts.append(jnp.where(same, part, MASK_FILL))
        scores = jnp.concatenate(parts, axis=0)
        power = jnp.exp(scores - jnp.max(scores, axis=-1, keepdims=True))
        probs = power / jnp.sum(power, axis=-1, keepdims=True)
        probs_keep[p] = probs
        contexts.append(pair_lanes(dot(probs.astype(BF), acts[:, at[2] : at[2] + 128])))
    extra = extra + begin([pltpu.make_async_copy(probs_keep, probs_out, out_sems.at[2])])
    context = jnp.concatenate(contexts, axis=1).astype(BF)
    acts[:, 4 * width : 5 * width] = context
    hidden = x + dot(context, held[1, :, width : 2 * width])
    floats[:, :width] = hidden
    normed_two = (hidden * inverse_rms(hidden) * gain_two).astype(BF)
    n2_ref[...] = normed_two
    acts[:, 5 * width : 6 * width] = normed_two
    extra = extra + begin([pltpu.make_async_copy(acts, acts_out, out_sems.at[3])])
    gates, lane = softmax_lanes(dot(normed_two, side), experts)
    floats[:, width : width + EXT] = gates
    value = jnp.sum(jnp.where(lane == route + LEAD, gates, 0.0), axis=-1, keepdims=True)
    floats[:, width + EXT :] = jnp.broadcast_to(value, gates.shape)
    finish(extra + begin([pltpu.make_async_copy(floats, floats_out, out_sems.at[4])]))


def pick_inputs(seq, *refs):
    place, own_feed, came_feed, segments, own_routes, came_routes, buckets = refs[:7]
    x_ref, dy_ref, info, sems = refs[7:]
    sec = place[0]
    for core in range(2):

        @pl.when(sec == core)
        def _(core=core):
            sources = (own_feed, came_feed) if core == 0 else (came_feed, own_feed)
            finish(
                begin(
                    [
                        pltpu.make_async_copy(sources[0].at[core], x_ref, sems.at[0]),
                        pltpu.make_async_copy(sources[1].at[core], dy_ref, sems.at[1]),
                    ]
                )
            )
            info[...] = jnp.full(info.shape, -2, jnp.int32)
            info[0:1, :seq] = segments[core : core + 1, :]
            info[1 + core : 2 + core, :seq] = own_routes[core : core + 1, :]
            info[2 - core : 3 - core, :seq] = came_routes[core : core + 1, :]
            info[3:4, : 2 * seq - 1] = buckets[...]


def routing_slots(shards, seq, experts, cap, *refs):
    place, infos, slots = refs[0], refs[1 : 1 + shards], refs[1 + shards]
    before = (
        lax.broadcasted_iota(jnp.int32, (seq, seq), 0)
        < lax.broadcasted_iota(jnp.int32, (seq, seq), 1)
    ).astype(BF)
    routes = jnp.concatenate(
        [info[1 + layer : 2 + layer, :seq] for layer in range(2) for info in infos], axis=0
    )
    rank = jnp.zeros(routes.shape, F32)
    for e in range(experts):
        mine = (routes == e).astype(F32)
        rank = rank + mine * dot(mine.astype(BF), before)
    slots[...] = (routes ^ place[1]) * cap + rank.astype(jnp.int32)


def slot_hot(slots, layer, shards, z, total):
    row = slots[layer * shards + z : layer * shards + z + 1, :]
    return (lax.broadcasted_iota(jnp.int32, (total, row.shape[1]), 0) == row).astype(BF)


def dispatch_rows(layer, count, shards, cap, *refs):
    slots = refs[0]
    toks = refs[1 : 1 + shards]
    blocks = refs[1 + shards :]
    for z in range(shards):
        rows = dot(slot_hot(slots, layer, shards, z, count * cap), toks[z][...]).astype(BF)
        for i in range(count):
            blocks[i][z * cap : (z + 1) * cap, :] = rows[i * cap : (i + 1) * cap]


def combine_rows(layer, count, shards, cap, *refs):
    slots = refs[0]
    blocks, refs = refs[1 : 1 + count], refs[1 + count :]
    more = (len(refs) - shards) // 2
    handed, toks, given = refs[:more], refs[more : more + shards], refs[more + shards :]
    for z in range(shards):
        rows = jnp.concatenate([b[z * cap : (z + 1) * cap, :] for b in blocks], axis=0)
        toks[z][...] = t_dot(slot_hot(slots, layer, shards, z, count * cap), rows).astype(BF)
    for source, target in zip(handed, given):
        target[...] = source[...]


def start_expert(layer, place, own, came, held, sems):
    def begin(pair):
        for i in range(2):
            pltpu.make_async_copy(pair[i], held.at[i], sems.at[i]).start()

    @pl.when(place[0] == layer)
    def _():
        begin(own)

    @pl.when(place[0] != layer)
    def _():
        begin(came)

    return [pltpu.make_async_copy(own[i], held.at[i], sems.at[i]) for i in range(2)]


def expert_forward(layer, count, *refs):
    place, own, came = refs[0], refs[1:3], refs[3:5]
    blocks = refs[5 : 5 + count]
    results, rows_out = refs[5 + count : 5 + 2 * count], refs[5 + 2 * count]
    held, sems, rows, out_sem = refs[6 + 2 * count :]
    copies = start_expert(layer, place, own, came, held, sems)
    each = blocks[0].shape[0]
    for i in range(count):
        rows[i * each : (i + 1) * each, :] = blocks[i][...]
    leaving = begin([pltpu.make_async_copy(rows, rows_out, out_sem)])
    finish(copies)
    for i in range(count):
        activated = gelu_parts(dot(blocks[i][...], held[0]))[0].astype(BF)
        results[i][...] = dot(activated, held[1]).astype(BF)
    finish(leaving)


def expert_backward(layer, count, experts, with_out, *refs):
    place, own, came, ext_in = refs[0], refs[1:3], refs[3:5], refs[5]
    if with_out:
        blocks, dy_in, refs = refs[6 : 6 + count], refs[6 + count : 6 + 2 * count], refs[6 + 2 * count :]
    else:
        rows_in, dys, refs = refs[6], refs[7 : 7 + count], refs[7 + count :]
    grads, refs = refs[:count], refs[count:]
    if with_out:
        results, refs = refs[:count], refs[count:]
    keep_out, held, sems, keep, ext, late, more_sems = refs
    copies = start_expert(layer, place, own, came, held, sems)
    each = grads[0].shape[0]
    loads = [pltpu.make_async_copy(ext_in, ext, more_sems.at[0])]
    if with_out:
        loads += [
            pltpu.make_async_copy(dy_in[i], late.at[pl.ds(i * each, each), :], more_sems.at[1 + i])
            for i in range(count)
        ]
    else:
        loads += [pltpu.make_async_copy(rows_in, late, more_sems.at[1])]
    begin(loads)
    finish(loads + copies)
    leaving = []
    for i in range(count):
        at = slice(i * each, (i + 1) * each)
        if with_out:
            rows, dy = blocks[i][...], late[at, :]
        else:
            rows, dy = late[at, :], dys[i][...]
        dy = dy.astype(F32)
        gates, lane = softmax_lanes(dot(rows, ext[...]), experts)
        mine = (lane == place[1] + LEAD).astype(F32)
        value = jnp.sum(gates * mine, axis=-1, keepdims=True)
        grad_expert = (value * dy).astype(BF)
        act, slope = gelu_parts(dot(rows, held[0]))
        act = act.astype(BF)
        grad_pre = (dot_t(grad_expert, held[1]) * slope).astype(BF)
        grad = dot_t(grad_pre, held[0])
        if with_out:
            result = dot(act, held[1])
            results[i][...] = result.astype(BF)
            grad_gate = jnp.sum(dy * result, axis=-1, keepdims=True)
            grad_logits = (grad_gate * value * (mine - gates)).astype(BF)
            grad = grad + dot_t(grad_logits, ext[...])
        grads[i][...] = grad.astype(BF)
        keep[0, at, :] = rows
        keep[1, at, :] = grad_pre
        keep[2, at, :] = act
        keep[3, at, :] = grad_expert
        leaving += begin(
            [
                pltpu.make_async_copy(
                    keep.at[:, pl.ds(i * each, each), :],
                    keep_out.at[:, pl.ds(i * each, each), :],
                    more_sems.at[1 + count + i],
                )
            ]
        )
    finish(leaving)


def attn_backward(layer, seq, width, experts, shards, own_rows, table_rows, *refs):
    place, info, held_in = refs[:3]
    refs = refs[3:]
    dy_ref, acts_in, probs_in, floats_in = refs[:4]
    refs = refs[4:]
    if layer == 0:
        tok_in, refs = refs[0], refs[1:]
    parts, refs = refs[:shards], refs[shards:]
    dx_ref, ship, stay, side_grad = refs[:4]
    ship_all, ship = ship, ship.at[pl.ds(0, seq), :]
    held, sem, acts, probs_all, floats, tok_keep, gj, g_rel, in_sems = refs[4:]
    loads = [
        pltpu.make_async_copy(floats_in, floats, in_sems.at[0]),
        pltpu.make_async_copy(acts_in, acts, in_sems.at[1]),
        pltpu.make_async_copy(probs_in, probs_all, in_sems.at[2]),
    ]
    if layer == 0:
        loads.append(pltpu.make_async_copy(tok_in, tok_keep, in_sems.at[3]))
    begin(loads)
    copies = begin([pltpu.make_async_copy(held_in, held, sem)])
    dy = dy_ref[...].astype(F32)
    grad_norm_two = sum(p[...].astype(F32) for p in parts)
    route = as_column(info[1 + layer : 2 + layer, :seq])
    bucket = as_column(info[3:4, :], 2 * seq - 2).astype(F32)
    bucket_row, head_sel = table_places(width, own_rows, table_rows)
    buckets = (bucket == bucket_row).astype(BF)
    finish(loads)
    hidden = floats[:, :width]
    x = acts[:, 6 * width :].astype(F32)
    state = acts
    finish(copies)
    side = held[0, :, 2 * width : 2 * width + EXT]
    gain_one, gain_two, _ = gain_rows(side)
    side_grad[...] = jnp.zeros_like(side_grad)
    if layer == 0:
        gates = floats[:, width : width + EXT]
        lane = lax.broadcasted_iota(jnp.int32, gates.shape, 1)
        hot = (lane == route + LEAD).astype(F32)
        grad_gate = jnp.sum(dy * tok_keep[...].astype(F32), axis=-1, keepdims=True)
        value = floats[:, width + EXT : width + EXT + 1]
        grad_logits = (grad_gate * value * (hot - gates)).astype(BF)
        grad_norm_two = grad_norm_two + dot_t(grad_logits, side)
        router_rows = t_dot(grad_logits, acts[:, 5 * width : 6 * width])
        side_grad[...] = router_rows[: side_grad.shape[0]]
    back, gain_two_grad = norm_back(hidden, gain_two, grad_norm_two)
    grad_hidden = dy + back
    grad_hidden_low = grad_hidden.astype(BF)
    grad_context = dot_t(grad_hidden_low, held[1, :, width : 2 * width]).astype(BF)
    scale = 1.0 / math.sqrt(HEAD_DIM)
    mirror = (
        lax.broadcasted_iota(jnp.int32, (seq, 2 * seq), 0)
        + lax.broadcasted_iota(jnp.int32, (seq, 2 * seq), 1)
        == seq - 1
    ).astype(BF)
    for p in range(HEADS // 2):
        lanes = slice(128 * p, 128 * p + 128)
        q2 = pair_rows(state[:, width + 128 * p : width + 128 * p + 128])
        keys = state[:, 2 * width + 128 * p : 2 * width + 128 * p + 128]
        vals = state[:, 3 * width + 128 * p : 3 * width + 128 * p + 128]
        g2 = pair_rows(grad_context[:, lanes])
        probs = probs_all[p]
        grad_probs = dot_t(g2, vals)
        grad_scores = probs * (
            grad_probs - jnp.sum(probs * grad_probs, axis=-1, keepdims=True)
        )
        grad_scores = grad_scores.astype(BF)
        gj[:, lanes] = (pair_lanes(dot(grad_scores, keys)) * scale).astype(BF)
        gj[:, width + 128 * p : width + 128 * p + 128] = (t_dot(grad_scores, q2) * scale).astype(BF)
        gj[:, 2 * width + 128 * p : 2 * width + 128 * p + 128] = t_dot(
            probs.astype(BF), g2
        ).astype(BF)
        turned = dot(grad_scores, mirror)
        for h in range(2):
            shifted = pltpu.roll(turned[h * seq : (h + 1) * seq], 0, axis=1, stride=1, stride_axis=0)
            g_rel[2 * p + h : 2 * p + h + 1, :] = jnp.sum(shifted, axis=0, keepdims=True)
    g_rel[HEADS:, :] = jnp.zeros_like(g_rel[HEADS:, :])
    offsets = g_rel[...]
    high = offsets.astype(BF)
    low = (offsets - high.astype(F32)).astype(BF)
    by_row = dot(high, buckets) + dot(low, buckets)
    side_grad[2:3, :] = jnp.sum(by_row * head_sel, axis=0, keepdims=True)
    side_grad[1:2, :] = gain_two_grad
    grad_normed = dot_t(gj[:, : 2 * width], held[0, :, : 2 * width]) + dot_t(
        gj[:, 2 * width :], held[1, :, :width]
    )
    back, gain_one_grad = norm_back(x, gain_one, grad_normed)
    side_grad[0:1, :] = gain_one_grad
    dx_ref[...] = (grad_hidden + back).astype(BF)
    normed = state[:, :width]
    halves = (ship, stay)
    for core in range(2):

        @pl.when(place[0] == core)
        def _(core=core):
            halves[1 - core][:, :width] = normed
            halves[1 - core][:, width : 3 * width] = gj[:, : 2 * width]
            halves[1 - core][:, 3 * width :] = jnp.zeros_like(normed)
            halves[core][:, :width] = normed
            halves[core][:, width : 2 * width] = gj[:, 2 * width :]
            halves[core][:, 2 * width : 3 * width] = state[:, 4 * width : 5 * width]
            halves[core][:, 3 * width :] = grad_hidden_low

    ship_all[seq:, :width] = side_grad[...].astype(BF)
    ship_all[seq:, width:] = jnp.zeros_like(ship_all[seq:, width:])


def last_output(seq, width, experts, shards, *refs):
    info, dy_ref, acts_in, floats_in, side_in = refs[:5]
    parts, refs = refs[5 : 5 + shards], refs[5 + shards :]
    out_ref, side_grad, normed, floats, sems = refs
    loads = begin(
        [
            pltpu.make_async_copy(floats_in, floats, sems.at[0]),
            pltpu.make_async_copy(acts_in.at[:, pl.ds(5 * width, width)], normed, sems.at[1]),
        ]
    )
    tok = sum(p[...].astype(F32) for p in parts).astype(BF).astype(F32)
    finish(loads)
    value = floats[:, width + EXT : width + EXT + 1]
    out_ref[...] = (floats[:, :width] + value * tok).astype(BF)
    gates = floats[:, width : width + EXT]
    lane = lax.broadcasted_iota(jnp.int32, gates.shape, 1)
    hot = (lane == as_column(info[2:3, :seq]) + LEAD).astype(F32)
    grad_gate = jnp.sum(dy_ref[...].astype(F32) * tok, axis=-1, keepdims=True)
    grad_logits = (grad_gate * value * (hot - gates)).astype(BF)
    side_grad[...] = side_in[...] + t_dot(grad_logits, normed[...])[: side_grad.shape[0]]


def attn_weights(width, count, parts, more, *refs):
    place, stay, came = refs[:3]
    total = refs[-1]
    handed, sides, outs = refs[3 : 3 + more], refs[3 + more : -1 - count - more], refs[-1 - count - more : -1]
    blocks, given = outs[:count], outs[count:]
    for source, target in zip(handed, given):
        target[...] = source[...]

    seq = stay.shape[0]

    def both(first, last):
        return jnp.concatenate([stay[:, first:last], came[:seq, first:last]], axis=0)

    unit = width // 2
    for i, part in enumerate(parts):
        at = slice(i * unit, (i + 1) * unit)

        @pl.when(place[0] == 0)
        def _(part=part, at=at):
            total[:, at] = t_dot(
                both(0, width), both(width + part * unit, width + (part + 1) * unit)
            ).astype(BF)

        @pl.when(place[0] != 0)
        def _(part=part, at=at):
            left = part // 2 * 2 * width
            right = left + width + part % 2 * unit
            total[:, at] = t_dot(both(left, left + width), both(right, right + unit)).astype(BF)

    if sides:
        block = jnp.zeros((width, EXT), F32)
        ours = (sides[0][...] + came[seq:, :width].astype(F32), sides[1][...] + sides[2][...])
        for layer, rows in enumerate(ours):
            pick = (
                lax.broadcasted_iota(jnp.int32, (rows.shape[0], EXT), 0) + layer * (EXT // 2)
                == lax.broadcasted_iota(jnp.int32, (rows.shape[0], EXT), 1)
            ).astype(BF)
            block = block + t_dot(rows.astype(BF), pick)
        total[:, len(parts) * unit :] = block.astype(BF)

    rows = blocks[0].shape[0]
    for i in range(count):
        first = pl.multiple_of(place[2 + i] * rows, rows) if count > 1 else 0
        blocks[i][...] = total[pl.ds(first, rows), :]


def last_swap(width, *refs):
    place, zero, one, send = refs

    @pl.when(place[0] == 0)
    def _():
        send[:, : 2 * width] = one[...]
        send[:, 2 * width :] = zero[:, 2 * width :]

    @pl.when(place[0] != 0)
    def _():
        send[...] = zero[...]


def last_grads(width, experts, *refs):
    place, zero, one, came = refs[:4]
    query, key, value, out_proj, gain_a, gain_f, table, router = refs[4:]

    def put_side(side):
        n = side.shape[0]
        across = lax.broadcasted_iota(jnp.int32, (n, n), 1)
        down = lax.broadcasted_iota(jnp.int32, (n, n), 0)

        def turned(i):
            return jnp.sum(
                jnp.where(across == down, side[:, i : i + 1], 0.0), axis=0, keepdims=True
            )

        for i, target in enumerate((gain_a, gain_f, table)):
            target[...] = turned(i)[:, : target.shape[1]]
        for e in range(experts):
            router[e : e + 1, :] = turned(LEAD + e)

    @pl.when(place[0] == 0)
    def _():
        query[...] = zero[:, :width]
        key[...] = zero[:, width : 2 * width]
        value[...] = came[:, :width]
        out_proj[...] = came[:, width : 2 * width]
        put_side(zero[:, 2 * width : 2 * width + EXT // 2])

    @pl.when(place[0] != 0)
    def _():
        query[...] = came[:, :width]
        key[...] = came[:, width : 2 * width]
        value[...] = one[:, :width]
        out_proj[...] = one[:, width:]
        put_side(came[:, 2 * width + EXT // 2 :])


def sum_blocks(count, at, *refs):
    place, parts = refs[0], refs[1 : 1 + count]
    blocks, total = refs[1 + count : -1], refs[-1]
    total[...] = sum(p[...].astype(F32) for p in parts)
    rows = blocks[0].shape[0]
    for i, block in enumerate(blocks):
        first = pl.multiple_of(place[at + i] * rows, rows) if len(blocks) > 1 else 0
        block[...] = total[pl.ds(first, rows), :].astype(block.dtype)


def join_rows(count, first_id, *refs):
    place, parts, whole = refs[0], refs[1 : 1 + count], refs[1 + count]
    rows = parts[0].shape[0]
    for i in range(count):
        at = pl.multiple_of(place[first_id + i] * rows, rows)
        whole[pl.ds(at, rows), :] = parts[i][...]


def pick_later(*refs):
    place, kept, came, later = refs

    @pl.when(place[0] == 0)
    def _():
        later[...] = came[...]

    @pl.when(place[0] != 0)
    def _():
        later[...] = kept[...]


def pack_weights(width, experts, table_rows, *refs):
    place, query, key, value, out_proj, gain_a, gain_f, table, router = refs[:9]
    send, keep, row_a, row_f, row_t, rows_r, sems = refs[9:]
    own_rows = row_a.shape[1]
    small = begin(
        [
            pltpu.make_async_copy(source, target, sems.at[4 + i])
            for i, (source, target) in enumerate(
                ((gain_a, row_a), (gain_f, row_f), (table, row_t), (router, rows_r))
            )
        ]
    )
    halves = (keep, send)
    for core in range(2):

        @pl.when(place[0] == core)
        def _(core=core):
            begin(
                [
                    pltpu.make_async_copy(
                        source,
                        halves[(core + i // 2) % 2].at[:, pl.ds(i % 2 * width, width)],
                        sems.at[i],
                    )
                    for i, source in enumerate((query, key, value, out_proj))
                ]
            )

    finish(small)
    columns = [as_column(row_a[...].astype(F32)), as_column(row_f[...].astype(F32))]
    line = row_t[...].astype(F32)
    down = lax.broadcasted_iota(jnp.int32, (own_rows, table_rows), 0)
    across = lax.broadcasted_iota(jnp.int32, (own_rows, table_rows), 1)
    columns.append(jnp.sum(jnp.where(down == across, line, 0.0), axis=1, keepdims=True))
    lines = rows_r[...].astype(F32)
    columns += [as_column(lines[e : e + 1]) for e in range(experts)]
    lane = lax.broadcasted_iota(jnp.int32, (own_rows, EXT), 1)
    block = jnp.zeros((own_rows, EXT), F32)
    for i, column in enumerate(columns):
        block = jnp.where(lane == i, column, block)
    keep[:, 2 * width :] = block.astype(BF)
    send[:, 2 * width :] = block.astype(BF)
    finish(
        [
            pltpu.make_async_copy(source, keep.at[:, pl.ds(0, width)], sems.at[i])
            for i, source in enumerate((query, key, value, out_proj))
        ]
    )


def expert_weights(other, *refs):
    place, keeps, refs = refs[0], refs[1:3], refs[3:]
    if other:
        in_ref, out_ref, held, sem = refs
    else:
        came_in, came_out, in_ref, out_ref, held, sem = refs
    for layer in range(2):

        @pl.when((place[0] == layer) != other)
        def _(layer=layer):
            pltpu.make_async_copy(keeps[layer], held, sem).start()

    pltpu.make_async_copy(keeps[0], held, sem).wait()
    grad_in = t_dot(held[0], held[1])
    grad_out = t_dot(held[2], held[3])
    if not other:
        grad_in = grad_in + came_in[...].astype(F32)
        grad_out = grad_out + came_out[...].astype(F32)
    in_ref[...] = grad_in.astype(in_ref.dtype)
    out_ref[...] = grad_out.astype(out_ref.dtype)


def body(
    feed, segments, routes, rel_bucket, gain_attn, gain_ffn, w_query, w_key, w_value, w_out_attn,
    rel_table, router, expert_in, expert_out,
):
    seq = feed.shape[2]
    width = feed.shape[3]
    experts = lax.axis_size("expert")
    shards = lax.axis_size("shard")
    cap = max(2, 2 * seq // experts)
    own_rows = w_query.shape[1]
    table_rows = rel_table.shape[1]
    quick = direct("expert") and direct("shard")
    blocks_count = experts if quick else 1
    wide = 2 * width + EXT
    side_rows = -(-(LEAD + experts) // 16) * 16
    sec = lax.axis_index("section")
    first = sec == 0
    place = jnp.concatenate(
        [
            jnp.stack([sec, lax.axis_index("expert")]).astype(jnp.int32),
            peer_ids("expert"),
            peer_ids("shard"),
        ]
    )
    row = out((seq, width))
    sems = pltpu.SemaphoreType.DMA

    small = [gain_attn, gain_ffn, rel_table, router[0].T]
    send, kept = call(
        functools.partial(pack_weights, width, experts, table_rows),
        [out((own_rows, wide))] * 2,
        [place, w_query[0], w_key[0], w_value[0], w_out_attn[0], *small],
        [SM] + [HB] * 8,
        [pltpu.VMEM(one.shape, BF) for one in small] + [sems((8,))],
        limit=60,
    )
    came = swap(send)
    part_zero = jnp.where(first, kept, came)

    own_experts = [expert_in[0, 0], expert_out[0, 0]]
    came_experts = [swap(expert_in[0, 0]), swap(expert_out[0, 0])]

    feed_own = feed[0]
    routes_own = routes[0, :, 0]
    layer_x, layer_dy, info = call(
        functools.partial(pick_inputs, seq),
        [row, row, out((8, 2 * seq), jnp.int32)],
        [
            place, feed_own, swap(feed_own), segments[:, 0], routes_own, swap(routes_own),
            rel_bucket[None, :],
        ],
        [SM, HB, AN] + [VM] * 4,
        [sems((2,))],
        after=came_experts,
    )

    infos = spread(info, "shard")


    def both_halves(mine):
        return mine + [swap(piece) for piece in mine]

    def plane_of(part, after=()):
        return call(
            functools.partial(join_rows, shards, 2 + experts),
            [out((shards * own_rows, wide))],
            [place, *spread(part, "shard")],
            [SM] + [VM] * shards,
            after=after,
        )[0]

    peers = [(i, 0) for i in range(experts)]
    if quick:
        planes = spread(plane_of(part_zero, after=[info]), "expert")
        weights_zero = both_halves(planes)
        joined_after = planes[1:]
        layouts = [peers, ()]
        (part_one,) = call(
            pick_later,
            [out((own_rows, wide))],
            [place, kept, came],
            [SM, VM, VM],
        )
        planes_one = spread(plane_of(part_one, after=joined_after), "expert")
    else:
        part_one = jnp.where(first, came, kept)
        weights_zero, weights_one = [
            both_halves([lax.all_gather(part, ("expert", "shard"), axis=0, tiled=True)])
            for part in (part_zero, part_one)
        ]
        joined_after = ()
        layouts = [(), ()]


    if quick:
        (slots,) = call(
            functools.partial(routing_slots, shards, seq, experts, cap),
            [out((2 * shards, seq), jnp.int32)],
            [place, *infos],
            [SM] + [VM] * shards,
            after=joined_after,
        )
    else:
        all_routes = jnp.stack([one[1:3, :seq] for one in infos], axis=1)
        hot = (all_routes[..., None] == peer_ids("expert")).astype(BF)
        positions = jnp.arange(seq, dtype=jnp.int32)
        before = (positions[:, None] > positions[None, :]).astype(BF)
        rank = jnp.einsum("ij,lzje->lzie", before, hot, preferred_element_type=F32)
        slot_in = jnp.arange(cap, dtype=jnp.int32).astype(F32)
        back_hot = (hot[..., None] * (rank[..., None] == slot_in).astype(BF)).reshape(
            2, shards, seq, experts * cap
        )
        to_hot = jnp.swapaxes(back_hot, 2, 3)

    block = out((shards * cap * experts // blocks_count, width))
    acts_kind = out((seq, 7 * width))
    probs_kind = out((HEADS // 2, 2 * seq, seq), F32)
    floats_kind = out((seq, width + 2 * EXT), F32)

    def buffer(kind):
        return pltpu.VMEM(kind.shape, kind.dtype)

    expert_scratch = [pltpu.VMEM((2, expert_in.shape[2], expert_in.shape[3]), BF), sems((2,))]
    expert_specs = [SM] + [AN] * 4

    def to_experts(layer, tokens, after=()):
        every = spread(tokens, "shard")
        if not quick:
            slot_rows = jnp.einsum(
                "zcs,zsd->czd", to_hot[layer], jnp.stack(every), preferred_element_type=F32
            )
            slot_rows = slot_rows.astype(BF).reshape(experts, cap * shards, width)
            moved = exchange([slot_rows[i] for i in range(experts)], "expert")
            return [jnp.concatenate(moved, axis=0)]
        blocks = call(
            functools.partial(dispatch_rows, layer, experts, shards, cap),
            [block] * experts,
            [slots, *every],
            [VM] * (1 + shards),
            after=after,
        )
        return exchange(blocks, "expert")

    def to_tokens(layer, blocks, later=(), after=()):
        if not quick:
            rows = blocks[0].reshape(experts, cap * shards, width)
            back = jnp.stack(exchange([rows[i] for i in range(experts)], "expert"))
            back = back.reshape(experts * cap, shards, width)
            tokens = jnp.einsum(
                "zsc,czd->zsd", back_hot[layer], back, preferred_element_type=F32
            ).astype(BF)
            return exchange([tokens[i] for i in range(shards)], "shard"), list(later)
        back = exchange(blocks, "expert")
        results = call(
            functools.partial(combine_rows, layer, experts, shards, cap),
            [row] * shards + [out(one.shape, one.dtype) for one in later],
            [slots, *back, *later],
            [VM] * (1 + experts + len(later)),
            after=after,
        )
        return exchange(results[:shards], "shard"), results[shards:]

    held_kind = out((2, width, wide))

    def attention(layer, pieces, ins, in_specs, after=()):
        count = len(pieces)
        first_outs = [row, row, row] if layer else [row]
        return call(
            functools.partial(
                attn_forward, layer, seq, width, experts, layouts[layer], count, shards, own_rows,
                table_rows,
            ),
            first_outs + [acts_kind, probs_kind, floats_kind, out((width, EXT)), held_kind],
            [place, info, *pieces, *ins],
            [SM, VM] + [VM] * count + in_specs,
            [
                buffer(held_kind), sems(()), buffer(acts_kind),
                buffer(probs_kind), buffer(floats_kind), pltpu.VMEM((width, EXT), BF), buffer(row),
                sems((5,)),
            ],
            out_specs=([VM, VM, HB] if layer else [VM]) + [HB] * 5,
            after=after,
        )

    def attention_back(layer, dy, state, tok, parts, after=()):
        acts, probs, floats, _, held = state
        return call(
            functools.partial(
                attn_backward, layer, seq, width, experts, shards, own_rows, table_rows,
            ),
            [
                row,
                out((seq + side_rows, 4 * width)),
                out((seq, 4 * width)),
                out((side_rows, width), F32),
            ],
            [place, info, held, dy, acts, probs, floats, *tok, *parts],
            [SM, VM, HB, VM] + [HB] * (3 + len(tok)) + [VM] * shards,
            [
                buffer(held_kind), sems(()), buffer(acts_kind),
                buffer(probs_kind), buffer(floats_kind), buffer(row),
                pltpu.VMEM((seq, 3 * width), BF), pltpu.VMEM((16, 2 * seq), F32), sems((4,)),
            ],
            after=after,
        )

    keep_kind = out((4, shards * cap * experts, width))

    def back_expert(layer, rows, dys, ext_side, with_out):
        results = call(
            functools.partial(expert_backward, layer, blocks_count, experts, with_out),
            [block] * (blocks_count * (2 if with_out else 1)) + [keep_kind],
            [place, *own_experts, *came_experts, ext_side, *rows, *dys],
            expert_specs + [HB]
            + ([VM] * blocks_count + [AN] * blocks_count if with_out else [HB] + [VM] * blocks_count),
            expert_scratch + [
                buffer(keep_kind), pltpu.VMEM((width, EXT), BF),
                pltpu.VMEM(keep_kind.shape[1:], BF), sems((1 + 2 * blocks_count,)),
            ],
            out_specs=[VM] * (blocks_count * (2 if with_out else 1)) + [HB],
        )
        return results[:blocks_count], results[blocks_count:-1], results[-1]

    row_parts = experts if quick else 1

    def weight_blocks(stay, came, parts, sides=(), after=(), later=()):
        columns = len(parts) * (width // 2) + (EXT if sides else 0)
        return call(
            functools.partial(attn_weights, width, row_parts, parts, len(later)),
            [out((width // row_parts, columns))] * row_parts
            + [out(one.shape, one.dtype) for one in later],
            [place, stay, came, *later, *sides],
            [SM] + [VM] * (2 + len(sides) + len(later)),
            [pltpu.VMEM((width, columns), BF)],
            after=after,
        )

    def sum_planes(blocks, after=()):
        if not quick:
            return blocks
        columns = blocks[0].shape[1]
        return call(
            functools.partial(sum_blocks, experts, 2 + experts),
            [out((own_rows, columns))] * shards,
            [place, *exchange(blocks, "expert")],
            [SM] + [VM] * experts,
            [pltpu.VMEM((shards * own_rows, columns), F32)],
            after=after,
        )

    def sum_rows(blocks):
        if not quick:
            return scatter_rows(blocks[0])
        columns = blocks[0].shape[1]
        (total,) = call(
            functools.partial(sum_blocks, shards, 0),
            [out((own_rows, columns), F32)],
            [place, *exchange(blocks, "shard")],
            [SM] + [VM] * shards,
            [pltpu.VMEM((own_rows, columns), F32)],
        )
        return total

    n2_zero, *state_zero = attention(
        0, weights_zero, [layer_x], [VM], after=[slots] if quick else ()
    )
    rows_zero = to_experts(0, n2_zero)
    *results, rows_zero = call(
        functools.partial(expert_forward, 0, blocks_count),
        [block] * blocks_count + [out(keep_kind.shape[1:])],
        [place, *own_experts, *came_experts, *rows_zero],
        expert_specs + [VM] * blocks_count,
        expert_scratch + [pltpu.VMEM(keep_kind.shape[1:], BF), sems(())],
        out_specs=[VM] * blocks_count + [HB],
        after=planes_one[1:] if quick else (),
    )
    toks, _ = to_tokens(0, results)
    if quick:
        (gathered,) = call(
            functools.partial(join_rows, experts, 2),
            [out((width, wide))],
            [place, *planes_one],
            [SM] + [VM] * experts,
            after=results[:1],
        )
        weights_one = both_halves([gathered])
    out_zero, n2_one, tok_zero, *state_one = attention(
        1, weights_one, [state_zero[2], *toks], [HB] + [VM] * shards
    )
    dys_one = to_experts(1, layer_dy)
    rows_one = to_experts(1, n2_one)
    grads, results, keep_one = back_expert(1, rows_one, dys_one, state_one[3], True)
    parts_one, results = to_tokens(1, grads, results)
    toks_one, _ = to_tokens(1, results)
    dx_one, ship_one, stay_one, side_one = attention_back(
        1, layer_dy, state_one, [], parts_one, after=toks_one[:1]
    )
    came_one = swap(ship_one)
    dys_zero = to_experts(0, dx_one)
    out_one, side_one = call(
        functools.partial(last_output, seq, width, experts, shards),
        [row, out((side_rows, width), F32)],
        [info, layer_dy, state_one[0], state_one[2], side_one, *toks_one],
        [VM, VM, HB, HB, VM] + [VM] * shards,
        [buffer(row), buffer(floats_kind), sems((2,))],
    )
    side_one_came = swap(side_one)
    grads, _, keep_zero = back_expert(0, [rows_zero], dys_zero, state_zero[3], False)
    matrix = (expert_in.shape[2], expert_in.shape[3])
    keep_scratch = [pltpu.VMEM(keep_one.shape, BF), sems(())]
    sent = call(
        functools.partial(expert_weights, True),
        [out(matrix)] * 2,
        [place, keep_zero, keep_one],
        [SM, HB, HB],
        keep_scratch,
    )
    came_grads = [swap(grad) for grad in sent]
    parts_zero, _ = to_tokens(0, grads, after=[side_one_came])
    blocks_one = weight_blocks(stay_one, came_one, (0, 1, 2, 3), after=parts_zero[:1])
    dx_zero, ship_zero, stay_zero, side_zero = attention_back(
        0, dx_one, state_zero, [tok_zero], parts_zero, after=[blocks_one[0], sent[0]]
    )
    planes_one_sum = sum_planes(blocks_one)
    came_zero = swap(ship_zero)
    blocks_zero = weight_blocks(
        stay_zero, came_zero, (0, 1, 2, 3), (side_zero, side_one, side_one_came),
        after=planes_one_sum[:1],
    )
    sum_one = sum_rows(planes_one_sum)
    own_grads = call(
        functools.partial(expert_weights, False),
        [out(matrix, F32)] * 2,
        [place, keep_zero, keep_one, *came_grads],
        [SM, HB, HB, VM, VM],
        keep_scratch,
        after=blocks_zero[:1],
    )
    sum_zero = sum_rows(sum_planes(blocks_zero, after=own_grads[:1]))
    (send,) = call(
        functools.partial(last_swap, width),
        [out((own_rows, wide), F32)],
        [place, sum_zero, sum_one],
        [SM] + [VM] * 2,
    )
    matrix_kind = out((own_rows, width), F32)
    weight_grads = call(
        functools.partial(last_grads, width, experts),
        [matrix_kind] * 4
        + [out((1, own_rows), F32)] * 2
        + [out((1, table_rows), F32), out((experts, own_rows), F32)],
        [place, sum_zero, sum_one, swap(send)],
        [SM] + [VM] * 3,
    )

    def by_batch(zero, one):
        came = swap(jnp.where(first, one, zero))
        kept = jnp.where(first, zero, one)
        return jnp.stack([jnp.where(first, kept, came), jnp.where(first, came, kept)])

    grad_query, grad_key, grad_value, grad_out, grad_a, grad_f, grad_table, grad_router = weight_grads
    return (
        by_batch(out_zero, out_one)[None],
        by_batch(dx_zero, dx_one)[None],
        grad_a,
        grad_f,
        grad_query[None],
        grad_key[None],
        grad_value[None],
        grad_out[None],
        grad_table,
        grad_router.T[None],
        own_grads[0][None, None],
        own_grads[1][None, None],
    )


def solution(mesh):
    rows = ("expert", "shard")
    tokens = P("section", None, rows, None)
    matrix = P("section", rows, None)
    vector = P("section", rows)
    expert_specs = (P("section", "expert", None, "shard"), P("section", "expert", "shard", None))
    in_specs = (
        tokens, P(None, rows, None), tokens, P(), vector, vector, matrix, matrix, matrix, matrix,
        vector, matrix, *expert_specs,
    )
    out_specs = (
        tokens, tokens, vector, vector, matrix, matrix, matrix, matrix, vector, matrix,
        *expert_specs,
    )
    return jax.shard_map(body, mesh=mesh, in_specs=in_specs, out_specs=out_specs, check_vma=False)
```

```python
import functools
import math

import jax
import jax.numpy as jnp
import numpy as np
from jax import lax
from jax.experimental import pallas as pl
from jax.experimental.pallas import tpu as pltpu
from jax.sharding import PartitionSpec as P

HEADS = 12
HEAD_DIM = 64
NB = 32
EXT = 128
LEAD = 3
EPSILON = 1e-06
MASK_FILL = -1e30
BF = jnp.bfloat16
F32 = jnp.float32
VM = pl.BlockSpec()
SM = pl.BlockSpec(memory_space=pltpu.SMEM)
HB = pl.BlockSpec(memory_space=pltpu.HBM)
AN = pl.BlockSpec(memory_space=pl.ANY)


def dot(a, b):
    return jnp.dot(a, b, preferred_element_type=F32)


def dot_t(a, b):
    return lax.dot_general(a, b, (((1,), (1,)), ((), ())), preferred_element_type=F32)


def t_dot(a, b):
    return lax.dot_general(a, b, (((0,), (0,)), ((), ())), preferred_element_type=F32)


def swap(value):
    return lax.ppermute(value, "section", [(0, 1), (1, 0)])


def direct(axis):
    count = lax.axis_size(axis)
    return count <= 4 and count & (count - 1) == 0


def peer_ids(axis):
    count = lax.axis_size(axis)
    ids = jnp.arange(count, dtype=jnp.int32)
    return ids ^ lax.axis_index(axis) if direct(axis) else ids


def hop(value, axis, step):
    count = lax.axis_size(axis)
    return lax.ppermute(value, axis, [(i, i ^ step) for i in range(count)])


def spread(value, axis):
    count = lax.axis_size(axis)
    if direct(axis):
        return [value] + [hop(value, axis, step) for step in range(1, count)]
    every = lax.all_gather(value, axis, axis=0)
    return [every[i] for i in range(count)]


def exchange(blocks, axis):
    count = lax.axis_size(axis)
    if direct(axis):
        return [blocks[0]] + [hop(blocks[step], axis, step) for step in range(1, count)]
    swapped = lax.all_to_all(jnp.stack(blocks), axis, 0, 0, tiled=True)
    return [swapped[i] for i in range(count)]


def scatter_rows(whole):
    for axis in ("expert", "shard"):
        count = lax.axis_size(axis)
        rows = whole.shape[0] // count
        ids = peer_ids(axis)
        blocks = [
            lax.dynamic_slice_in_dim(whole, ids[i] * rows, rows, axis=0).astype(BF)
            for i in range(count)
        ]
        whole = sum(block.astype(F32) for block in exchange(blocks, axis))
    return whole


def call(kernel, outs, ins, specs, scratch=(), flops=0, out_specs=None, after=(), limit=28):
    count = len(ins)
    moved = sum(math.prod(a.shape) * a.dtype.itemsize for a in (*ins, *outs))

    def run(*refs):
        kernel(*refs[:count], *refs[count + len(after) :])

    return pl.pallas_call(
        run,
        out_shape=list(outs),
        in_specs=list(specs) + [AN] * len(after),
        out_specs=list(out_specs or [VM] * len(outs)),
        scratch_shapes=list(scratch),
        compiler_params=pltpu.CompilerParams(vmem_limit_bytes=limit * 1024 * 1024),
        cost_estimate=pl.CostEstimate(flops=flops, bytes_accessed=moved, transcendentals=0),
    )(*ins, *after)


def out(shape, kind=BF):
    return jax.ShapeDtypeStruct(shape, kind)


def begin(copies):
    for copy in copies:
        copy.start()
    return copies


def finish(copies):
    for copy in copies:
        copy.wait()


def join_weights(place, pieces, held, layout):
    plane = pieces[0].shape[0]
    for part in range(2):
        target = place[0] if part == 0 else 1 - place[0]
        for i, (peer, first) in enumerate(layout):
            piece = pieces[part * len(layout) + i]
            at = pl.multiple_of(place[2 + peer] * plane + first, piece.shape[0])
            held[target, pl.ds(at, piece.shape[0]), :] = piece[...]


def as_column(row, turned=None):
    n = row.shape[1]
    across = lax.broadcasted_iota(jnp.int32, (n, n), 1)
    down = lax.broadcasted_iota(jnp.int32, (n, n), 0)
    if turned is not None:
        down = turned - down
    return jnp.sum(jnp.where(across == down, row, jnp.zeros_like(row)), axis=1, keepdims=True)


def table_places(width, own_rows, table_rows):
    spot = lax.broadcasted_iota(jnp.int32, (16, width), 1).astype(F32)
    owner = jnp.floor((spot + 0.5) * (1.0 / own_rows))
    rest = spot - owner * own_rows
    flat = owner * table_rows + rest
    bucket = jnp.floor((flat + 0.5) * (1.0 / HEADS))
    head = flat - bucket * HEADS
    real = rest < table_rows
    row = lax.broadcasted_iota(jnp.int32, (16, width), 0).astype(F32)
    return jnp.where(real, bucket, -1.0)[0:1], (real & (head == row)).astype(F32)


def inverse_rms(value):
    return lax.rsqrt(jnp.mean(value * value, axis=-1, keepdims=True) + EPSILON)


def norm_back(value, gain, grad):
    scale = inverse_rms(value)
    scaled = value * scale
    gained = grad * gain
    back = scale * (gained - scaled * jnp.mean(gained * scaled, axis=-1, keepdims=True))
    return back, jnp.sum(grad * scaled, axis=0, keepdims=True)


def gain_rows(side):
    pick = (
        lax.broadcasted_iota(jnp.int32, (16, EXT), 0)
        == lax.broadcasted_iota(jnp.int32, (16, EXT), 1)
    ).astype(BF)
    rows = dot_t(pick, side)
    return rows[0:1], rows[1:2], rows[2:3]


def gelu_parts(value):
    c = math.sqrt(2.0 / math.pi)
    square = value * value
    inner = jnp.tanh(c * (value + 0.044715 * square * value))
    grad = 0.5 * (1.0 + inner) + 0.5 * value * (1.0 - inner * inner) * (
        c + (3.0 * 0.044715 * c) * square
    )
    return 0.5 * value * (1.0 + inner), grad


def softmax_lanes(logits, experts):
    lane = lax.broadcasted_iota(jnp.int32, logits.shape, 1)
    valid = (lane >= LEAD) & (lane < LEAD + experts)
    logits = jnp.where(valid, logits, MASK_FILL)
    power = jnp.exp(logits - jnp.max(logits, axis=-1, keepdims=True))
    power = jnp.where(valid, power, 0.0)
    return power / jnp.sum(power, axis=-1, keepdims=True), lane


def pair_rows(value):
    low_lanes = lax.broadcasted_iota(jnp.int32, value.shape, 1) < HEAD_DIM
    zero = jnp.zeros_like(value)
    return jnp.concatenate(
        [jnp.where(low_lanes, value, zero), jnp.where(low_lanes, zero, value)], axis=0
    )


def pair_lanes(value):
    half = value.shape[0] // 2
    low_lanes = lax.broadcasted_iota(jnp.int32, (half, value.shape[1]), 1) < HEAD_DIM
    return jnp.where(low_lanes, value[:half], value[half:])


def attn_forward(layer, seq, width, experts, layout, count, shards, own_rows, table_rows, *refs):
    place, info = refs[:2]
    refs = refs[2:]
    pieces, refs = refs[:count], refs[count:]
    if layer == 0:
        (x_ref,), refs = refs[:1], refs[1:]
        n2_ref, refs = refs[0], refs[1:]
        extra = []
    else:
        (hid_ref,), toks, refs = refs[:1], refs[1:-16], refs[-16:]
        out_ref, n2_ref, tok_out = refs[:3]
        refs = refs[3:]
    acts_out, probs_out, floats_out, ext_out, held_out = refs[:5]
    held, sem, acts, probs_keep, floats, ext_keep, low_keep, out_sems = refs[5:]
    if layer == 0:
        low = x_ref[...]
    else:
        coming = pltpu.make_async_copy(hid_ref, floats, out_sems.at[0])
        coming.start()
        tok = sum(t[...].astype(F32) for t in toks).astype(BF)
        low_keep[...] = tok
        coming.wait()
        gate = floats[:, width + EXT : width + EXT + 1]
        low = (floats[:, :width] + gate * tok.astype(F32)).astype(BF)
        out_ref[...] = low
        extra = begin([pltpu.make_async_copy(low_keep, tok_out, out_sems.at[0])])
    acts[:, 6 * width :] = low
    x = low.astype(F32)
    scaled = x * inverse_rms(x)
    seg_row = info[0:1, :seq]
    same = as_column(seg_row) == seg_row
    route = as_column(info[1 + layer : 2 + layer, :seq])
    bucket = as_column(info[3:4, :]).astype(F32)
    bucket_row, head_sel = table_places(width, own_rows, table_rows)
    buckets = (bucket == bucket_row).astype(BF)
    if layout:
        join_weights(place, pieces, held, layout)
    else:
        held[place[0]] = pieces[0][...]
        held[1 - place[0]] = pieces[1][...]
    extra = extra + begin([pltpu.make_async_copy(held, held_out, sem)])
    side = held[0, :, 2 * width : 2 * width + EXT]
    ext_keep[...] = side
    extra = extra + begin([pltpu.make_async_copy(ext_keep, ext_out, out_sems.at[1])])
    gain_one, gain_two, table_row = gain_rows(side)
    table = dot_t((head_sel * table_row).astype(BF), buckets)
    normed = (scaled * gain_one).astype(BF)
    acts[:, :width] = normed
    acts[:, width : 3 * width] = dot(normed, held[0, :, : 2 * width]).astype(BF)
    acts[:, 3 * width : 4 * width] = dot(normed, held[1, :, :width]).astype(BF)
    scale = 1.0 / math.sqrt(HEAD_DIM)
    contexts = []
    for p in range(HEADS // 2):
        at = [(1 + i) * width + 128 * p for i in range(3)]
        q2 = pair_rows(acts[:, at[0] : at[0] + 128])
        scores = dot_t(q2, acts[:, at[1] : at[1] + 128]) * scale
        parts = []
        for h in (2 * p, 2 * p + 1):
            line = jnp.broadcast_to(table[h : h + 1], (seq, 2 * seq))
            bias = pltpu.roll(line, seq + 1, axis=1, stride=1, stride_axis=0)[:, :seq]
            part = scores[seq * (h - 2 * p) : seq * (h - 2 * p) + seq] + bias
            parts.append(jnp.where(same, part, MASK_FILL))
        scores = jnp.concatenate(parts, axis=0)
        power = jnp.exp(scores - jnp.max(scores, axis=-1, keepdims=True))
        probs = power / jnp.sum(power, axis=-1, keepdims=True)
        probs_keep[p] = probs
        contexts.append(pair_lanes(dot(probs.astype(BF), acts[:, at[2] : at[2] + 128])))
    extra = extra + begin([pltpu.make_async_copy(probs_keep, probs_out, out_sems.at[2])])
    context = jnp.concatenate(contexts, axis=1).astype(BF)
    acts[:, 4 * width : 5 * width] = context
    hidden = x + dot(context, held[1, :, width : 2 * width])
    floats[:, :width] = hidden
    normed_two = (hidden * inverse_rms(hidden) * gain_two).astype(BF)
    n2_ref[...] = normed_two
    acts[:, 5 * width : 6 * width] = normed_two
    extra = extra + begin([pltpu.make_async_copy(acts, acts_out, out_sems.at[3])])
    gates, lane = softmax_lanes(dot(normed_two, side), experts)
    floats[:, width : width + EXT] = gates
    value = jnp.sum(jnp.where(lane == route + LEAD, gates, 0.0), axis=-1, keepdims=True)
    floats[:, width + EXT :] = jnp.broadcast_to(value, gates.shape)
    finish(extra + begin([pltpu.make_async_copy(floats, floats_out, out_sems.at[4])]))


def pick_inputs(seq, *refs):
    place, own_feed, came_feed, segments, own_routes, came_routes, buckets = refs[:7]
    x_ref, dy_ref, info, sems = refs[7:]
    sec = place[0]
    for core in range(2):

        @pl.when(sec == core)
        def _(core=core):
            sources = (own_feed, came_feed) if core == 0 else (came_feed, own_feed)
            finish(
                begin(
                    [
                        pltpu.make_async_copy(sources[0].at[core], x_ref, sems.at[0]),
                        pltpu.make_async_copy(sources[1].at[core], dy_ref, sems.at[1]),
                    ]
                )
            )
            info[...] = jnp.full(info.shape, -2, jnp.int32)
            info[0:1, :seq] = segments[core : core + 1, :]
            info[1 + core : 2 + core, :seq] = own_routes[core : core + 1, :]
            info[2 - core : 3 - core, :seq] = came_routes[core : core + 1, :]
            info[3:4, : 2 * seq - 1] = buckets[...]


def routing_slots(shards, seq, experts, cap, *refs):
    place, infos, slots = refs[0], refs[1 : 1 + shards], refs[1 + shards]
    before = (
        lax.broadcasted_iota(jnp.int32, (seq, seq), 0)
        < lax.broadcasted_iota(jnp.int32, (seq, seq), 1)
    ).astype(BF)
    routes = jnp.concatenate(
        [info[1 + layer : 2 + layer, :seq] for layer in range(2) for info in infos], axis=0
    )
    rank = jnp.zeros(routes.shape, F32)
    for e in range(experts):
        mine = (routes == e).astype(F32)
        rank = rank + mine * dot(mine.astype(BF), before)
    slots[...] = (routes ^ place[1]) * cap + rank.astype(jnp.int32)


def slot_hot(slots, layer, shards, z, total):
    row = slots[layer * shards + z : layer * shards + z + 1, :]
    return (lax.broadcasted_iota(jnp.int32, (total, row.shape[1]), 0) == row).astype(BF)


def dispatch_rows(layer, count, shards, cap, *refs):
    slots = refs[0]
    toks = refs[1 : 1 + shards]
    blocks = refs[1 + shards :]
    for z in range(shards):
        rows = dot(slot_hot(slots, layer, shards, z, count * cap), toks[z][...]).astype(BF)
        for i in range(count):
            blocks[i][z * cap : (z + 1) * cap, :] = rows[i * cap : (i + 1) * cap]


def combine_rows(layer, count, shards, cap, *refs):
    slots = refs[0]
    blocks, refs = refs[1 : 1 + count], refs[1 + count :]
    more = (len(refs) - shards) // 2
    handed, toks, given = refs[:more], refs[more : more + shards], refs[more + shards :]
    for z in range(shards):
        rows = jnp.concatenate([b[z * cap : (z + 1) * cap, :] for b in blocks], axis=0)
        toks[z][...] = t_dot(slot_hot(slots, layer, shards, z, count * cap), rows).astype(BF)
    for source, target in zip(handed, given):
        target[...] = source[...]


def start_expert(layer, place, own, came, held, sems):
    def begin(pair):
        for i in range(2):
            pltpu.make_async_copy(pair[i], held.at[i], sems.at[i]).start()

    @pl.when(place[0] == layer)
    def _():
        begin(own)

    @pl.when(place[0] != layer)
    def _():
        begin(came)

    return [pltpu.make_async_copy(own[i], held.at[i], sems.at[i]) for i in range(2)]


def expert_forward(layer, count, *refs):
    place, own, came = refs[0], refs[1:3], refs[3:5]
    blocks = refs[5 : 5 + count]
    results, rows_out = refs[5 + count : 5 + 2 * count], refs[5 + 2 * count]
    held, sems, rows, out_sem = refs[6 + 2 * count :]
    copies = start_expert(layer, place, own, came, held, sems)
    each = blocks[0].shape[0]
    for i in range(count):
        rows[i * each : (i + 1) * each, :] = blocks[i][...]
    leaving = begin([pltpu.make_async_copy(rows, rows_out, out_sem)])
    finish(copies)
    for i in range(count):
        activated = gelu_parts(dot(blocks[i][...], held[0]))[0].astype(BF)
        results[i][...] = dot(activated, held[1]).astype(BF)
    finish(leaving)


def expert_backward(layer, count, experts, with_out, *refs):
    place, own, came, ext_in = refs[0], refs[1:3], refs[3:5], refs[5]
    if with_out:
        blocks, dy_in, refs = refs[6 : 6 + count], refs[6 + count : 6 + 2 * count], refs[6 + 2 * count :]
    else:
        rows_in, dys, refs = refs[6], refs[7 : 7 + count], refs[7 + count :]
    grads, refs = refs[:count], refs[count:]
    if with_out:
        results, refs = refs[:count], refs[count:]
    keep_out, held, sems, keep, ext, late, more_sems = refs
    copies = start_expert(layer, place, own, came, held, sems)
    each = grads[0].shape[0]
    loads = [pltpu.make_async_copy(ext_in, ext, more_sems.at[0])]
    if with_out:
        loads += [
            pltpu.make_async_copy(dy_in[i], late.at[pl.ds(i * each, each), :], more_sems.at[1 + i])
            for i in range(count)
        ]
    else:
        loads += [pltpu.make_async_copy(rows_in, late, more_sems.at[1])]
    begin(loads)
    finish(loads + copies)
    leaving = []
    for i in range(count):
        at = slice(i * each, (i + 1) * each)
        if with_out:
            rows, dy = blocks[i][...], late[at, :]
        else:
            rows, dy = late[at, :], dys[i][...]
        dy = dy.astype(F32)
        gates, lane = softmax_lanes(dot(rows, ext[...]), experts)
        mine = (lane == place[1] + LEAD).astype(F32)
        value = jnp.sum(gates * mine, axis=-1, keepdims=True)
        grad_expert = (value * dy).astype(BF)
        act, slope = gelu_parts(dot(rows, held[0]))
        act = act.astype(BF)
        grad_pre = (dot_t(grad_expert, held[1]) * slope).astype(BF)
        grad = dot_t(grad_pre, held[0])
        if with_out:
            result = dot(act, held[1])
            results[i][...] = result.astype(BF)
            grad_gate = jnp.sum(dy * result, axis=-1, keepdims=True)
            grad_logits = (grad_gate * value * (mine - gates)).astype(BF)
            grad = grad + dot_t(grad_logits, ext[...])
        grads[i][...] = grad.astype(BF)
        keep[0, at, :] = rows
        keep[1, at, :] = grad_pre
        keep[2, at, :] = act
        keep[3, at, :] = grad_expert
        leaving += begin(
            [
                pltpu.make_async_copy(
                    keep.at[:, pl.ds(i * each, each), :],
                    keep_out.at[:, pl.ds(i * each, each), :],
                    more_sems.at[1 + count + i],
                )
            ]
        )
    finish(leaving)


def attn_backward(layer, seq, width, experts, shards, own_rows, table_rows, *refs):
    place, info, held_in = refs[:3]
    refs = refs[3:]
    dy_ref, acts_in, probs_in, floats_in = refs[:4]
    refs = refs[4:]
    if layer == 0:
        tok_in, refs = refs[0], refs[1:]
    parts, refs = refs[:shards], refs[shards:]
    dx_ref, ship, stay, side_grad = refs[:4]
    ship_all, ship = ship, ship.at[pl.ds(0, seq), :]
    held, sem, acts, probs_all, floats, tok_keep, gj, g_rel, in_sems = refs[4:]
    loads = [
        pltpu.make_async_copy(floats_in, floats, in_sems.at[0]),
        pltpu.make_async_copy(acts_in, acts, in_sems.at[1]),
        pltpu.make_async_copy(probs_in, probs_all, in_sems.at[2]),
    ]
    if layer == 0:
        loads.append(pltpu.make_async_copy(tok_in, tok_keep, in_sems.at[3]))
    begin(loads)
    copies = begin([pltpu.make_async_copy(held_in, held, sem)])
    dy = dy_ref[...].astype(F32)
    grad_norm_two = sum(p[...].astype(F32) for p in parts)
    route = as_column(info[1 + layer : 2 + layer, :seq])
    bucket = as_column(info[3:4, :], 2 * seq - 2).astype(F32)
    bucket_row, head_sel = table_places(width, own_rows, table_rows)
    buckets = (bucket == bucket_row).astype(BF)
    finish(loads)
    hidden = floats[:, :width]
    x = acts[:, 6 * width :].astype(F32)
    state = acts
    finish(copies)
    side = held[0, :, 2 * width : 2 * width + EXT]
    gain_one, gain_two, _ = gain_rows(side)
    side_grad[...] = jnp.zeros_like(side_grad)
    if layer == 0:
        gates = floats[:, width : width + EXT]
        lane = lax.broadcasted_iota(jnp.int32, gates.shape, 1)
        hot = (lane == route + LEAD).astype(F32)
        grad_gate = jnp.sum(dy * tok_keep[...].astype(F32), axis=-1, keepdims=True)
        value = floats[:, width + EXT : width + EXT + 1]
        grad_logits = (grad_gate * value * (hot - gates)).astype(BF)
        grad_norm_two = grad_norm_two + dot_t(grad_logits, side)
        router_rows = t_dot(grad_logits, acts[:, 5 * width : 6 * width])
        side_grad[...] = router_rows[: side_grad.shape[0]]
    back, gain_two_grad = norm_back(hidden, gain_two, grad_norm_two)
    grad_hidden = dy + back
    grad_hidden_low = grad_hidden.astype(BF)
    grad_context = dot_t(grad_hidden_low, held[1, :, width : 2 * width]).astype(BF)
    scale = 1.0 / math.sqrt(HEAD_DIM)
    mirror = (
        lax.broadcasted_iota(jnp.int32, (seq, 2 * seq), 0)
        + lax.broadcasted_iota(jnp.int32, (seq, 2 * seq), 1)
        == seq - 1
    ).astype(BF)
    for p in range(HEADS // 2):
        lanes = slice(128 * p, 128 * p + 128)
        q2 = pair_rows(state[:, width + 128 * p : width + 128 * p + 128])
        keys = state[:, 2 * width + 128 * p : 2 * width + 128 * p + 128]
        vals = state[:, 3 * width + 128 * p : 3 * width + 128 * p + 128]
        g2 = pair_rows(grad_context[:, lanes])
        probs = probs_all[p]
        grad_probs = dot_t(g2, vals)
        grad_scores = probs * (
            grad_probs - jnp.sum(probs * grad_probs, axis=-1, keepdims=True)
        )
        grad_scores = grad_scores.astype(BF)
        gj[:, lanes] = (pair_lanes(dot(grad_scores, keys)) * scale).astype(BF)
        gj[:, width + 128 * p : width + 128 * p + 128] = (t_dot(grad_scores, q2) * scale).astype(BF)
        gj[:, 2 * width + 128 * p : 2 * width + 128 * p + 128] = t_dot(
            probs.astype(BF), g2
        ).astype(BF)
        turned = dot(grad_scores, mirror)
        for h in range(2):
            shifted = pltpu.roll(turned[h * seq : (h + 1) * seq], 0, axis=1, stride=1, stride_axis=0)
            g_rel[2 * p + h : 2 * p + h + 1, :] = jnp.sum(shifted, axis=0, keepdims=True)
    g_rel[HEADS:, :] = jnp.zeros_like(g_rel[HEADS:, :])
    offsets = g_rel[...]
    high = offsets.astype(BF)
    low = (offsets - high.astype(F32)).astype(BF)
    by_row = dot(high, buckets) + dot(low, buckets)
    side_grad[2:3, :] = jnp.sum(by_row * head_sel, axis=0, keepdims=True)
    side_grad[1:2, :] = gain_two_grad
    grad_normed = dot_t(gj[:, : 2 * width], held[0, :, : 2 * width]) + dot_t(
        gj[:, 2 * width :], held[1, :, :width]
    )
    back, gain_one_grad = norm_back(x, gain_one, grad_normed)
    side_grad[0:1, :] = gain_one_grad
    dx_ref[...] = (grad_hidden + back).astype(BF)
    normed = state[:, :width]
    halves = (ship, stay)
    for core in range(2):

        @pl.when(place[0] == core)
        def _(core=core):
            halves[1 - core][:, :width] = normed
            halves[1 - core][:, width : 3 * width] = gj[:, : 2 * width]
            halves[1 - core][:, 3 * width :] = jnp.zeros_like(normed)
            halves[core][:, :width] = normed
            halves[core][:, width : 2 * width] = gj[:, 2 * width :]
            halves[core][:, 2 * width : 3 * width] = state[:, 4 * width : 5 * width]
            halves[core][:, 3 * width :] = grad_hidden_low

    ship_all[seq:, :width] = side_grad[...].astype(BF)
    ship_all[seq:, width:] = jnp.zeros_like(ship_all[seq:, width:])


def last_output(seq, width, experts, shards, *refs):
    info, dy_ref, acts_in, floats_in, side_in = refs[:5]
    parts, refs = refs[5 : 5 + shards], refs[5 + shards :]
    out_ref, side_grad, normed, floats, sems = refs
    loads = begin(
        [
            pltpu.make_async_copy(floats_in, floats, sems.at[0]),
            pltpu.make_async_copy(acts_in.at[:, pl.ds(5 * width, width)], normed, sems.at[1]),
        ]
    )
    tok = sum(p[...].astype(F32) for p in parts).astype(BF).astype(F32)
    finish(loads)
    value = floats[:, width + EXT : width + EXT + 1]
    out_ref[...] = (floats[:, :width] + value * tok).astype(BF)
    gates = floats[:, width : width + EXT]
    lane = lax.broadcasted_iota(jnp.int32, gates.shape, 1)
    hot = (lane == as_column(info[2:3, :seq]) + LEAD).astype(F32)
    grad_gate = jnp.sum(dy_ref[...].astype(F32) * tok, axis=-1, keepdims=True)
    grad_logits = (grad_gate * value * (hot - gates)).astype(BF)
    side_grad[...] = side_in[...] + t_dot(grad_logits, normed[...])[: side_grad.shape[0]]


def attn_weights(width, count, parts, more, relay, *refs):
    place, stay, came = refs[:3]
    total = refs[-1]
    handed, sides, outs = refs[3 : 3 + more], refs[3 + more : -1 - count - more], refs[-1 - count - more : -1]
    blocks, given = outs[:count], outs[count:]
    for source, target in zip(handed, given):
        target[...] = source[...]

    seq = stay.shape[0]

    def both(first, last):
        return jnp.concatenate([stay[:, first:last], came[:seq, first:last]], axis=0)

    unit = width // 2
    for i, part in enumerate(parts):
        at = slice(i * unit, (i + 1) * unit)

        @pl.when(place[0] == 0)
        def _(part=part, at=at):
            total[:, at] = t_dot(
                both(0, width), both(width + part * unit, width + (part + 1) * unit)
            ).astype(BF)

        @pl.when(place[0] != 0)
        def _(part=part, at=at):
            left = part // 2 * 2 * width
            right = left + width + part % 2 * unit
            total[:, at] = t_dot(both(left, left + width), both(right, right + unit)).astype(BF)

    if sides:
        block = jnp.zeros((width, EXT), F32)
        ours = (sides[0][...] + came[seq:, :width].astype(F32), sides[1][...] + sides[2][...])
        for layer, rows in enumerate(ours):
            pick = (
                lax.broadcasted_iota(jnp.int32, (rows.shape[0], EXT), 0) + layer * (EXT // 2)
                == lax.broadcasted_iota(jnp.int32, (rows.shape[0], EXT), 1)
            ).astype(BF)
            block = block + t_dot(rows.astype(BF), pick)
        total[:, len(parts) * unit :] = block.astype(BF)

    if relay:
        rows = blocks[0].shape[0] // 2
        cut = blocks[0].shape[1]
        columns = (slice(0, cut), slice(cut, total.shape[1]))
        for block, ids, at in zip(blocks, ((1, 3), (0, 2), (2, 3), (0, 1)), (0, 0, 1, 1)):
            for i, peer in enumerate(ids):
                first = pl.multiple_of(place[2 + peer] * rows, rows)
                block[i * rows : (i + 1) * rows, :] = total[pl.ds(first, rows), columns[at]]
        return
    rows = blocks[0].shape[0]
    for i in range(count):
        first = pl.multiple_of(place[2 + i] * rows, rows) if count > 1 else 0
        blocks[i][...] = total[pl.ds(first, rows), :]


def halve_sums(*refs):
    came_x, kept_x, came_y, kept_y, own_x, on_x, own_y, on_y = refs
    for came, kept, own, on in ((came_x, kept_x, own_x, on_x), (came_y, kept_y, own_y, on_y)):
        rows = own.shape[0]
        own[...] = came[:rows].astype(F32) + kept[:rows].astype(F32)
        on[...] = (came[rows:].astype(F32) + kept[rows:].astype(F32)).astype(BF)


def join_sums(at, *refs):
    place, own_x, came_x, own_y, came_y = refs[:5]
    blocks, total = refs[5:-1], refs[-1]
    cut = own_x.shape[1]
    total[:, :cut] = own_x[...] + came_x[...].astype(F32)
    total[:, cut:] = own_y[...] + came_y[...].astype(F32)
    rows = blocks[0].shape[0]
    for i, block in enumerate(blocks):
        first = pl.multiple_of(place[at + i] * rows, rows)
        block[...] = total[pl.ds(first, rows), :].astype(block.dtype)


def last_swap(width, *refs):
    place, zero, one, send = refs

    @pl.when(place[0] == 0)
    def _():
        send[:, : 2 * width] = one[...]
        send[:, 2 * width :] = zero[:, 2 * width :]

    @pl.when(place[0] != 0)
    def _():
        send[...] = zero[...]


def last_grads(width, experts, *refs):
    place, zero, one, came = refs[:4]
    query, key, value, out_proj, gain_a, gain_f, table, router = refs[4:]

    def put_side(side):
        n = side.shape[0]
        across = lax.broadcasted_iota(jnp.int32, (n, n), 1)
        down = lax.broadcasted_iota(jnp.int32, (n, n), 0)

        def turned(i):
            return jnp.sum(
                jnp.where(across == down, side[:, i : i + 1], 0.0), axis=0, keepdims=True
            )

        for i, target in enumerate((gain_a, gain_f, table)):
            target[...] = turned(i)[:, : target.shape[1]]
        for e in range(experts):
            router[e : e + 1, :] = turned(LEAD + e)

    @pl.when(place[0] == 0)
    def _():
        query[...] = zero[:, :width]
        key[...] = zero[:, width : 2 * width]
        value[...] = came[:, :width]
        out_proj[...] = came[:, width : 2 * width]
        put_side(zero[:, 2 * width : 2 * width + EXT // 2])

    @pl.when(place[0] != 0)
    def _():
        query[...] = came[:, :width]
        key[...] = came[:, width : 2 * width]
        value[...] = one[:, :width]
        out_proj[...] = one[:, width:]
        put_side(came[:, 2 * width + EXT // 2 :])


def sum_blocks(count, at, *refs):
    place, parts = refs[0], refs[1 : 1 + count]
    blocks, total = refs[1 + count : -1], refs[-1]
    total[...] = sum(p[...].astype(F32) for p in parts)
    rows = blocks[0].shape[0]
    for i, block in enumerate(blocks):
        first = pl.multiple_of(place[at + i] * rows, rows) if len(blocks) > 1 else 0
        block[...] = total[pl.ds(first, rows), :].astype(block.dtype)


def join_rows(count, first_id, *refs):
    place, parts, whole = refs[0], refs[1 : 1 + count], refs[1 + count]
    rows = parts[0].shape[0]
    for i in range(count):
        at = pl.multiple_of(place[first_id + i] * rows, rows)
        whole[pl.ds(at, rows), :] = parts[i][...]


def pick_later(*refs):
    place, kept, came, later = refs

    @pl.when(place[0] == 0)
    def _():
        later[...] = came[...]

    @pl.when(place[0] != 0)
    def _():
        later[...] = kept[...]


def join_planes(layout, *refs):
    place, pieces, whole = refs[0], refs[1:-1], refs[-1]
    plane = pieces[0].shape[0]
    for (peer, first), piece in zip(layout, pieces):
        at = pl.multiple_of(place[2 + peer] * plane + first, piece.shape[0])
        whole[pl.ds(at, piece.shape[0]), :] = piece[...]


def pack_weights(width, experts, table_rows, *refs):
    place, query, key, value, out_proj, gain_a, gain_f, table, router = refs[:9]
    send, keep, row_a, row_f, row_t, rows_r, sems = refs[9:]
    own_rows = row_a.shape[1]
    small = begin(
        [
            pltpu.make_async_copy(source, target, sems.at[4 + i])
            for i, (source, target) in enumerate(
                ((gain_a, row_a), (gain_f, row_f), (table, row_t), (router, rows_r))
            )
        ]
    )
    halves = (keep, send)
    for core in range(2):

        @pl.when(place[0] == core)
        def _(core=core):
            begin(
                [
                    pltpu.make_async_copy(
                        source,
                        halves[(core + i // 2) % 2].at[:, pl.ds(i % 2 * width, width)],
                        sems.at[i],
                    )
                    for i, source in enumerate((query, key, value, out_proj))
                ]
            )

    finish(small)
    columns = [as_column(row_a[...].astype(F32)), as_column(row_f[...].astype(F32))]
    line = row_t[...].astype(F32)
    down = lax.broadcasted_iota(jnp.int32, (own_rows, table_rows), 0)
    across = lax.broadcasted_iota(jnp.int32, (own_rows, table_rows), 1)
    columns.append(jnp.sum(jnp.where(down == across, line, 0.0), axis=1, keepdims=True))
    lines = rows_r[...].astype(F32)
    columns += [as_column(lines[e : e + 1]) for e in range(experts)]
    lane = lax.broadcasted_iota(jnp.int32, (own_rows, EXT), 1)
    block = jnp.zeros((own_rows, EXT), F32)
    for i, column in enumerate(columns):
        block = jnp.where(lane == i, column, block)
    keep[:, 2 * width :] = block.astype(BF)
    send[:, 2 * width :] = block.astype(BF)
    finish(
        [
            pltpu.make_async_copy(source, keep.at[:, pl.ds(0, width)], sems.at[i])
            for i, source in enumerate((query, key, value, out_proj))
        ]
    )


def expert_weights(other, *refs):
    place, keeps, refs = refs[0], refs[1:3], refs[3:]
    if other:
        in_ref, out_ref, held, sem = refs
    else:
        came_in, came_out, in_ref, out_ref, held, sem = refs
    for layer in range(2):

        @pl.when((place[0] == layer) != other)
        def _(layer=layer):
            pltpu.make_async_copy(keeps[layer], held, sem).start()

    pltpu.make_async_copy(keeps[0], held, sem).wait()
    grad_in = t_dot(held[0], held[1])
    grad_out = t_dot(held[2], held[3])
    if not other:
        grad_in = grad_in + came_in[...].astype(F32)
        grad_out = grad_out + came_out[...].astype(F32)
    in_ref[...] = grad_in.astype(in_ref.dtype)
    out_ref[...] = grad_out.astype(out_ref.dtype)


def body(
    feed, segments, routes, rel_bucket, gain_attn, gain_ffn, w_query, w_key, w_value, w_out_attn,
    rel_table, router, expert_in, expert_out,
):
    seq = feed.shape[2]
    width = feed.shape[3]
    experts = lax.axis_size("expert")
    shards = lax.axis_size("shard")
    cap = max(2, 2 * seq // experts)
    own_rows = w_query.shape[1]
    table_rows = rel_table.shape[1]
    quick = direct("expert") and direct("shard")
    blocks_count = experts if quick else 1
    wide = 2 * width + EXT
    side_rows = -(-(LEAD + experts) // 16) * 16
    sec = lax.axis_index("section")
    first = sec == 0
    place = jnp.concatenate(
        [
            jnp.stack([sec, lax.axis_index("expert")]).astype(jnp.int32),
            peer_ids("expert"),
            peer_ids("shard"),
        ]
    )
    row = out((seq, width))
    sems = pltpu.SemaphoreType.DMA

    small = [gain_attn, gain_ffn, rel_table, router[0].T]
    send, kept = call(
        functools.partial(pack_weights, width, experts, table_rows),
        [out((own_rows, wide))] * 2,
        [place, w_query[0], w_key[0], w_value[0], w_out_attn[0], *small],
        [SM] + [HB] * 8,
        [pltpu.VMEM(one.shape, BF) for one in small] + [sems((8,))],
        limit=60,
    )
    came = swap(send)
    part_zero = jnp.where(first, kept, came)

    own_experts = [expert_in[0, 0], expert_out[0, 0]]
    came_experts = [swap(expert_in[0, 0]), swap(expert_out[0, 0])]

    feed_own = feed[0]
    routes_own = routes[0, :, 0]
    layer_x, layer_dy, info = call(
        functools.partial(pick_inputs, seq),
        [row, row, out((8, 2 * seq), jnp.int32)],
        [
            place, feed_own, swap(feed_own), segments[:, 0], routes_own, swap(routes_own),
            rel_bucket[None, :],
        ],
        [SM, HB, AN] + [VM] * 4,
        [sems((2,))],
        after=came_experts,
    )

    infos = spread(info, "shard")


    def both_halves(mine):
        return mine + [swap(piece) for piece in mine]

    def plane_of(part, after=()):
        return call(
            functools.partial(join_rows, shards, 2 + experts),
            [out((shards * own_rows, wide))],
            [place, *spread(part, "shard")],
            [SM] + [VM] * shards,
            after=after,
        )[0]

    half = shards * own_rows // 2
    relay = experts == 4 and half % 16 == 0

    def planes_of(plane):
        if not relay:
            return spread(plane, "expert")
        beside = [hop(plane, "expert", 1), hop(plane, "expert", 2)]
        across = [hop(beside[1][:half], "expert", 1), hop(beside[0][half:], "expert", 2)]
        return [plane, *beside, *across]

    peers = [(i, 0) for i in range(experts)]
    if relay:
        peers = peers + [(experts - 1, half)]
    if quick:
        planes = planes_of(plane_of(part_zero, after=[info]))
        weights_zero = both_halves(planes)
        joined_after = planes[1:3]
        layouts = [peers, ()]
        (part_one,) = call(
            pick_later,
            [out((own_rows, wide))],
            [place, kept, came],
            [SM, VM, VM],
        )
        planes_one = planes_of(plane_of(part_one, after=joined_after))
    else:
        part_one = jnp.where(first, came, kept)
        weights_zero, weights_one = [
            both_halves([lax.all_gather(part, ("expert", "shard"), axis=0, tiled=True)])
            for part in (part_zero, part_one)
        ]
        joined_after = ()
        layouts = [(), ()]


    if quick:
        (slots,) = call(
            functools.partial(routing_slots, shards, seq, experts, cap),
            [out((2 * shards, seq), jnp.int32)],
            [place, *infos],
            [SM] + [VM] * shards,
            after=joined_after,
        )
    else:
        all_routes = jnp.stack([one[1:3, :seq] for one in infos], axis=1)
        hot = (all_routes[..., None] == peer_ids("expert")).astype(BF)
        positions = jnp.arange(seq, dtype=jnp.int32)
        before = (positions[:, None] > positions[None, :]).astype(BF)
        rank = jnp.einsum("ij,lzje->lzie", before, hot, preferred_element_type=F32)
        slot_in = jnp.arange(cap, dtype=jnp.int32).astype(F32)
        back_hot = (hot[..., None] * (rank[..., None] == slot_in).astype(BF)).reshape(
            2, shards, seq, experts * cap
        )
        to_hot = jnp.swapaxes(back_hot, 2, 3)

    block = out((shards * cap * experts // blocks_count, width))
    acts_kind = out((seq, 7 * width))
    probs_kind = out((HEADS // 2, 2 * seq, seq), F32)
    floats_kind = out((seq, width + 2 * EXT), F32)

    def buffer(kind):
        return pltpu.VMEM(kind.shape, kind.dtype)

    expert_scratch = [pltpu.VMEM((2, expert_in.shape[2], expert_in.shape[3]), BF), sems((2,))]
    expert_specs = [SM] + [AN] * 4

    def to_experts(layer, tokens, after=()):
        every = spread(tokens, "shard")
        if not quick:
            slot_rows = jnp.einsum(
                "zcs,zsd->czd", to_hot[layer], jnp.stack(every), preferred_element_type=F32
            )
            slot_rows = slot_rows.astype(BF).reshape(experts, cap * shards, width)
            moved = exchange([slot_rows[i] for i in range(experts)], "expert")
            return [jnp.concatenate(moved, axis=0)]
        blocks = call(
            functools.partial(dispatch_rows, layer, experts, shards, cap),
            [block] * experts,
            [slots, *every],
            [VM] * (1 + shards),
            after=after,
        )
        return exchange(blocks, "expert")

    def to_tokens(layer, blocks, later=(), after=()):
        if not quick:
            rows = blocks[0].reshape(experts, cap * shards, width)
            back = jnp.stack(exchange([rows[i] for i in range(experts)], "expert"))
            back = back.reshape(experts * cap, shards, width)
            tokens = jnp.einsum(
                "zsc,czd->zsd", back_hot[layer], back, preferred_element_type=F32
            ).astype(BF)
            return exchange([tokens[i] for i in range(shards)], "shard"), list(later)
        back = exchange(blocks, "expert")
        results = call(
            functools.partial(combine_rows, layer, experts, shards, cap),
            [row] * shards + [out(one.shape, one.dtype) for one in later],
            [slots, *back, *later],
            [VM] * (1 + experts + len(later)),
            after=after,
        )
        return exchange(results[:shards], "shard"), results[shards:]

    held_kind = out((2, width, wide))

    def attention(layer, pieces, ins, in_specs, after=()):
        count = len(pieces)
        first_outs = [row, row, row] if layer else [row]
        return call(
            functools.partial(
                attn_forward, layer, seq, width, experts, layouts[layer], count, shards, own_rows,
                table_rows,
            ),
            first_outs + [acts_kind, probs_kind, floats_kind, out((width, EXT)), held_kind],
            [place, info, *pieces, *ins],
            [SM, VM] + [VM] * count + in_specs,
            [
                buffer(held_kind), sems(()), buffer(acts_kind),
                buffer(probs_kind), buffer(floats_kind), pltpu.VMEM((width, EXT), BF), buffer(row),
                sems((5,)),
            ],
            out_specs=([VM, VM, HB] if layer else [VM]) + [HB] * 5,
            after=after,
        )

    def attention_back(layer, dy, state, tok, parts, after=()):
        acts, probs, floats, _, held = state
        return call(
            functools.partial(
                attn_backward, layer, seq, width, experts, shards, own_rows, table_rows,
            ),
            [
                row,
                out((seq + side_rows, 4 * width)),
                out((seq, 4 * width)),
                out((side_rows, width), F32),
            ],
            [place, info, held, dy, acts, probs, floats, *tok, *parts],
            [SM, VM, HB, VM] + [HB] * (3 + len(tok)) + [VM] * shards,
            [
                buffer(held_kind), sems(()), buffer(acts_kind),
                buffer(probs_kind), buffer(floats_kind), buffer(row),
                pltpu.VMEM((seq, 3 * width), BF), pltpu.VMEM((16, 2 * seq), F32), sems((4,)),
            ],
            after=after,
        )

    keep_kind = out((4, shards * cap * experts, width))

    def back_expert(layer, rows, dys, ext_side, with_out):
        results = call(
            functools.partial(expert_backward, layer, blocks_count, experts, with_out),
            [block] * (blocks_count * (2 if with_out else 1)) + [keep_kind],
            [place, *own_experts, *came_experts, ext_side, *rows, *dys],
            expert_specs + [HB]
            + ([VM] * blocks_count + [AN] * blocks_count if with_out else [HB] + [VM] * blocks_count),
            expert_scratch + [
                buffer(keep_kind), pltpu.VMEM((width, EXT), BF),
                pltpu.VMEM(keep_kind.shape[1:], BF), sems((1 + 2 * blocks_count,)),
            ],
            out_specs=[VM] * (blocks_count * (2 if with_out else 1)) + [HB],
        )
        return results[:blocks_count], results[blocks_count:-1], results[-1]

    row_parts = experts if quick else 1
    relay = quick and relay

    def cut_of(columns):
        return -(-columns // (2 * EXT)) * EXT

    def weight_blocks(stay, came, parts, sides=(), after=(), later=()):
        columns = len(parts) * (width // 2) + (EXT if sides else 0)
        return call(
            functools.partial(attn_weights, width, row_parts, parts, len(later), relay),
            (
                [out((width // 2, cut_of(columns)))] * 2
                + [out((width // 2, columns - cut_of(columns)))] * 2
                if relay
                else [out((width // row_parts, columns))] * row_parts
            )
            + [out(one.shape, one.dtype) for one in later],
            [place, stay, came, *later, *sides],
            [SM] + [VM] * (2 + len(sides) + len(later)),
            [pltpu.VMEM((width, columns), BF)],
            after=after,
        )

    def sum_planes(blocks, after=()):
        if not quick:
            return blocks
        if relay:
            send_x, kept_x, send_y, kept_y = blocks
            rows, cut, rest = width // 4, kept_x.shape[1], kept_y.shape[1]
            own_x, on_x, own_y, on_y = call(
                halve_sums,
                [out((rows, cut), F32), out((rows, cut)), out((rows, rest), F32), out((rows, rest))],
                [hop(send_x, "expert", 1), kept_x, hop(send_y, "expert", 2), kept_y],
                [VM] * 4,
            )
            return call(
                functools.partial(join_sums, 2 + experts),
                [out((own_rows, cut + rest))] * shards,
                [place, own_x, hop(on_x, "expert", 2), own_y, hop(on_y, "expert", 1)],
                [SM] + [VM] * 4,
                [pltpu.VMEM((rows, cut + rest), F32)],
                after=after,
            )
        columns = blocks[0].shape[1]
        return call(
            functools.partial(sum_blocks, experts, 2 + experts),
            [out((own_rows, columns))] * shards,
            [place, *exchange(blocks, "expert")],
            [SM] + [VM] * experts,
            [pltpu.VMEM((shards * own_rows, columns), F32)],
            after=after,
        )

    def sum_rows(blocks):
        if not quick:
            return scatter_rows(blocks[0])
        columns = blocks[0].shape[1]
        (total,) = call(
            functools.partial(sum_blocks, shards, 0),
            [out((own_rows, columns), F32)],
            [place, *exchange(blocks, "shard")],
            [SM] + [VM] * shards,
            [pltpu.VMEM((own_rows, columns), F32)],
        )
        return total

    n2_zero, *state_zero = attention(
        0, weights_zero, [layer_x], [VM], after=[slots] if quick else ()
    )
    rows_zero = to_experts(0, n2_zero)
    *results, rows_zero = call(
        functools.partial(expert_forward, 0, blocks_count),
        [block] * blocks_count + [out(keep_kind.shape[1:])],
        [place, *own_experts, *came_experts, *rows_zero],
        expert_specs + [VM] * blocks_count,
        expert_scratch + [pltpu.VMEM(keep_kind.shape[1:], BF), sems(())],
        out_specs=[VM] * blocks_count + [HB],
        after=planes_one[1:] if quick else (),
    )
    toks, _ = to_tokens(0, results)
    if quick:
        (gathered,) = call(
            functools.partial(join_planes, peers),
            [out((width, wide))],
            [place, *planes_one],
            [SM] + [VM] * len(planes_one),
            after=results[:1],
        )
        weights_one = both_halves([gathered])
    out_zero, n2_one, tok_zero, *state_one = attention(
        1, weights_one, [state_zero[2], *toks], [HB] + [VM] * shards
    )
    dys_one = to_experts(1, layer_dy)
    rows_one = to_experts(1, n2_one)
    grads, results, keep_one = back_expert(1, rows_one, dys_one, state_one[3], True)
    parts_one, results = to_tokens(1, grads, results)
    toks_one, _ = to_tokens(1, results)
    dx_one, ship_one, stay_one, side_one = attention_back(
        1, layer_dy, state_one, [], parts_one, after=toks_one[:1]
    )
    came_one = swap(ship_one)
    dys_zero = to_experts(0, dx_one)
    out_one, side_one = call(
        functools.partial(last_output, seq, width, experts, shards),
        [row, out((side_rows, width), F32)],
        [info, layer_dy, state_one[0], state_one[2], side_one, *toks_one],
        [VM, VM, HB, HB, VM] + [VM] * shards,
        [buffer(row), buffer(floats_kind), sems((2,))],
    )
    side_one_came = swap(side_one)
    grads, _, keep_zero = back_expert(0, [rows_zero], dys_zero, state_zero[3], False)
    matrix = (expert_in.shape[2], expert_in.shape[3])
    keep_scratch = [pltpu.VMEM(keep_one.shape, BF), sems(())]
    sent = call(
        functools.partial(expert_weights, True),
        [out(matrix)] * 2,
        [place, keep_zero, keep_one],
        [SM, HB, HB],
        keep_scratch,
    )
    came_grads = [swap(grad) for grad in sent]
    parts_zero, _ = to_tokens(0, grads, after=[side_one_came])
    blocks_one = weight_blocks(stay_one, came_one, (0, 1, 2, 3), after=parts_zero[:1])
    dx_zero, ship_zero, stay_zero, side_zero = attention_back(
        0, dx_one, state_zero, [tok_zero], parts_zero, after=[blocks_one[0], sent[0]]
    )
    planes_one_sum = sum_planes(blocks_one)
    came_zero = swap(ship_zero)
    blocks_zero = weight_blocks(
        stay_zero, came_zero, (0, 1, 2, 3), (side_zero, side_one, side_one_came),
        after=planes_one_sum[:1],
    )
    sum_one = sum_rows(planes_one_sum)
    own_grads = call(
        functools.partial(expert_weights, False),
        [out(matrix, F32)] * 2,
        [place, keep_zero, keep_one, *came_grads],
        [SM, HB, HB, VM, VM],
        keep_scratch,
        after=blocks_zero[:1],
    )
    sum_zero = sum_rows(sum_planes(blocks_zero, after=own_grads[:1]))
    (send,) = call(
        functools.partial(last_swap, width),
        [out((own_rows, wide), F32)],
        [place, sum_zero, sum_one],
        [SM] + [VM] * 2,
    )
    matrix_kind = out((own_rows, width), F32)
    weight_grads = call(
        functools.partial(last_grads, width, experts),
        [matrix_kind] * 4
        + [out((1, own_rows), F32)] * 2
        + [out((1, table_rows), F32), out((experts, own_rows), F32)],
        [place, sum_zero, sum_one, swap(send)],
        [SM] + [VM] * 3,
    )

    def by_batch(zero, one):
        came = swap(jnp.where(first, one, zero))
        kept = jnp.where(first, zero, one)
        return jnp.stack([jnp.where(first, kept, came), jnp.where(first, came, kept)])

    grad_query, grad_key, grad_value, grad_out, grad_a, grad_f, grad_table, grad_router = weight_grads
    return (
        by_batch(out_zero, out_one)[None],
        by_batch(dx_zero, dx_one)[None],
        grad_a,
        grad_f,
        grad_query[None],
        grad_key[None],
        grad_value[None],
        grad_out[None],
        grad_table,
        grad_router.T[None],
        own_grads[0][None, None],
        own_grads[1][None, None],
    )


def solution(mesh):
    rows = ("expert", "shard")
    tokens = P("section", None, rows, None)
    matrix = P("section", rows, None)
    vector = P("section", rows)
    expert_specs = (P("section", "expert", None, "shard"), P("section", "expert", "shard", None))
    in_specs = (
        tokens, P(None, rows, None), tokens, P(), vector, vector, matrix, matrix, matrix, matrix,
        vector, matrix, *expert_specs,
    )
    out_specs = (
        tokens, tokens, vector, vector, matrix, matrix, matrix, matrix, vector, matrix,
        *expert_specs,
    )
    return jax.shard_map(body, mesh=mesh, in_specs=in_specs, out_specs=out_specs, check_vma=False)
```

```python
import functools
import math

import jax
import jax.numpy as jnp
import numpy as np
from jax import lax
from jax.experimental import pallas as pl
from jax.experimental.pallas import tpu as pltpu
from jax.sharding import PartitionSpec as P

HEADS = 12
HEAD_DIM = 64
NB = 32
EXT = 128
LEAD = 3
EPSILON = 1e-06
MASK_FILL = -1e30
BF = jnp.bfloat16
F32 = jnp.float32
VM = pl.BlockSpec()
SM = pl.BlockSpec(memory_space=pltpu.SMEM)
HB = pl.BlockSpec(memory_space=pltpu.HBM)
AN = pl.BlockSpec(memory_space=pl.ANY)


def dot(a, b):
    return jnp.dot(a, b, preferred_element_type=F32)


def dot_t(a, b):
    return lax.dot_general(a, b, (((1,), (1,)), ((), ())), preferred_element_type=F32)


def t_dot(a, b):
    return lax.dot_general(a, b, (((0,), (0,)), ((), ())), preferred_element_type=F32)


def swap(value):
    return lax.ppermute(value, "section", [(0, 1), (1, 0)])


def direct(axis):
    count = lax.axis_size(axis)
    return count <= 4 and count & (count - 1) == 0


def peer_ids(axis):
    count = lax.axis_size(axis)
    ids = jnp.arange(count, dtype=jnp.int32)
    return ids ^ lax.axis_index(axis) if direct(axis) else ids


def hop(value, axis, step):
    count = lax.axis_size(axis)
    return lax.ppermute(value, axis, [(i, i ^ step) for i in range(count)])


def spread(value, axis):
    count = lax.axis_size(axis)
    if direct(axis):
        return [value] + [hop(value, axis, step) for step in range(1, count)]
    every = lax.all_gather(value, axis, axis=0)
    return [every[i] for i in range(count)]


def exchange(blocks, axis):
    count = lax.axis_size(axis)
    if direct(axis):
        return [blocks[0]] + [hop(blocks[step], axis, step) for step in range(1, count)]
    swapped = lax.all_to_all(jnp.stack(blocks), axis, 0, 0, tiled=True)
    return [swapped[i] for i in range(count)]


def scatter_rows(whole):
    for axis in ("expert", "shard"):
        count = lax.axis_size(axis)
        rows = whole.shape[0] // count
        ids = peer_ids(axis)
        blocks = [
            lax.dynamic_slice_in_dim(whole, ids[i] * rows, rows, axis=0).astype(BF)
            for i in range(count)
        ]
        whole = sum(block.astype(F32) for block in exchange(blocks, axis))
    return whole


def call(kernel, outs, ins, specs, scratch=(), flops=0, out_specs=None, after=(), limit=28):
    count = len(ins)
    moved = sum(math.prod(a.shape) * a.dtype.itemsize for a in (*ins, *outs))

    def run(*refs):
        kernel(*refs[:count], *refs[count + len(after) :])

    return pl.pallas_call(
        run,
        out_shape=list(outs),
        in_specs=list(specs) + [AN] * len(after),
        out_specs=list(out_specs or [VM] * len(outs)),
        scratch_shapes=list(scratch),
        compiler_params=pltpu.CompilerParams(vmem_limit_bytes=limit * 1024 * 1024),
        cost_estimate=pl.CostEstimate(flops=flops, bytes_accessed=moved, transcendentals=0),
    )(*ins, *after)


def out(shape, kind=BF):
    return jax.ShapeDtypeStruct(shape, kind)


def begin(copies):
    for copy in copies:
        copy.start()
    return copies


def finish(copies):
    for copy in copies:
        copy.wait()


def join_weights(place, pieces, held, layout):
    plane = pieces[0].shape[0]
    for part in range(2):
        target = place[0] if part == 0 else 1 - place[0]
        for i, (peer, first) in enumerate(layout):
            piece = pieces[part * len(layout) + i]
            at = pl.multiple_of(place[2 + peer] * plane + first, piece.shape[0])
            held[target, pl.ds(at, piece.shape[0]), :] = piece[...]


def as_column(row, turned=None):
    n = row.shape[1]
    across = lax.broadcasted_iota(jnp.int32, (n, n), 1)
    down = lax.broadcasted_iota(jnp.int32, (n, n), 0)
    if turned is not None:
        down = turned - down
    return jnp.sum(jnp.where(across == down, row, jnp.zeros_like(row)), axis=1, keepdims=True)


def table_places(width, own_rows, table_rows):
    spot = lax.broadcasted_iota(jnp.int32, (16, width), 1).astype(F32)
    owner = jnp.floor((spot + 0.5) * (1.0 / own_rows))
    rest = spot - owner * own_rows
    flat = owner * table_rows + rest
    bucket = jnp.floor((flat + 0.5) * (1.0 / HEADS))
    head = flat - bucket * HEADS
    real = rest < table_rows
    row = lax.broadcasted_iota(jnp.int32, (16, width), 0).astype(F32)
    return jnp.where(real, bucket, -1.0)[0:1], (real & (head == row)).astype(F32)


def inverse_rms(value):
    return lax.rsqrt(jnp.mean(value * value, axis=-1, keepdims=True) + EPSILON)


def norm_back(value, gain, grad):
    scale = inverse_rms(value)
    scaled = value * scale
    gained = grad * gain
    back = scale * (gained - scaled * jnp.mean(gained * scaled, axis=-1, keepdims=True))
    return back, jnp.sum(grad * scaled, axis=0, keepdims=True)


def gain_rows(side):
    pick = (
        lax.broadcasted_iota(jnp.int32, (16, EXT), 0)
        == lax.broadcasted_iota(jnp.int32, (16, EXT), 1)
    ).astype(BF)
    rows = dot_t(pick, side)
    return rows[0:1], rows[1:2], rows[2:3]


def gelu_parts(value):
    c = math.sqrt(2.0 / math.pi)
    square = value * value
    inner = jnp.tanh(c * (value + 0.044715 * square * value))
    grad = 0.5 * (1.0 + inner) + 0.5 * value * (1.0 - inner * inner) * (
        c + (3.0 * 0.044715 * c) * square
    )
    return 0.5 * value * (1.0 + inner), grad


def softmax_lanes(logits, experts):
    lane = lax.broadcasted_iota(jnp.int32, logits.shape, 1)
    valid = (lane >= LEAD) & (lane < LEAD + experts)
    logits = jnp.where(valid, logits, MASK_FILL)
    power = jnp.exp(logits - jnp.max(logits, axis=-1, keepdims=True))
    power = jnp.where(valid, power, 0.0)
    return power / jnp.sum(power, axis=-1, keepdims=True), lane


def pair_rows(value):
    low_lanes = lax.broadcasted_iota(jnp.int32, value.shape, 1) < HEAD_DIM
    zero = jnp.zeros_like(value)
    return jnp.concatenate(
        [jnp.where(low_lanes, value, zero), jnp.where(low_lanes, zero, value)], axis=0
    )


def pair_lanes(value):
    half = value.shape[0] // 2
    low_lanes = lax.broadcasted_iota(jnp.int32, (half, value.shape[1]), 1) < HEAD_DIM
    return jnp.where(low_lanes, value[:half], value[half:])


def attn_forward(layer, seq, width, experts, layout, count, shards, own_rows, table_rows, *refs):
    place, info = refs[:2]
    refs = refs[2:]
    pieces, refs = refs[:count], refs[count:]
    if layer == 0:
        (x_ref,), refs = refs[:1], refs[1:]
        n2_ref, refs = refs[0], refs[1:]
        extra = []
    else:
        (hid_ref,), toks, refs = refs[:1], refs[1:-16], refs[-16:]
        out_ref, n2_ref, tok_out = refs[:3]
        refs = refs[3:]
    acts_out, probs_out, floats_out, ext_out, held_out = refs[:5]
    held, sem, acts, probs_keep, floats, ext_keep, low_keep, out_sems = refs[5:]
    if layer == 0:
        low = x_ref[...]
    else:
        coming = pltpu.make_async_copy(hid_ref, floats, out_sems.at[0])
        coming.start()
        tok = sum(t[...].astype(F32) for t in toks).astype(BF)
        low_keep[...] = tok
        coming.wait()
        gate = floats[:, width + EXT : width + EXT + 1]
        low = (floats[:, :width] + gate * tok.astype(F32)).astype(BF)
        out_ref[...] = low
        extra = begin([pltpu.make_async_copy(low_keep, tok_out, out_sems.at[0])])
    acts[:, 6 * width :] = low
    x = low.astype(F32)
    scaled = x * inverse_rms(x)
    seg_row = info[0:1, :seq]
    same = as_column(seg_row) == seg_row
    route = as_column(info[1 + layer : 2 + layer, :seq])
    bucket = as_column(info[3:4, :]).astype(F32)
    bucket_row, head_sel = table_places(width, own_rows, table_rows)
    buckets = (bucket == bucket_row).astype(BF)
    if layout:
        join_weights(place, pieces, held, layout)
    else:
        held[place[0]] = pieces[0][...]
        held[1 - place[0]] = pieces[1][...]
    extra = extra + begin([pltpu.make_async_copy(held, held_out, sem)])
    side = held[0, :, 2 * width : 2 * width + EXT]
    ext_keep[...] = side
    extra = extra + begin([pltpu.make_async_copy(ext_keep, ext_out, out_sems.at[1])])
    gain_one, gain_two, table_row = gain_rows(side)
    table = dot_t((head_sel * table_row).astype(BF), buckets)
    normed = (scaled * gain_one).astype(BF)
    acts[:, :width] = normed
    acts[:, width : 3 * width] = dot(normed, held[0, :, : 2 * width]).astype(BF)
    acts[:, 3 * width : 4 * width] = dot(normed, held[1, :, :width]).astype(BF)
    scale = 1.0 / math.sqrt(HEAD_DIM)
    contexts = []
    for p in range(HEADS // 2):
        at = [(1 + i) * width + 128 * p for i in range(3)]
        q2 = pair_rows(acts[:, at[0] : at[0] + 128])
        scores = dot_t(q2, acts[:, at[1] : at[1] + 128]) * scale
        parts = []
        for h in (2 * p, 2 * p + 1):
            line = jnp.broadcast_to(table[h : h + 1], (seq, 2 * seq))
            bias = pltpu.roll(line, seq + 1, axis=1, stride=1, stride_axis=0)[:, :seq]
            part = scores[seq * (h - 2 * p) : seq * (h - 2 * p) + seq] + bias
            parts.append(jnp.where(same, part, MASK_FILL))
        scores = jnp.concatenate(parts, axis=0)
        power = jnp.exp(scores - jnp.max(scores, axis=-1, keepdims=True))
        probs = power / jnp.sum(power, axis=-1, keepdims=True)
        probs_keep[p] = probs
        contexts.append(pair_lanes(dot(probs.astype(BF), acts[:, at[2] : at[2] + 128])))
    extra = extra + begin([pltpu.make_async_copy(probs_keep, probs_out, out_sems.at[2])])
    context = jnp.concatenate(contexts, axis=1).astype(BF)
    acts[:, 4 * width : 5 * width] = context
    hidden = x + dot(context, held[1, :, width : 2 * width])
    floats[:, :width] = hidden
    normed_two = (hidden * inverse_rms(hidden) * gain_two).astype(BF)
    n2_ref[...] = normed_two
    acts[:, 5 * width : 6 * width] = normed_two
    extra = extra + begin([pltpu.make_async_copy(acts, acts_out, out_sems.at[3])])
    gates, lane = softmax_lanes(dot(normed_two, side), experts)
    floats[:, width : width + EXT] = gates
    value = jnp.sum(jnp.where(lane == route + LEAD, gates, 0.0), axis=-1, keepdims=True)
    floats[:, width + EXT :] = jnp.broadcast_to(value, gates.shape)
    finish(extra + begin([pltpu.make_async_copy(floats, floats_out, out_sems.at[4])]))


def pick_inputs(seq, *refs):
    place, own_feed, came_feed, segments, own_routes, came_routes, buckets = refs[:7]
    x_ref, dy_ref, info, sems = refs[7:]
    sec = place[0]
    for core in range(2):

        @pl.when(sec == core)
        def _(core=core):
            sources = (own_feed, came_feed) if core == 0 else (came_feed, own_feed)
            finish(
                begin(
                    [
                        pltpu.make_async_copy(sources[0].at[core], x_ref, sems.at[0]),
                        pltpu.make_async_copy(sources[1].at[core], dy_ref, sems.at[1]),
                    ]
                )
            )
            info[...] = jnp.full(info.shape, -2, jnp.int32)
            info[0:1, :seq] = segments[core : core + 1, :]
            info[1 + core : 2 + core, :seq] = own_routes[core : core + 1, :]
            info[2 - core : 3 - core, :seq] = came_routes[core : core + 1, :]
            info[3:4, : 2 * seq - 1] = buckets[...]


def routing_slots(shards, seq, experts, cap, *refs):
    place, infos, slots = refs[0], refs[1 : 1 + shards], refs[1 + shards]
    before = (
        lax.broadcasted_iota(jnp.int32, (seq, seq), 0)
        < lax.broadcasted_iota(jnp.int32, (seq, seq), 1)
    ).astype(BF)
    routes = jnp.concatenate(
        [info[1 + layer : 2 + layer, :seq] for layer in range(2) for info in infos], axis=0
    )
    rank = jnp.zeros(routes.shape, F32)
    for e in range(experts):
        mine = (routes == e).astype(F32)
        rank = rank + mine * dot(mine.astype(BF), before)
    slots[...] = (routes ^ place[1]) * cap + rank.astype(jnp.int32)


def slot_hot(slots, layer, shards, z, total):
    row = slots[layer * shards + z : layer * shards + z + 1, :]
    return (lax.broadcasted_iota(jnp.int32, (total, row.shape[1]), 0) == row).astype(BF)


def dispatch_rows(layer, count, shards, cap, *refs):
    slots = refs[0]
    toks = refs[1 : 1 + shards]
    blocks = refs[1 + shards :]
    for z in range(shards):
        rows = dot(slot_hot(slots, layer, shards, z, count * cap), toks[z][...]).astype(BF)
        for i in range(count):
            blocks[i][z * cap : (z + 1) * cap, :] = rows[i * cap : (i + 1) * cap]


def combine_rows(layer, count, shards, cap, *refs):
    slots = refs[0]
    blocks, refs = refs[1 : 1 + count], refs[1 + count :]
    more = (len(refs) - shards) // 2
    handed, toks, given = refs[:more], refs[more : more + shards], refs[more + shards :]
    for z in range(shards):
        rows = jnp.concatenate([b[z * cap : (z + 1) * cap, :] for b in blocks], axis=0)
        toks[z][...] = t_dot(slot_hot(slots, layer, shards, z, count * cap), rows).astype(BF)
    for source, target in zip(handed, given):
        target[...] = source[...]


def start_expert(layer, place, own, came, held, sems):
    def begin(pair):
        for i in range(2):
            pltpu.make_async_copy(pair[i], held.at[i], sems.at[i]).start()

    @pl.when(place[0] == layer)
    def _():
        begin(own)

    @pl.when(place[0] != layer)
    def _():
        begin(came)

    return [pltpu.make_async_copy(own[i], held.at[i], sems.at[i]) for i in range(2)]


def expert_forward(layer, count, *refs):
    place, own, came = refs[0], refs[1:3], refs[3:5]
    blocks = refs[5 : 5 + count]
    results, rows_out = refs[5 + count : 5 + 2 * count], refs[5 + 2 * count]
    held, sems, rows, out_sem = refs[6 + 2 * count :]
    copies = start_expert(layer, place, own, came, held, sems)
    each = blocks[0].shape[0]
    for i in range(count):
        rows[i * each : (i + 1) * each, :] = blocks[i][...]
    leaving = begin([pltpu.make_async_copy(rows, rows_out, out_sem)])
    finish(copies)
    for i in range(count):
        activated = gelu_parts(dot(blocks[i][...], held[0]))[0].astype(BF)
        results[i][...] = dot(activated, held[1]).astype(BF)
    finish(leaving)


def expert_backward(layer, count, experts, with_out, *refs):
    place, own, came, ext_in = refs[0], refs[1:3], refs[3:5], refs[5]
    if with_out:
        blocks, dy_in, refs = refs[6 : 6 + count], refs[6 + count : 6 + 2 * count], refs[6 + 2 * count :]
    else:
        rows_in, dys, refs = refs[6], refs[7 : 7 + count], refs[7 + count :]
    grads, refs = refs[:count], refs[count:]
    if with_out:
        results, refs = refs[:count], refs[count:]
    keep_out, held, sems, keep, ext, late, more_sems = refs
    copies = start_expert(layer, place, own, came, held, sems)
    each = grads[0].shape[0]
    loads = [pltpu.make_async_copy(ext_in, ext, more_sems.at[0])]
    if with_out:
        loads += [
            pltpu.make_async_copy(dy_in[i], late.at[pl.ds(i * each, each), :], more_sems.at[1 + i])
            for i in range(count)
        ]
    else:
        loads += [pltpu.make_async_copy(rows_in, late, more_sems.at[1])]
    begin(loads)
    finish(loads + copies)
    leaving = []
    for i in range(count):
        at = slice(i * each, (i + 1) * each)
        if with_out:
            rows, dy = blocks[i][...], late[at, :]
        else:
            rows, dy = late[at, :], dys[i][...]
        dy = dy.astype(F32)
        gates, lane = softmax_lanes(dot(rows, ext[...]), experts)
        mine = (lane == place[1] + LEAD).astype(F32)
        value = jnp.sum(gates * mine, axis=-1, keepdims=True)
        grad_expert = (value * dy).astype(BF)
        act, slope = gelu_parts(dot(rows, held[0]))
        act = act.astype(BF)
        grad_pre = (dot_t(grad_expert, held[1]) * slope).astype(BF)
        grad = dot_t(grad_pre, held[0])
        if with_out:
            result = dot(act, held[1])
            results[i][...] = result.astype(BF)
            grad_gate = jnp.sum(dy * result, axis=-1, keepdims=True)
            grad_logits = (grad_gate * value * (mine - gates)).astype(BF)
            grad = grad + dot_t(grad_logits, ext[...])
        grads[i][...] = grad.astype(BF)
        keep[0, at, :] = rows
        keep[1, at, :] = grad_pre
        keep[2, at, :] = act
        keep[3, at, :] = grad_expert
        leaving += begin(
            [
                pltpu.make_async_copy(
                    keep.at[:, pl.ds(i * each, each), :],
                    keep_out.at[:, pl.ds(i * each, each), :],
                    more_sems.at[1 + count + i],
                )
            ]
        )
    finish(leaving)


def attn_backward(layer, seq, width, experts, shards, own_rows, table_rows, *refs):
    place, info, held_in = refs[:3]
    refs = refs[3:]
    dy_ref, acts_in, probs_in, floats_in = refs[:4]
    refs = refs[4:]
    if layer == 0:
        tok_in, refs = refs[0], refs[1:]
    parts, refs = refs[:shards], refs[shards:]
    dx_ref, ship, stay, side_grad = refs[:4]
    ship_all, ship = ship, ship.at[pl.ds(0, seq), :]
    held, sem, acts, probs_all, floats, tok_keep, gj, g_rel, in_sems = refs[4:]
    loads = [
        pltpu.make_async_copy(floats_in, floats, in_sems.at[0]),
        pltpu.make_async_copy(acts_in, acts, in_sems.at[1]),
        pltpu.make_async_copy(probs_in, probs_all, in_sems.at[2]),
    ]
    if layer == 0:
        loads.append(pltpu.make_async_copy(tok_in, tok_keep, in_sems.at[3]))
    begin(loads)
    copies = begin([pltpu.make_async_copy(held_in, held, sem)])
    dy = dy_ref[...].astype(F32)
    grad_norm_two = sum(p[...].astype(F32) for p in parts)
    route = as_column(info[1 + layer : 2 + layer, :seq])
    bucket = as_column(info[3:4, :], 2 * seq - 2).astype(F32)
    bucket_row, head_sel = table_places(width, own_rows, table_rows)
    buckets = (bucket == bucket_row).astype(BF)
    finish(loads)
    hidden = floats[:, :width]
    x = acts[:, 6 * width :].astype(F32)
    state = acts
    finish(copies)
    side = held[0, :, 2 * width : 2 * width + EXT]
    gain_one, gain_two, _ = gain_rows(side)
    side_grad[...] = jnp.zeros_like(side_grad)
    if layer == 0:
        gates = floats[:, width : width + EXT]
        lane = lax.broadcasted_iota(jnp.int32, gates.shape, 1)
        hot = (lane == route + LEAD).astype(F32)
        grad_gate = jnp.sum(dy * tok_keep[...].astype(F32), axis=-1, keepdims=True)
        value = floats[:, width + EXT : width + EXT + 1]
        grad_logits = (grad_gate * value * (hot - gates)).astype(BF)
        grad_norm_two = grad_norm_two + dot_t(grad_logits, side)
        router_rows = t_dot(grad_logits, acts[:, 5 * width : 6 * width])
        side_grad[...] = router_rows[: side_grad.shape[0]]
    back, gain_two_grad = norm_back(hidden, gain_two, grad_norm_two)
    grad_hidden = dy + back
    grad_hidden_low = grad_hidden.astype(BF)
    grad_context = dot_t(grad_hidden_low, held[1, :, width : 2 * width]).astype(BF)
    scale = 1.0 / math.sqrt(HEAD_DIM)
    mirror = (
        lax.broadcasted_iota(jnp.int32, (seq, 2 * seq), 0)
        + lax.broadcasted_iota(jnp.int32, (seq, 2 * seq), 1)
        == seq - 1
    ).astype(BF)
    for p in range(HEADS // 2):
        lanes = slice(128 * p, 128 * p + 128)
        q2 = pair_rows(state[:, width + 128 * p : width + 128 * p + 128])
        keys = state[:, 2 * width + 128 * p : 2 * width + 128 * p + 128]
        vals = state[:, 3 * width + 128 * p : 3 * width + 128 * p + 128]
        g2 = pair_rows(grad_context[:, lanes])
        probs = probs_all[p]
        grad_probs = dot_t(g2, vals)
        grad_scores = probs * (
            grad_probs - jnp.sum(probs * grad_probs, axis=-1, keepdims=True)
        )
        grad_scores = grad_scores.astype(BF)
        gj[:, lanes] = (pair_lanes(dot(grad_scores, keys)) * scale).astype(BF)
        gj[:, width + 128 * p : width + 128 * p + 128] = (t_dot(grad_scores, q2) * scale).astype(BF)
        gj[:, 2 * width + 128 * p : 2 * width + 128 * p + 128] = t_dot(
            probs.astype(BF), g2
        ).astype(BF)
        turned = dot(grad_scores, mirror)
        for h in range(2):
            shifted = pltpu.roll(turned[h * seq : (h + 1) * seq], 0, axis=1, stride=1, stride_axis=0)
            g_rel[2 * p + h : 2 * p + h + 1, :] = jnp.sum(shifted, axis=0, keepdims=True)
    g_rel[HEADS:, :] = jnp.zeros_like(g_rel[HEADS:, :])
    offsets = g_rel[...]
    high = offsets.astype(BF)
    low = (offsets - high.astype(F32)).astype(BF)
    by_row = dot(high, buckets) + dot(low, buckets)
    side_grad[2:3, :] = jnp.sum(by_row * head_sel, axis=0, keepdims=True)
    side_grad[1:2, :] = gain_two_grad
    grad_normed = dot_t(gj[:, : 2 * width], held[0, :, : 2 * width]) + dot_t(
        gj[:, 2 * width :], held[1, :, :width]
    )
    back, gain_one_grad = norm_back(x, gain_one, grad_normed)
    side_grad[0:1, :] = gain_one_grad
    dx_ref[...] = (grad_hidden + back).astype(BF)
    normed = state[:, :width]
    halves = (ship, stay)
    for core in range(2):

        @pl.when(place[0] == core)
        def _(core=core):
            halves[1 - core][:, :width] = normed
            halves[1 - core][:, width : 3 * width] = gj[:, : 2 * width]
            halves[1 - core][:, 3 * width :] = jnp.zeros_like(normed)
            halves[core][:, :width] = normed
            halves[core][:, width : 2 * width] = gj[:, 2 * width :]
            halves[core][:, 2 * width : 3 * width] = state[:, 4 * width : 5 * width]
            halves[core][:, 3 * width :] = grad_hidden_low

    ship_all[seq:, :width] = side_grad[...].astype(BF)
    ship_all[seq:, width:] = jnp.zeros_like(ship_all[seq:, width:])


def last_output(seq, width, experts, shards, *refs):
    info, dy_ref, acts_in, floats_in, side_in = refs[:5]
    parts, refs = refs[5 : 5 + shards], refs[5 + shards :]
    out_ref, side_grad, normed, floats, sems = refs
    loads = begin(
        [
            pltpu.make_async_copy(floats_in, floats, sems.at[0]),
            pltpu.make_async_copy(acts_in.at[:, pl.ds(5 * width, width)], normed, sems.at[1]),
        ]
    )
    tok = sum(p[...].astype(F32) for p in parts).astype(BF).astype(F32)
    finish(loads)
    value = floats[:, width + EXT : width + EXT + 1]
    out_ref[...] = (floats[:, :width] + value * tok).astype(BF)
    gates = floats[:, width : width + EXT]
    lane = lax.broadcasted_iota(jnp.int32, gates.shape, 1)
    hot = (lane == as_column(info[2:3, :seq]) + LEAD).astype(F32)
    grad_gate = jnp.sum(dy_ref[...].astype(F32) * tok, axis=-1, keepdims=True)
    grad_logits = (grad_gate * value * (hot - gates)).astype(BF)
    side_grad[...] = side_in[...] + t_dot(grad_logits, normed[...])[: side_grad.shape[0]]


def attn_weights(width, count, parts, more, relay, *refs):
    place, stay, came = refs[:3]
    total = refs[-1]
    handed, sides, outs = refs[3 : 3 + more], refs[3 + more : -1 - count - more], refs[-1 - count - more : -1]
    blocks, given = outs[:count], outs[count:]
    for source, target in zip(handed, given):
        target[...] = source[...]

    seq = stay.shape[0]

    def both(first, last):
        return jnp.concatenate([stay[:, first:last], came[:seq, first:last]], axis=0)

    unit = width // 2
    for i, part in enumerate(parts):
        at = slice(i * unit, (i + 1) * unit)

        @pl.when(place[0] == 0)
        def _(part=part, at=at):
            total[:, at] = t_dot(
                both(0, width), both(width + part * unit, width + (part + 1) * unit)
            ).astype(BF)

        @pl.when(place[0] != 0)
        def _(part=part, at=at):
            left = part // 2 * 2 * width
            right = left + width + part % 2 * unit
            total[:, at] = t_dot(both(left, left + width), both(right, right + unit)).astype(BF)

    if sides:
        block = jnp.zeros((width, EXT), F32)
        ours = (sides[0][...] + came[seq:, :width].astype(F32), sides[1][...] + sides[2][...])
        for layer, rows in enumerate(ours):
            pick = (
                lax.broadcasted_iota(jnp.int32, (rows.shape[0], EXT), 0) + layer * (EXT // 2)
                == lax.broadcasted_iota(jnp.int32, (rows.shape[0], EXT), 1)
            ).astype(BF)
            block = block + t_dot(rows.astype(BF), pick)
        total[:, len(parts) * unit :] = block.astype(BF)

    if relay:
        rows = blocks[0].shape[0] // 2
        cut = blocks[0].shape[1]
        columns = (slice(0, cut), slice(cut, total.shape[1]))
        for block, ids, at in zip(blocks, ((1, 3), (0, 2), (2, 3), (0, 1)), (0, 0, 1, 1)):
            for i, peer in enumerate(ids):
                first = pl.multiple_of(place[2 + peer] * rows, rows)
                block[i * rows : (i + 1) * rows, :] = total[pl.ds(first, rows), columns[at]]
        return
    rows = blocks[0].shape[0]
    for i in range(count):
        first = pl.multiple_of(place[2 + i] * rows, rows) if count > 1 else 0
        blocks[i][...] = total[pl.ds(first, rows), :]


def halve_sums(*refs):
    came_x, kept_x, came_y, kept_y, own_x, on_x, own_y, on_y = refs
    for came, kept, own, on in ((came_x, kept_x, own_x, on_x), (came_y, kept_y, own_y, on_y)):
        rows = own.shape[0]
        own[...] = came[:rows].astype(F32) + kept[:rows].astype(F32)
        on[...] = (came[rows:].astype(F32) + kept[rows:].astype(F32)).astype(BF)


def join_sums(at, *refs):
    place, own_x, came_x, own_y, came_y = refs[:5]
    blocks, total = refs[5:-1], refs[-1]
    cut = own_x.shape[1]
    total[:, :cut] = own_x[...] + came_x[...].astype(F32)
    total[:, cut:] = own_y[...] + came_y[...].astype(F32)
    rows = blocks[0].shape[0]
    for i, block in enumerate(blocks):
        first = pl.multiple_of(place[at + i] * rows, rows)
        block[...] = total[pl.ds(first, rows), :].astype(block.dtype)


def last_swap(width, *refs):
    place, zero, one, send = refs

    @pl.when(place[0] == 0)
    def _():
        send[:, : 2 * width] = one[...]
        send[:, 2 * width :] = zero[:, 2 * width :]

    @pl.when(place[0] != 0)
    def _():
        send[...] = zero[...]


def last_grads(width, experts, *refs):
    place, zero, one, came = refs[:4]
    query, key, value, out_proj, gain_a, gain_f, table, router = refs[4:]

    def put_side(side):
        n = side.shape[0]
        across = lax.broadcasted_iota(jnp.int32, (n, n), 1)
        down = lax.broadcasted_iota(jnp.int32, (n, n), 0)

        def turned(i):
            return jnp.sum(
                jnp.where(across == down, side[:, i : i + 1], 0.0), axis=0, keepdims=True
            )

        for i, target in enumerate((gain_a, gain_f, table)):
            target[...] = turned(i)[:, : target.shape[1]]
        for e in range(experts):
            router[e : e + 1, :] = turned(LEAD + e)

    @pl.when(place[0] == 0)
    def _():
        query[...] = zero[:, :width]
        key[...] = zero[:, width : 2 * width]
        value[...] = came[:, :width]
        out_proj[...] = came[:, width : 2 * width]
        put_side(zero[:, 2 * width : 2 * width + EXT // 2])

    @pl.when(place[0] != 0)
    def _():
        query[...] = came[:, :width]
        key[...] = came[:, width : 2 * width]
        value[...] = one[:, :width]
        out_proj[...] = one[:, width:]
        put_side(came[:, 2 * width + EXT // 2 :])


def sum_blocks(count, at, *refs):
    place, parts = refs[0], refs[1 : 1 + count]
    blocks, total = refs[1 + count : -1], refs[-1]
    total[...] = sum(p[...].astype(F32) for p in parts)
    rows = blocks[0].shape[0]
    for i, block in enumerate(blocks):
        first = pl.multiple_of(place[at + i] * rows, rows) if len(blocks) > 1 else 0
        block[...] = total[pl.ds(first, rows), :].astype(block.dtype)


def join_rows(count, first_id, *refs):
    place, parts, whole = refs[0], refs[1 : 1 + count], refs[1 + count]
    rows = parts[0].shape[0]
    for i in range(count):
        at = pl.multiple_of(place[first_id + i] * rows, rows)
        whole[pl.ds(at, rows), :] = parts[i][...]


def pick_later(*refs):
    place, kept, came, later = refs

    @pl.when(place[0] == 0)
    def _():
        later[...] = came[...]

    @pl.when(place[0] != 0)
    def _():
        later[...] = kept[...]


def join_planes(layout, *refs):
    place, pieces, whole = refs[0], refs[1:-1], refs[-1]
    plane = pieces[0].shape[0]
    for (peer, first), piece in zip(layout, pieces):
        at = pl.multiple_of(place[2 + peer] * plane + first, piece.shape[0])
        whole[pl.ds(at, piece.shape[0]), :] = piece[...]


def pack_weights(width, experts, table_rows, *refs):
    place, query, key, value, out_proj, gain_a, gain_f, table, router = refs[:9]
    send, keep, row_a, row_f, row_t, rows_r, sems = refs[9:]
    own_rows = row_a.shape[1]
    small = begin(
        [
            pltpu.make_async_copy(source, target, sems.at[4 + i])
            for i, (source, target) in enumerate(
                ((gain_a, row_a), (gain_f, row_f), (table, row_t), (router, rows_r))
            )
        ]
    )
    halves = (keep, send)
    for core in range(2):

        @pl.when(place[0] == core)
        def _(core=core):
            begin(
                [
                    pltpu.make_async_copy(
                        source,
                        halves[(core + i // 2) % 2].at[:, pl.ds(i % 2 * width, width)],
                        sems.at[i],
                    )
                    for i, source in enumerate((query, key, value, out_proj))
                ]
            )

    finish(small)
    columns = [as_column(row_a[...].astype(F32)), as_column(row_f[...].astype(F32))]
    line = row_t[...].astype(F32)
    down = lax.broadcasted_iota(jnp.int32, (own_rows, table_rows), 0)
    across = lax.broadcasted_iota(jnp.int32, (own_rows, table_rows), 1)
    columns.append(jnp.sum(jnp.where(down == across, line, 0.0), axis=1, keepdims=True))
    lines = rows_r[...].astype(F32)
    columns += [as_column(lines[e : e + 1]) for e in range(experts)]
    lane = lax.broadcasted_iota(jnp.int32, (own_rows, EXT), 1)
    block = jnp.zeros((own_rows, EXT), F32)
    for i, column in enumerate(columns):
        block = jnp.where(lane == i, column, block)
    keep[:, 2 * width :] = block.astype(BF)
    send[:, 2 * width :] = block.astype(BF)
    finish(
        [
            pltpu.make_async_copy(source, keep.at[:, pl.ds(0, width)], sems.at[i])
            for i, source in enumerate((query, key, value, out_proj))
        ]
    )


def expert_weights(other, *refs):
    place, keeps, refs = refs[0], refs[1:3], refs[3:]
    if other:
        both_ref, held, sem = refs
        in_ref, out_ref = both_ref.at[0], both_ref.at[1]
    else:
        came, in_ref, out_ref, held, sem = refs
    for layer in range(2):

        @pl.when((place[0] == layer) != other)
        def _(layer=layer):
            pltpu.make_async_copy(keeps[layer], held, sem).start()

    pltpu.make_async_copy(keeps[0], held, sem).wait()
    grad_in = t_dot(held[0], held[1])
    grad_out = t_dot(held[2], held[3])
    if not other:
        grad_in = grad_in + came[0].astype(F32)
        grad_out = grad_out + came[1].astype(F32)
    in_ref[...] = grad_in.astype(in_ref.dtype)
    out_ref[...] = grad_out.astype(out_ref.dtype)


def body(
    feed, segments, routes, rel_bucket, gain_attn, gain_ffn, w_query, w_key, w_value, w_out_attn,
    rel_table, router, expert_in, expert_out,
):
    seq = feed.shape[2]
    width = feed.shape[3]
    experts = lax.axis_size("expert")
    shards = lax.axis_size("shard")
    cap = max(2, 2 * seq // experts)
    own_rows = w_query.shape[1]
    table_rows = rel_table.shape[1]
    quick = direct("expert") and direct("shard")
    blocks_count = experts if quick else 1
    wide = 2 * width + EXT
    side_rows = -(-(LEAD + experts) // 16) * 16
    sec = lax.axis_index("section")
    first = sec == 0
    place = jnp.concatenate(
        [
            jnp.stack([sec, lax.axis_index("expert")]).astype(jnp.int32),
            peer_ids("expert"),
            peer_ids("shard"),
        ]
    )
    row = out((seq, width))
    sems = pltpu.SemaphoreType.DMA

    small = [gain_attn, gain_ffn, rel_table, router[0].T]
    send, kept = call(
        functools.partial(pack_weights, width, experts, table_rows),
        [out((own_rows, wide))] * 2,
        [place, w_query[0], w_key[0], w_value[0], w_out_attn[0], *small],
        [SM] + [HB] * 8,
        [pltpu.VMEM(one.shape, BF) for one in small] + [sems((8,))],
        limit=60,
    )
    came = swap(send)
    part_zero = jnp.where(first, kept, came)

    own_experts = [expert_in[0, 0], expert_out[0, 0]]
    came_experts = [swap(expert_in[0, 0]), swap(expert_out[0, 0])]

    feed_own = feed[0]
    routes_own = routes[0, :, 0]
    layer_x, layer_dy, info = call(
        functools.partial(pick_inputs, seq),
        [row, row, out((8, 2 * seq), jnp.int32)],
        [
            place, feed_own, swap(feed_own), segments[:, 0], routes_own, swap(routes_own),
            rel_bucket[None, :],
        ],
        [SM, HB, AN] + [VM] * 4,
        [sems((2,))],
        after=came_experts,
    )

    infos = spread(info, "shard")


    def both_halves(mine):
        return mine + [swap(piece) for piece in mine]

    def plane_of(part, after=()):
        return call(
            functools.partial(join_rows, shards, 2 + experts),
            [out((shards * own_rows, wide))],
            [place, *spread(part, "shard")],
            [SM] + [VM] * shards,
            after=after,
        )[0]

    half = shards * own_rows // 2
    relay = experts == 4 and half % 16 == 0

    def planes_of(plane):
        if not relay:
            return spread(plane, "expert")
        beside = [hop(plane, "expert", 1), hop(plane, "expert", 2)]
        across = [hop(beside[1][:half], "expert", 1), hop(beside[0][half:], "expert", 2)]
        return [plane, *beside, *across]

    peers = [(i, 0) for i in range(experts)]
    if relay:
        peers = peers + [(experts - 1, half)]
    if quick:
        planes = planes_of(plane_of(part_zero, after=[info]))
        weights_zero = both_halves(planes)
        joined_after = planes[1:3]
        layouts = [peers, ()]
        (part_one,) = call(
            pick_later,
            [out((own_rows, wide))],
            [place, kept, came],
            [SM, VM, VM],
        )
        planes_one = planes_of(plane_of(part_one, after=joined_after))
    else:
        part_one = jnp.where(first, came, kept)
        weights_zero, weights_one = [
            both_halves([lax.all_gather(part, ("expert", "shard"), axis=0, tiled=True)])
            for part in (part_zero, part_one)
        ]
        joined_after = ()
        layouts = [(), ()]


    if quick:
        (slots,) = call(
            functools.partial(routing_slots, shards, seq, experts, cap),
            [out((2 * shards, seq), jnp.int32)],
            [place, *infos],
            [SM] + [VM] * shards,
            after=joined_after,
        )
    else:
        all_routes = jnp.stack([one[1:3, :seq] for one in infos], axis=1)
        hot = (all_routes[..., None] == peer_ids("expert")).astype(BF)
        positions = jnp.arange(seq, dtype=jnp.int32)
        before = (positions[:, None] > positions[None, :]).astype(BF)
        rank = jnp.einsum("ij,lzje->lzie", before, hot, preferred_element_type=F32)
        slot_in = jnp.arange(cap, dtype=jnp.int32).astype(F32)
        back_hot = (hot[..., None] * (rank[..., None] == slot_in).astype(BF)).reshape(
            2, shards, seq, experts * cap
        )
        to_hot = jnp.swapaxes(back_hot, 2, 3)

    block = out((shards * cap * experts // blocks_count, width))
    acts_kind = out((seq, 7 * width))
    probs_kind = out((HEADS // 2, 2 * seq, seq), F32)
    floats_kind = out((seq, width + 2 * EXT), F32)

    def buffer(kind):
        return pltpu.VMEM(kind.shape, kind.dtype)

    expert_scratch = [pltpu.VMEM((2, expert_in.shape[2], expert_in.shape[3]), BF), sems((2,))]
    expert_specs = [SM] + [AN] * 4

    def to_experts(layer, tokens, after=()):
        every = spread(tokens, "shard")
        if not quick:
            slot_rows = jnp.einsum(
                "zcs,zsd->czd", to_hot[layer], jnp.stack(every), preferred_element_type=F32
            )
            slot_rows = slot_rows.astype(BF).reshape(experts, cap * shards, width)
            moved = exchange([slot_rows[i] for i in range(experts)], "expert")
            return [jnp.concatenate(moved, axis=0)]
        blocks = call(
            functools.partial(dispatch_rows, layer, experts, shards, cap),
            [block] * experts,
            [slots, *every],
            [VM] * (1 + shards),
            after=after,
        )
        return exchange(blocks, "expert")

    def to_tokens(layer, blocks, later=(), after=()):
        if not quick:
            rows = blocks[0].reshape(experts, cap * shards, width)
            back = jnp.stack(exchange([rows[i] for i in range(experts)], "expert"))
            back = back.reshape(experts * cap, shards, width)
            tokens = jnp.einsum(
                "zsc,czd->zsd", back_hot[layer], back, preferred_element_type=F32
            ).astype(BF)
            return exchange([tokens[i] for i in range(shards)], "shard"), list(later)
        back = exchange(blocks, "expert")
        results = call(
            functools.partial(combine_rows, layer, experts, shards, cap),
            [row] * shards + [out(one.shape, one.dtype) for one in later],
            [slots, *back, *later],
            [VM] * (1 + experts + len(later)),
            after=after,
        )
        return exchange(results[:shards], "shard"), results[shards:]

    held_kind = out((2, width, wide))

    def attention(layer, pieces, ins, in_specs, after=()):
        count = len(pieces)
        first_outs = [row, row, row] if layer else [row]
        return call(
            functools.partial(
                attn_forward, layer, seq, width, experts, layouts[layer], count, shards, own_rows,
                table_rows,
            ),
            first_outs + [acts_kind, probs_kind, floats_kind, out((width, EXT)), held_kind],
            [place, info, *pieces, *ins],
            [SM, VM] + [VM] * count + in_specs,
            [
                buffer(held_kind), sems(()), buffer(acts_kind),
                buffer(probs_kind), buffer(floats_kind), pltpu.VMEM((width, EXT), BF), buffer(row),
                sems((5,)),
            ],
            out_specs=([VM, VM, HB] if layer else [VM]) + [HB] * 5,
            after=after,
        )

    def attention_back(layer, dy, state, tok, parts, after=()):
        acts, probs, floats, _, held = state
        return call(
            functools.partial(
                attn_backward, layer, seq, width, experts, shards, own_rows, table_rows,
            ),
            [
                row,
                out((seq + side_rows, 4 * width)),
                out((seq, 4 * width)),
                out((side_rows, width), F32),
            ],
            [place, info, held, dy, acts, probs, floats, *tok, *parts],
            [SM, VM, HB, VM] + [HB] * (3 + len(tok)) + [VM] * shards,
            [
                buffer(held_kind), sems(()), buffer(acts_kind),
                buffer(probs_kind), buffer(floats_kind), buffer(row),
                pltpu.VMEM((seq, 3 * width), BF), pltpu.VMEM((16, 2 * seq), F32), sems((4,)),
            ],
            after=after,
        )

    keep_kind = out((4, shards * cap * experts, width))

    def back_expert(layer, rows, dys, ext_side, with_out):
        results = call(
            functools.partial(expert_backward, layer, blocks_count, experts, with_out),
            [block] * (blocks_count * (2 if with_out else 1)) + [keep_kind],
            [place, *own_experts, *came_experts, ext_side, *rows, *dys],
            expert_specs + [HB]
            + ([VM] * blocks_count + [AN] * blocks_count if with_out else [HB] + [VM] * blocks_count),
            expert_scratch + [
                buffer(keep_kind), pltpu.VMEM((width, EXT), BF),
                pltpu.VMEM(keep_kind.shape[1:], BF), sems((1 + 2 * blocks_count,)),
            ],
            out_specs=[VM] * (blocks_count * (2 if with_out else 1)) + [HB],
        )
        return results[:blocks_count], results[blocks_count:-1], results[-1]

    row_parts = experts if quick else 1
    relay = quick and relay

    def cut_of(columns):
        return -(-columns // (2 * EXT)) * EXT

    def weight_blocks(stay, came, parts, sides=(), after=(), later=()):
        columns = len(parts) * (width // 2) + (EXT if sides else 0)
        return call(
            functools.partial(attn_weights, width, row_parts, parts, len(later), relay),
            (
                [out((width // 2, cut_of(columns)))] * 2
                + [out((width // 2, columns - cut_of(columns)))] * 2
                if relay
                else [out((width // row_parts, columns))] * row_parts
            )
            + [out(one.shape, one.dtype) for one in later],
            [place, stay, came, *later, *sides],
            [SM] + [VM] * (2 + len(sides) + len(later)),
            [pltpu.VMEM((width, columns), BF)],
            after=after,
        )

    def sum_planes(blocks, after=()):
        if not quick:
            return blocks
        if relay:
            send_x, kept_x, send_y, kept_y = blocks
            rows, cut, rest = width // 4, kept_x.shape[1], kept_y.shape[1]
            own_x, on_x, own_y, on_y = call(
                halve_sums,
                [out((rows, cut), F32), out((rows, cut)), out((rows, rest), F32), out((rows, rest))],
                [hop(send_x, "expert", 1), kept_x, hop(send_y, "expert", 2), kept_y],
                [VM] * 4,
            )
            return call(
                functools.partial(join_sums, 2 + experts),
                [out((own_rows, cut + rest))] * shards,
                [place, own_x, hop(on_x, "expert", 2), own_y, hop(on_y, "expert", 1)],
                [SM] + [VM] * 4,
                [pltpu.VMEM((rows, cut + rest), F32)],
                after=after,
            )
        columns = blocks[0].shape[1]
        return call(
            functools.partial(sum_blocks, experts, 2 + experts),
            [out((own_rows, columns))] * shards,
            [place, *exchange(blocks, "expert")],
            [SM] + [VM] * experts,
            [pltpu.VMEM((shards * own_rows, columns), F32)],
            after=after,
        )

    def sum_rows(blocks):
        if not quick:
            return scatter_rows(blocks[0])
        columns = blocks[0].shape[1]
        (total,) = call(
            functools.partial(sum_blocks, shards, 0),
            [out((own_rows, columns), F32)],
            [place, *exchange(blocks, "shard")],
            [SM] + [VM] * shards,
            [pltpu.VMEM((own_rows, columns), F32)],
        )
        return total

    n2_zero, *state_zero = attention(
        0, weights_zero, [layer_x], [VM], after=[slots] if quick else ()
    )
    rows_zero = to_experts(0, n2_zero)
    *results, rows_zero = call(
        functools.partial(expert_forward, 0, blocks_count),
        [block] * blocks_count + [out(keep_kind.shape[1:])],
        [place, *own_experts, *came_experts, *rows_zero],
        expert_specs + [VM] * blocks_count,
        expert_scratch + [pltpu.VMEM(keep_kind.shape[1:], BF), sems(())],
        out_specs=[VM] * blocks_count + [HB],
        after=planes_one[1:] if quick else (),
    )
    toks, _ = to_tokens(0, results)
    if quick:
        (gathered,) = call(
            functools.partial(join_planes, peers),
            [out((width, wide))],
            [place, *planes_one],
            [SM] + [VM] * len(planes_one),
            after=results[:1],
        )
        weights_one = both_halves([gathered])
    out_zero, n2_one, tok_zero, *state_one = attention(
        1, weights_one, [state_zero[2], *toks], [HB] + [VM] * shards
    )
    dys_one = to_experts(1, layer_dy)
    rows_one = to_experts(1, n2_one)
    grads, results, keep_one = back_expert(1, rows_one, dys_one, state_one[3], True)
    parts_one, results = to_tokens(1, grads, results)
    toks_one, _ = to_tokens(1, results)
    dx_one, ship_one, stay_one, side_one = attention_back(
        1, layer_dy, state_one, [], parts_one, after=toks_one[:1]
    )
    came_one = swap(ship_one)
    dys_zero = to_experts(0, dx_one)
    out_one, side_one = call(
        functools.partial(last_output, seq, width, experts, shards),
        [row, out((side_rows, width), F32)],
        [info, layer_dy, state_one[0], state_one[2], side_one, *toks_one],
        [VM, VM, HB, HB, VM] + [VM] * shards,
        [buffer(row), buffer(floats_kind), sems((2,))],
    )
    side_one_came = swap(side_one)
    grads, _, keep_zero = back_expert(0, [rows_zero], dys_zero, state_zero[3], False)
    matrix = (expert_in.shape[2], expert_in.shape[3])
    keep_scratch = [pltpu.VMEM(keep_one.shape, BF), sems(())]
    sent = call(
        functools.partial(expert_weights, True),
        [out((2, *matrix))],
        [place, keep_zero, keep_one],
        [SM, HB, HB],
        keep_scratch,
    )
    came_grads = [swap(grad) for grad in sent]
    parts_zero, _ = to_tokens(0, grads, after=[side_one_came])
    blocks_one = weight_blocks(stay_one, came_one, (0, 1, 2, 3), after=parts_zero[:1])
    dx_zero, ship_zero, stay_zero, side_zero = attention_back(
        0, dx_one, state_zero, [tok_zero], parts_zero, after=[blocks_one[0], sent[0]]
    )
    planes_one_sum = sum_planes(blocks_one)
    came_zero = swap(ship_zero)
    blocks_zero = weight_blocks(
        stay_zero, came_zero, (0, 1, 2, 3), (side_zero, side_one, side_one_came),
        after=planes_one_sum[:1],
    )
    sum_one = sum_rows(planes_one_sum)
    own_grads = call(
        functools.partial(expert_weights, False),
        [out(matrix, F32)] * 2,
        [place, keep_zero, keep_one, *came_grads],
        [SM, HB, HB, VM],
        keep_scratch,
        after=blocks_zero[:1],
    )
    sum_zero = sum_rows(sum_planes(blocks_zero, after=own_grads[:1]))
    (send,) = call(
        functools.partial(last_swap, width),
        [out((own_rows, wide), F32)],
        [place, sum_zero, sum_one],
        [SM] + [VM] * 2,
    )
    matrix_kind = out((own_rows, width), F32)
    weight_grads = call(
        functools.partial(last_grads, width, experts),
        [matrix_kind] * 4
        + [out((1, own_rows), F32)] * 2
        + [out((1, table_rows), F32), out((experts, own_rows), F32)],
        [place, sum_zero, sum_one, swap(send)],
        [SM] + [VM] * 3,
    )

    def by_batch(zero, one):
        came = swap(jnp.where(first, one, zero))
        kept = jnp.where(first, zero, one)
        return jnp.stack([jnp.where(first, kept, came), jnp.where(first, came, kept)])

    grad_query, grad_key, grad_value, grad_out, grad_a, grad_f, grad_table, grad_router = weight_grads
    return (
        by_batch(out_zero, out_one)[None],
        by_batch(dx_zero, dx_one)[None],
        grad_a,
        grad_f,
        grad_query[None],
        grad_key[None],
        grad_value[None],
        grad_out[None],
        grad_table,
        grad_router.T[None],
        own_grads[0][None, None],
        own_grads[1][None, None],
    )


def solution(mesh):
    rows = ("expert", "shard")
    tokens = P("section", None, rows, None)
    matrix = P("section", rows, None)
    vector = P("section", rows)
    expert_specs = (P("section", "expert", None, "shard"), P("section", "expert", "shard", None))
    in_specs = (
        tokens, P(None, rows, None), tokens, P(), vector, vector, matrix, matrix, matrix, matrix,
        vector, matrix, *expert_specs,
    )
    out_specs = (
        tokens, tokens, vector, vector, matrix, matrix, matrix, matrix, vector, matrix,
        *expert_specs,
    )
    return jax.shard_map(body, mesh=mesh, in_specs=in_specs, out_specs=out_specs, check_vma=False)
```
